256 devices in a mesh: lon: 16 (over x_hi, z), lat: 16 (over y, x_lo, core).
Axes of the slice: x: 4 (x_hi: 2, x_lo: 2; x = x_hi * 2 + x_lo), y: 4, z: 8, core: 2. Of those that a mesh axis runs over, the one named last changes fastest.
Arguments:
- fields: bfloat16 [4, 192, 96, 512], P(None, 'lat', 'lon'), may hold values from -6 to 6
- cotangent: bfloat16 [4, 192, 96, 512], P(None, 'lat', 'lon'), may hold values from -6 to 6
- land_ids: int32 [192, 96], replicated, may hold values from 0 to 2
- gain_a: float32 [512], replicated, may hold values from 0.1 to 1.9
- table_a: float32 [16, 3, 3], replicated, may hold values from -3 to 300
- qkv_weight_a: bfloat16 [512, 1536], replicated, may hold values from -0.25 to 0.25
- out_weight_a: bfloat16 [512, 512], replicated, may hold values from -0.25 to 0.25
- gain_b: float32 [512], replicated, may hold values from 0.1 to 1.9
- table_b: float32 [16, 3, 3], replicated, may hold values from -3 to 300
- qkv_weight_b: bfloat16 [512, 1536], replicated, may hold values from -0.25 to 0.25
- out_weight_b: bfloat16 [512, 512], replicated, may hold values from -0.25 to 0.25
Outputs:
- advanced: bfloat16 [4, 192, 96, 512], P(None, 'lat', 'lon')
- grad_fields: bfloat16 [4, 192, 96, 512], P(None, 'lat', 'lon')
- grad_qkv_a: float32 [512, 1536], P('lat', 'lon')
- grad_out_a: float32 [512, 512], P('lat', 'lon')
- grad_qkv_b: float32 [512, 1536], P('lat', 'lon')
- grad_out_b: float32 [512, 512], P('lat', 'lon')
The draws below stay inside these ranges and needn't reach their ends.
Inputs may be any that keep to these rules, and one draw needn't show every extreme that they name: `land_ids`: class of each grid column: 0 sea, 1 land, 2 polar ice.
All inputs are finite; a program needn't handle non-finite values.
Results may differ from the reference program's by a relative error of at most 0.035.
Values may be sent and summed in bfloat16 or wider, within the bound.
No kernel may reach another device: no remote copies, remote signals or barrier semaphores. Data moves between devices by JAX's collectives and lax.ppermute only.
A program may use at most 128 MiB of HBM per device.

```python
import jax
import jax.numpy as jnp
from jax import lax

D = 512
HEADS = 16
WLEV = 2
WLAT = 12
WLON = 6
LEV = 4
LAT = 192
LON = 96


def table_law(key):
    first = jax.random.fold_in(key, 0)
    base = jax.random.uniform(first, (HEADS, 3, 3), jnp.float32, -3.0, 3.0)
    return base


def draw_table_a(key, part):
    key = jax.random.fold_in(key, 17)
    return table_law(key)


def draw_table_b(key, part):
    key = jax.random.fold_in(key, 29)
    return table_law(key)


def with_ends(entries, own_key, least, top_value):
    place = [jax.random.randint(jax.random.fold_in(own_key, axis), (), 0, length) for axis, length in enumerate(entries.shape)]
    longest = entries.shape.index(max(entries.shape))
    beside = place[:longest] + [(place[longest] + 1) % entries.shape[longest]] + place[longest + 1:]
    return entries.at[tuple(place)].set(least).at[tuple(beside)].set(top_value)


def with_spikes(drawn, rng, source, target, shards_of, factor):
    owner, partner = [(jnp.arange(drawn.shape[axis_at]) // (drawn.shape[axis_at] // shards_of)).reshape([-1 if axis == axis_at else 1 for axis in range(drawn.ndim)]) for axis_at in (source, target)]
    chosen = jax.random.permutation(rng, shards_of)[partner]
    strong = (owner == chosen) | (owner == (partner + shards_of // 2) % shards_of)
    return jnp.where(strong, factor * drawn, drawn)


def steps_of(key, shape, pieces, low, top_value):
    level = 1.0
    for position, shards_of in pieces:
        heights = jax.random.uniform(jax.random.fold_in(jax.random.fold_in(key, 6), position), (shards_of,), jnp.float32, low / len(pieces), top_value / len(pieces))
        level = level * jnp.repeat(jnp.exp(heights), shape[position] // shards_of).reshape((-1,) + (1,) * (len(shape) - 1 - position))
    return level


def scatter_about(own_key, extent, scale, most, pieces=(), held_as=jnp.bfloat16):
    entries = scale * jax.random.normal(own_key, extent, jnp.float32)
    if pieces:
        entries = entries * steps_of(own_key, extent, pieces, -0.22, 0.18)
    return jnp.clip(entries, -most, most).astype(held_as)


def gaussian_with(rng, shape, scale, most, shards, heavy, kind=jnp.bfloat16):
    values = scale * jax.random.normal(rng, shape, jnp.float32)
    if shards:
        values = values * steps_of(rng, shape, shards, -0.22, 0.18)
    return jnp.clip(with_spikes(values, jax.random.fold_in(rng, 3), *heavy), -most, most).astype(kind)


def setup_inputs(seed: int = 0) -> dict:
    seeds = jax.random.split(jax.random.key(seed), 12)
    return {
        "fields": scatter_about(seeds[0], (LEV, LAT, LON, D), 1.0, 6.0, ((1, 16), (2, 16))),
        "cotangent": gaussian_with(seeds[1], (LEV, LAT, LON, D), 1.0, 6.0, ((1, 16), (2, 16)), (2, 3, 16, 2.0)),
        "land_ids": with_ends(jax.random.randint(seeds[2], (LAT, LON), 0, 3), jax.random.fold_in(seeds[2], 1), 0, 2).astype(jnp.int32),
        "gain_a": jnp.clip(1.0 + 0.18 * jax.random.normal(seeds[3], (D,), jnp.float32), 0.1, 1.9),
        "table_a": draw_table_a(jax.random.fold_in(seeds[11], 71), 0),
        "qkv_weight_a": scatter_about(seeds[5], (D, 3 * D), D ** -0.5, 0.25),
        "out_weight_a": scatter_about(seeds[6], (D, D), D ** -0.5, 0.25),
        "gain_b": jnp.clip(1.0 + 0.18 * jax.random.normal(seeds[7], (D,), jnp.float32), 0.1, 1.9),
        "table_b": draw_table_b(jax.random.fold_in(seeds[11], 71), 0),
        "qkv_weight_b": scatter_about(seeds[9], (D, 3 * D), D ** -0.5, 0.25),
        "out_weight_b": scatter_about(seeds[10], (D, D), D ** -0.5, 0.25),
    }


EPS = 1e-05
NEG = -1000000000.0

def layer_norm(inputs, gain):
    centre = inputs - lax.optimization_barrier(jnp.mean(inputs, axis=-1, keepdims=True))
    spread = lax.optimization_barrier(jnp.mean(centre * centre, axis=-1, keepdims=True))
    return (centre * lax.rsqrt(spread + EPS) * gain).astype(jnp.bfloat16)

def attend(packed, bias):
    count, length, triple = packed.shape
    width = triple // 3
    heads = bias.shape[1]
    head_size = width // heads
    query = packed[:, :, :width].reshape(count, length, heads, head_size)
    keys = packed[:, :, width:2 * width].reshape(count, length, heads, head_size)
    values = packed[:, :, 2 * width:].reshape(count, length, heads, head_size)
    scores = jnp.einsum('nqhd,nkhd->nhqk', query, keys, preferred_element_type=jnp.float32)
    scores = scores * head_size ** (-0.5) + bias
    weights = jax.nn.softmax(scores, axis=-1).astype(jnp.bfloat16)
    mixed = jnp.einsum('nhqk,nkhd->nqhd', weights, values, preferred_element_type=jnp.float32)
    return mixed.reshape(count, length, width).astype(jnp.bfloat16)

def windows(grid):
    levels, rows, columns, feats = grid.shape
    parted = grid.reshape(levels // WLEV, WLEV, rows // WLAT, WLAT, columns // WLON, WLON, feats)
    parted = parted.transpose(2, 4, 0, 1, 3, 5, 6)
    return parted.reshape(rows // WLAT, columns // WLON * (levels // WLEV), WLEV * WLAT * WLON, feats)

def unwindows(parted, levels, rows, columns):
    feats = parted.shape[-1]
    grid = parted.reshape(rows // WLAT, columns // WLON, levels // WLEV, WLEV, WLAT, WLON, feats)
    return grid.transpose(2, 3, 0, 4, 1, 5, 6).reshape(levels, rows, columns, feats)

def class_onehot(ids, levels):
    rows, columns = ids.shape
    grid = jnp.broadcast_to(ids[None, :, :, None], (levels, rows, columns, 1))
    parted = windows(grid)
    return (parted == jnp.arange(3, dtype=jnp.int32)).astype(jnp.float32)

def region_extra(flags, levels, columns):
    rows = flags.shape[0]
    grid = jnp.broadcast_to(flags[None, :, None, None], (levels, rows, columns, 1))
    parted = windows(grid)
    gap = jnp.abs(parted - jnp.swapaxes(parted, -1, -2))
    return (NEG * gap)[..., None, :, :]

def make_bias(onehot, table):
    return jnp.einsum('nqa,hab,nkb->nhqk', onehot, table, onehot, precision=lax.Precision.HIGHEST)

def forward_windows(inputs, onehot, extra, gain, table, qkv_weight, out_weight):
    count, length, width = inputs.shape
    normed = layer_norm(inputs, gain)
    packed = jnp.dot(normed.reshape(count * length, width), qkv_weight, preferred_element_type=jnp.float32)
    packed = packed.astype(jnp.bfloat16).reshape(count, length, 3 * width)
    bias = make_bias(onehot, table) + extra
    mixed = attend(packed, bias)
    delta = jnp.dot(mixed.reshape(count * length, width), out_weight, preferred_element_type=jnp.float32)
    return (delta.reshape(count, length, width), normed, packed, mixed)

def backward_windows(inputs, onehot, extra, gain, table, qkv_weight, out_weight, normed, packed, mixed, upstream):
    count, length, width = inputs.shape
    total = count * length
    upstream_flat = upstream.reshape(total, width)
    grad_out = jnp.dot(mixed.reshape(total, width).T, upstream_flat, preferred_element_type=jnp.float32)
    d_mixed = jnp.dot(upstream_flat, out_weight.T, preferred_element_type=jnp.float32)
    d_mixed = d_mixed.astype(jnp.bfloat16).reshape(count, length, width)
    bias = make_bias(onehot, table) + extra
    _, pull_attend = jax.vjp(lambda packed_in: attend(packed_in, bias), packed)
    d_packed = pull_attend(d_mixed)[0].reshape(total, 3 * width)
    grad_qkv = jnp.dot(normed.reshape(total, width).T, d_packed, preferred_element_type=jnp.float32)
    d_normed = jnp.dot(d_packed, qkv_weight.T, preferred_element_type=jnp.float32)
    d_normed = d_normed.astype(jnp.bfloat16).reshape(count, length, width)
    _, pull_norm = jax.vjp(lambda inputs_in: layer_norm(inputs_in, gain), inputs)
    return (pull_norm(d_normed)[0], grad_qkv, grad_out)

def reference(fields, cotangent, land_ids, gain_a, table_a, qkv_weight_a, out_weight_a, gain_b, table_b, qkv_weight_b, out_weight_b):
    levels, rows, columns, width = fields.shape
    fields_wide = fields.astype(jnp.float32)
    onehot_a = class_onehot(land_ids, levels)
    zero_extra = jnp.zeros(onehot_a.shape[:2] + (1, 1, 1), jnp.float32)
    inputs_a = windows(fields_wide)

    def forward_a(items):
        return forward_windows(items[0], items[1], items[2], gain_a, table_a, qkv_weight_a, out_weight_a)
    delta_a, normed_a, packed_a, mixed_a = lax.map(forward_a, (inputs_a, onehot_a, zero_extra))
    middle = (fields_wide + unwindows(delta_a, levels, rows, columns)).astype(jnp.bfloat16)
    shift_in = (-(WLAT // 2), -(WLON // 2))
    shift_back = (WLAT // 2, WLON // 2)
    middle_rolled = jnp.roll(middle, shift_in, axis=(1, 2))
    onehot_b = class_onehot(jnp.roll(land_ids, shift_in, axis=(0, 1)), levels)
    flags = (jnp.arange(rows) >= rows - WLAT // 2).astype(jnp.float32)
    extra_b = region_extra(flags, levels, columns)
    inputs_b = windows(middle_rolled.astype(jnp.float32))

    def forward_b(items):
        return forward_windows(items[0], items[1], items[2], gain_b, table_b, qkv_weight_b, out_weight_b)
    delta_b, normed_b, packed_b, mixed_b = lax.map(forward_b, (inputs_b, onehot_b, extra_b))
    delta_grid = jnp.roll(unwindows(delta_b, levels, rows, columns), shift_back, axis=(1, 2))
    advanced = (middle.astype(jnp.float32) + delta_grid).astype(jnp.bfloat16)
    start = (jnp.zeros((width, 3 * width), jnp.float32), jnp.zeros((width, width), jnp.float32))
    upstream_b = windows(jnp.roll(cotangent, shift_in, axis=(1, 2)))

    def backward_b(carry, items):
        d_inputs, grad_qkv, grad_out = backward_windows(items[0], items[1], items[2], gain_b, table_b, qkv_weight_b, out_weight_b, items[3], items[4], items[5], items[6])
        return ((carry[0] + grad_qkv, carry[1] + grad_out), d_inputs)
    (grad_qkv_b, grad_out_b), d_inputs_b = lax.scan(backward_b, start, (inputs_b, onehot_b, extra_b, normed_b, packed_b, mixed_b, upstream_b))
    d_grid_b = jnp.roll(unwindows(d_inputs_b, levels, rows, columns), shift_back, axis=(1, 2))
    grad_middle = (cotangent.astype(jnp.float32) + d_grid_b).astype(jnp.bfloat16)

    def backward_a(carry, items):
        d_inputs, grad_qkv, grad_out = backward_windows(items[0], items[1], items[2], gain_a, table_a, qkv_weight_a, out_weight_a, items[3], items[4], items[5], items[6])
        return ((carry[0] + grad_qkv, carry[1] + grad_out), d_inputs)
    (grad_qkv_a, grad_out_a), d_inputs_a = lax.scan(backward_a, start, (inputs_a, onehot_a, zero_extra, normed_a, packed_a, mixed_a, windows(grad_middle)))
    grad_fields = (grad_middle.astype(jnp.float32) + unwindows(d_inputs_a, levels, rows, columns)).astype(jnp.bfloat16)
    return (advanced, grad_fields, grad_qkv_a, grad_out_a, grad_qkv_b, grad_out_b)
```

```python
import jax
import jax.numpy as jnp
import numpy as np
from jax import lax
from jax.experimental import pallas as pl
from jax.experimental.pallas import tpu as pltpu
from jax.sharding import PartitionSpec as P

WINDOWS = 2
LENGTH = 144
QUARTER = 36
TOKENS = WINDOWS * LENGTH
PIECE = WINDOWS * QUARTER
WIDTH = 512
HEADS = 16
HEAD = 32
GROUP = 128
GROUPS = WIDTH // GROUP
PER_GROUP = GROUP // HEAD
PADDED = 384
ROOT = HEAD**0.5
EPS = 1e-05
NEG = -1000000000.0
VMEM_LIMIT = 48 * 1024 * 1024
F32 = jnp.float32
BF16 = jnp.bfloat16


def _tables():
    place = np.zeros((TOKENS, PADDED), np.float32)
    sort = np.zeros((TOKENS, TOKENS), np.float32)
    where = np.zeros((LENGTH, 8), np.int32)
    for window in range(WINDOWS):
        for quadrant in range(4):
            for level in range(2):
                for row in range(6):
                    for column in range(3):
                        inner = level * 18 + row * 3 + column
                        at = quadrant * QUARTER + inner
                        token = window * LENGTH + at
                        lat = quadrant // 2 * 6 + row
                        lon = quadrant % 2 * 3 + column
                        source = ((2 * window + level) * 12 + lat) * 8 + lon
                        place[token, source] = 1
                        sort[quadrant * PIECE + window * QUARTER + inner, token] = 1
                        where[at, 0] = lat
                        where[at, 1] = lon
    return place, sort, where


PLACE, SORT, WHERE = _tables()


def mm(left, right):
    return jnp.dot(left, right, preferred_element_type=F32)


def mm_t(left, right):
    return lax.dot_general(left, right, (((1,), (1,)), ((), ())), preferred_element_type=F32)


def normalise(inputs):
    centre = inputs - jnp.mean(inputs, axis=-1, keepdims=True)
    spread = jnp.mean(centre * centre, axis=-1, keepdims=True)
    scale = lax.rsqrt(spread + EPS)
    return centre * scale, scale


def lanes(shape):
    return lax.broadcasted_iota(jnp.int32, shape, 1)


def head_masks():
    lane = lanes((1, GROUP))
    return [
        ((lane >= h * HEAD) & (lane < (h + 1) * HEAD)).astype(F32).astype(BF16)
        for h in range(PER_GROUP)
    ]


def bias_features(ids_ref, where_ref, table_ref, spare_ref, shift, last):
    lat_at = lax.axis_index("lat")
    lon_at = lax.axis_index("lon")
    rows, columns = ids_ref.shape
    row = where_ref[:, 0:1]
    column = where_ref[:, 1:2] + (lon_at * 6 + shift // 2)
    at = row + (lat_at * 12 + shift)
    at = jnp.where(at >= rows, at - rows, at)
    column = jnp.where(column >= columns, column - columns, column)
    pick = (lanes((LENGTH, rows)) == at).astype(F32).astype(BF16)
    found = mm(pick, ids_ref[...].astype(F32).astype(BF16))
    found = jnp.where(lanes((LENGTH, columns)) == column, found, 0.0)
    kind = jnp.sum(found, axis=1, keepdims=True).astype(jnp.int32)
    lane = lanes((LENGTH, GROUP))
    third = (lane >= 3).astype(jnp.int32) + (lane >= 6).astype(jnp.int32)
    query = ((lane < 9) & (third == kind)).astype(F32)
    key = ((lane < 3) & (lane == kind)).astype(F32)
    if last:
        flag = ((row >= 6) & (lat_at == lax.axis_size("lat") - 1)).astype(F32)
        query = jnp.where(lane == 9, flag, jnp.where(lane == 10, 1.0 - flag, query))
        key = jnp.where(lane == 3, 1.0 - flag, jnp.where(lane == 4, flag, key))
    small = (16, GROUP)
    lane = lanes(small)
    sub = lax.broadcasted_iota(jnp.int32, small, 0)
    third = (lane >= 3).astype(jnp.int32) + (lane >= 6).astype(jnp.int32)
    part = lane - 3 * third
    spots = {
        (first, second): (lane < 9) & (third == first) & (sub == second)
        for first in range(3)
        for second in range(3)
    }
    fixed = jnp.where(((sub == 3) & (lane == 9)) | ((sub == 4) & (lane == 10)), NEG * ROOT, 0.0)
    for head in range(HEADS):
        entry = fixed
        for (first, second), spot in spots.items():
            entry = jnp.where(spot, table_ref[head, first, second] * ROOT, entry)
        high = entry.astype(BF16).astype(F32)
        middle = (entry - high).astype(BF16).astype(F32)
        low = entry - high - middle
        entry = jnp.where(part == 0, high, jnp.where(part == 1, middle, low))
        entry = jnp.where(lane >= 9, high, entry)
        spare_ref[:, head * GROUP : (head + 1) * GROUP] = entry.astype(BF16)
    features = mm(key.astype(BF16)[:, :16], spare_ref[...])
    return query.astype(BF16), features.astype(BF16)


def forward_core(
    inputs, gain, qkv_ref, out_ref, query_features, key_ref, packed_ref, probs_ref, mixed_t_ref
):
    hat, _ = normalise(inputs)
    normed = (hat * gain).astype(BF16)
    packed_ref[...] = mm(normed, qkv_ref[...]).astype(BF16)
    masks = head_masks()
    factor = F32(1.0 / ROOT * np.log2(np.e))
    for window in range(WINDOWS):
        rows = slice(window * LENGTH, (window + 1) * LENGTH)
        for group in range(GROUPS):
            at = group * GROUP
            query = packed_ref[rows, at : at + GROUP]
            keys = packed_ref[rows, WIDTH + at : WIDTH + at + GROUP]
            values_t = packed_ref[rows, 2 * WIDTH + at : 2 * WIDTH + at + GROUP].T
            for h in range(PER_GROUP):
                head = group * PER_GROUP + h
                left = jnp.concatenate([keys, key_ref[:, head * GROUP : (head + 1) * GROUP]], axis=1)
                right = jnp.concatenate([query * masks[h], query_features], axis=1)
                scores = mm_t(left, right)
                top = jnp.max(scores, axis=0, keepdims=True)
                raised = jnp.exp2((scores - top) * factor)
                total = jnp.sum(raised, axis=0, keepdims=True)
                probs = (raised * (1.0 / total)).astype(BF16)
                probs_ref[window * HEADS + head] = probs
                mixed = mm(values_t[h * HEAD : (h + 1) * HEAD], probs)
                mixed_t_ref[window, head * HEAD : (head + 1) * HEAD, :] = mixed.astype(BF16)
    parts = []
    for window in range(WINDOWS):
        parts.append(mm(mixed_t_ref[window].T, out_ref[...]))
    return normed, jnp.concatenate(parts, axis=0)


def backward_core(upstream, out_ref, packed_ref, probs_ref, mixed_t_ref, d_packed_ref):
    masks = head_masks()
    for window in range(WINDOWS):
        rows = slice(window * LENGTH, (window + 1) * LENGTH)
        here = upstream[rows]
        d_mixed = mm_t(here, out_ref[...]).astype(BF16)
        d_mixed_t = mm_t(out_ref[...], here).astype(BF16)
        for group in range(GROUPS):
            at = group * GROUP
            query = packed_ref[rows, at : at + GROUP]
            keys = packed_ref[rows, WIDTH + at : WIDTH + at + GROUP]
            values = packed_ref[rows, 2 * WIDTH + at : 2 * WIDTH + at + GROUP]
            keys_t = keys.T
            up = d_mixed[:, at : at + GROUP]
            dots = d_mixed_t[at : at + GROUP].astype(F32) * mixed_t_ref[
                window, at : at + GROUP, :
            ].astype(F32)
            d_values = jnp.zeros((LENGTH, GROUP), F32)
            d_keys = jnp.zeros((LENGTH, GROUP), F32)
            d_query = []
            for h in range(PER_GROUP):
                head = group * PER_GROUP + h
                probs = probs_ref[window * HEADS + head]
                up_here = up * masks[h]
                query_here = query * masks[h]
                d_probs = mm_t(values, up_here)
                inner = jnp.sum(dots[h * HEAD : (h + 1) * HEAD], axis=0, keepdims=True)
                d_scores = probs.astype(F32) * ((d_probs - inner) * F32(1.0 / ROOT))
                d_scores = d_scores.astype(BF16)
                d_values = d_values + mm(probs, up_here)
                d_keys = d_keys + mm(d_scores, query_here)
                d_query.append(mm(keys_t[h * HEAD : (h + 1) * HEAD], d_scores))
            d_query = jnp.concatenate(d_query, axis=0).T
            d_packed_ref[rows, at : at + GROUP] = d_query.astype(BF16)
            d_packed_ref[rows, WIDTH + at : WIDTH + at + GROUP] = d_keys.astype(BF16)
            d_packed_ref[rows, 2 * WIDTH + at : 2 * WIDTH + at + GROUP] = d_values.astype(BF16)


def norm_backward(inputs, gain, d_packed, qkv_ref):
    d_normed = mm_t(d_packed, qkv_ref[...]).astype(BF16).astype(F32)
    hat, scale = normalise(inputs)
    d_hat = d_normed * gain
    mean = jnp.mean(d_hat, axis=-1, keepdims=True)
    along = jnp.mean(d_hat * hat, axis=-1, keepdims=True)
    return scale * (d_hat - mean - hat * along)


def grads_half(half, normed_t_ref, mixed_t_ref, upstream, d_packed_ref, result_ref):
    def blocks(ref, *first):
        return [
            ref[(*first, pl.ds(pl.multiple_of((2 * block + half) * 32, 32), 32), slice(None))]
            for block in range(8)
        ]

    left = jnp.concatenate(blocks(normed_t_ref), axis=0)
    result_ref[:, : 3 * WIDTH] = mm(left, d_packed_ref[...]).astype(BF16)
    total = None
    for window in range(WINDOWS):
        left = jnp.concatenate(blocks(mixed_t_ref, window), axis=0)
        part = mm(left, upstream[window * LENGTH : (window + 1) * LENGTH])
        total = part if total is None else total + part
    result_ref[:, 3 * WIDTH :] = total.astype(BF16)


def load_grid(ref, place, spare_ref):
    spare_ref[...] = jnp.zeros((PADDED, WIDTH), F32)
    for level in range(4):
        for row in range(12):
            at = (level * 12 + row) * 8
            spare_ref[at : at + 6, :] = ref[level, row].astype(F32)
    return mm(place, spare_ref[...].astype(BF16))


def store_grid(ref, place_t, tokens):
    spread = mm(place_t, tokens)
    for level in range(4):
        for row in range(12):
            at = (level * 12 + row) * 8
            ref[level, row] = spread[at : at + 6].astype(BF16)


def split_pieces(sort, first, second, refs):
    first = mm(sort, first)
    second = mm(sort, second)
    for at, ref in enumerate(refs):
        rows = slice(at * PIECE, (at + 1) * PIECE)
        ref[...] = jnp.concatenate([first[rows], second[rows]], axis=0).astype(BF16)


def join_pieces(sort_t, refs):
    wide = [ref[...].astype(F32) for ref in refs]
    first = jnp.concatenate([part[:PIECE] for part in wide], axis=0).astype(BF16)
    second = jnp.concatenate([part[PIECE:] for part in wide], axis=0).astype(BF16)
    return mm(sort_t, first), mm(sort_t, second)


def kernel_forward_a(
    fields, cotangent, ids, gain, table, qkv, out, place, sort, where,
    piece0, piece1, piece2, piece3, inputs_out, middle_out, upstream_out, normed_out, packed, probs, mixed_t,
    grid, spare, key_features,
):
    query_features, features = bias_features(ids, where, table, spare, 0, False)
    key_features[...] = features
    inputs = load_grid(fields, place[...], grid)
    inputs_out[...] = inputs.astype(BF16)
    normed, delta = forward_core(
        inputs, gain[...].reshape(1, WIDTH), qkv, out, query_features, key_features, packed, probs, mixed_t
    )
    normed_out[...] = normed
    middle = (inputs + delta).astype(BF16)
    upstream = load_grid(cotangent, place[...], grid).astype(BF16)
    middle_out[...] = middle
    upstream_out[...] = upstream
    split_pieces(sort[...], middle, upstream, (piece0, piece1, piece2, piece3))


def kernel_block_b(
    piece0, piece1, piece2, piece3, ids, gain, table, qkv, out, sort, sort_t, where,
    back0, back1, back2, back3, normed_out, upstream_out, mixed_t, d_packed,
    packed, probs, spare, key_features,
):
    query_features, features = bias_features(ids, where, table, spare, 6, True)
    key_features[...] = features
    inputs, upstream = join_pieces(sort_t[...], (piece0, piece1, piece2, piece3))
    upstream = upstream.astype(BF16)
    upstream_out[...] = upstream
    gain_row = gain[...].reshape(1, WIDTH)
    normed, delta = forward_core(
        inputs, gain_row, qkv, out, query_features, key_features, packed, probs, mixed_t
    )
    normed_out[...] = normed
    backward_core(upstream, out, packed, probs, mixed_t, d_packed)
    d_inputs = norm_backward(inputs, gain_row, d_packed[...], qkv)
    split_pieces(sort[...], delta.astype(BF16), d_inputs.astype(BF16), (back0, back1, back2, back3))


def kernel_grads(normed, mixed_t, upstream, d_packed, send, keep, normed_t):
    normed_t[...] = normed[...].T
    core = lax.axis_index("lat") % 2
    grads_half(1 - core, normed_t, mixed_t, upstream[...], d_packed, send)
    grads_half(core, normed_t, mixed_t, upstream[...], d_packed, keep)


def kernel_backward_a(
    back0, back1, back2, back3, upstream, out, packed, probs, mixed_t, normed, sort_t,
    grad_middle_out, delta_out, d_packed, send, normed_t,
):
    delta, d_inputs = join_pieces(sort_t[...], (back0, back1, back2, back3))
    delta_out[...] = delta.astype(BF16)
    grad_middle = (upstream[...].astype(F32) + d_inputs).astype(BF16)
    grad_middle_out[...] = grad_middle
    backward_core(grad_middle, out, packed, probs, mixed_t, d_packed)
    normed_t[...] = normed[...].T
    core = lax.axis_index("lat") % 2
    grads_half(1 - core, normed_t, mixed_t, grad_middle, d_packed, send)


def kernel_finish_a(
    inputs, middle, delta, grad_middle, gain, qkv, d_packed, normed_t, mixed_t, place_t,
    keep, advanced, grad_fields,
):
    core = lax.axis_index("lat") % 2
    grads_half(core, normed_t, mixed_t, grad_middle[...], d_packed, keep)
    total = (middle[...].astype(F32) + delta[...].astype(F32)).astype(BF16)
    store_grid(advanced, place_t[...], total)
    d_inputs = norm_backward(
        inputs[...].astype(F32), gain[...].reshape(1, WIDTH), d_packed[...], qkv
    )
    total = (grad_middle[...].astype(F32) + d_inputs).astype(BF16)
    store_grid(grad_fields, place_t[...], total)


def call(kernel, outs, scratch, args, in_scalar=()):
    return pl.pallas_call(
        kernel,
        out_shape=tuple(jax.ShapeDtypeStruct(shape, kind) for shape, kind in outs),
        in_specs=[
            pl.BlockSpec(memory_space=pltpu.SMEM if at in in_scalar else pltpu.VMEM)
            for at in range(len(args))
        ],
        out_specs=tuple(pl.BlockSpec(memory_space=pltpu.VMEM) for _ in outs),
        scratch_shapes=[pltpu.VMEM(shape, kind) for shape, kind in scratch],
        compiler_params=pltpu.CompilerParams(vmem_limit_bytes=VMEM_LIMIT),
    )(*args)


def permute(array, axis, target):
    length = lax.axis_size(axis)
    return lax.ppermute(array, axis, [(i, target(i) % length) for i in range(length)])


def permute_both(array, by):
    lons, lats = lax.axis_size("lon"), lax.axis_size("lat")
    pairs = [
        (lon * lats + lat, (lon + by) % lons * lats + (lat + by) % lats)
        for lon in range(lons)
        for lat in range(lats)
    ]
    return lax.ppermute(array, ("lon", "lat"), pairs)


def pick(array, at):
    return lax.dynamic_index_in_dim(array, at, 0, keepdims=False)


def add(*parts):
    return sum(part.astype(F32) for part in parts).astype(BF16)


def reduce_lat(send, keep):
    lat = lax.axis_index("lat")
    y = lat // 4
    near = lat // 2 % 2
    whole = add(keep, permute(send, "lat", lambda i: i ^ 1)).reshape(4, 2, 32, 4 * WIDTH)
    half = 2 * WIDTH
    one, two = whole[..., :half], whole[..., half:]
    got_one = permute(jnp.stack([pick(one, y ^ 1), pick(one, y ^ 2)]), "lat", lambda i: i ^ 4)
    got_two = permute(jnp.stack([pick(two, y ^ 3), pick(two, y ^ 2)]), "lat", lambda i: i ^ 12)
    keep_one = add(pick(one, y), got_one[0])
    send_one = add(pick(one, y ^ 3), got_one[1])
    keep_two = add(pick(two, y), got_two[0])
    send_two = add(pick(two, y ^ 1), got_two[1])
    last_one = permute(send_one, "lat", lambda i: i ^ 12)
    last_two = permute(send_two, "lat", lambda i: i ^ 4)
    both = jnp.concatenate([add(keep_one, last_one), add(keep_two, last_two)], axis=-1)
    got = permute(pick(both, 1 - near), "lat", lambda i: i ^ 2)
    return add(pick(both, near), got)


def by_lon(rows):
    qkv = rows[:, : 3 * WIDTH].reshape(32, 16, 96).transpose(1, 0, 2)
    out = rows[:, 3 * WIDTH :].reshape(32, 16, 32).transpose(1, 0, 2)
    return jnp.concatenate([qkv, out], axis=-1)


def reduce_lon(blocks):
    lon = lax.axis_index("lon")
    for step in (4, 1):
        at = lon // step % 4
        blocks = blocks.reshape((4, -1) + blocks.shape[1:])
        got = [pick(blocks, at)]
        for k in (1, 2, 3):
            got.append(permute(pick(blocks, at ^ k), "lon", lambda i: i ^ (step * k)))
        blocks = add(*got)
    return blocks[0]


def body(
    fields, cotangent, land_ids, gain_a, table_a, qkv_weight_a, out_weight_a,
    gain_b, table_b, qkv_weight_b, out_weight_b,
):
    place = jnp.asarray(PLACE, BF16)
    place_t = jnp.asarray(PLACE.T, BF16)
    sort = jnp.asarray(SORT, BF16)
    sort_t = jnp.asarray(SORT.T, BF16)
    where = jnp.asarray(WHERE)
    piece = ((2 * PIECE, WIDTH), BF16)
    token = ((TOKENS, WIDTH), BF16)
    packed = ((TOKENS, 3 * WIDTH), BF16)
    probs = ((WINDOWS * HEADS, LENGTH, LENGTH), BF16)
    mixed_t = ((WINDOWS, WIDTH, LENGTH), BF16)
    half_grads = ((WIDTH // 2, 4 * WIDTH), BF16)
    normed_t = ((WIDTH, TOKENS), BF16)
    spare = ((16, HEADS * GROUP), BF16)
    features = ((LENGTH, HEADS * GROUP), BF16)

    p0, p1, p2, p3, inputs_a, middle_a, upstream_a, normed_a, packed_a, probs_a, mixed_a = call(
        kernel_forward_a,
        [piece] * 4 + [token] * 4 + [packed, probs, mixed_t],
        [((PADDED, WIDTH), F32), spare, features],
        (fields, cotangent, land_ids, gain_a, table_a, qkv_weight_a, out_weight_a, place, sort, where),
        (4,),
    )
    diagonal = permute_both(p0, -1)
    below = permute(p1, "lat", lambda i: i - 1)
    eastern = permute(p2, "lon", lambda i: i - 1)
    b0, b1, b2, b3, normed_b, upstream_b, mixed_b, d_packed_b = call(
        kernel_block_b,
        [piece] * 4 + [token] * 2 + [mixed_t, packed],
        [packed, probs, spare, features],
        (p3, eastern, below, diagonal, land_ids, gain_b, table_b, qkv_weight_b, out_weight_b, sort, sort_t, where),
        (6,),
    )
    diagonal = permute_both(b3, 1)
    above = permute(b2, "lat", lambda i: i + 1)
    western = permute(b1, "lon", lambda i: i + 1)
    send_b, keep_b = call(
        kernel_grads, [half_grads] * 2, [normed_t], (normed_b, mixed_b, upstream_b, d_packed_b)
    )
    grad_middle, delta_b, d_packed_a, send_a, normed_a_t = call(
        kernel_backward_a,
        [token, token, packed, half_grads, normed_t],
        [],
        (diagonal, above, western, b0, upstream_a, out_weight_a, packed_a, probs_a, mixed_a, normed_a, sort_t),
    )
    keep_a, advanced, grad_fields = call(
        kernel_finish_a,
        [half_grads, (fields.shape, BF16), (fields.shape, BF16)],
        [],
        (inputs_a, middle_a, delta_b, grad_middle, gain_a, qkv_weight_a, d_packed_a, normed_a_t, mixed_a, place_t),
    )
    grads_b = by_lon(reduce_lat(send_b, keep_b))
    grads_a = by_lon(reduce_lat(send_a, keep_a))
    grads = reduce_lon(jnp.stack([grads_a, grads_b], axis=1)).astype(F32)
    return (
        advanced, grad_fields,
        grads[0, :, :96], grads[0, :, 96:], grads[1, :, :96], grads[1, :, 96:],
    )


def solution(mesh):
    grid = P(None, "lat", "lon", None)
    return jax.shard_map(
        body,
        mesh=mesh,
        in_specs=(grid, grid) + (P(),) * 9,
        out_specs=(grid, grid) + (P("lat", "lon"),) * 4,
        check_vma=False,
    )
```

```python
import jax
import jax.numpy as jnp
import numpy as np
from jax import lax
from jax.experimental import pallas as pl
from jax.experimental.pallas import tpu as pltpu
from jax.sharding import PartitionSpec as P

WINDOWS = 2
LENGTH = 144
QUARTER = 36
TOKENS = WINDOWS * LENGTH
PIECE = WINDOWS * QUARTER
WIDTH = 512
HEADS = 16
HEAD = 32
GROUP = 128
GROUPS = WIDTH // GROUP
PER_GROUP = GROUP // HEAD
ROOT = HEAD**0.5
EPS = 1e-05
NEG = -1000000000.0
VMEM_LIMIT = 24 * 1024 * 1024
F32 = jnp.float32
BF16 = jnp.bfloat16


def _tables():
    place = np.zeros((TOKENS, TOKENS), np.float32)
    sort = np.zeros((TOKENS, TOKENS), np.float32)
    where = np.zeros((LENGTH, 8), np.int32)
    for window in range(WINDOWS):
        for quadrant in range(4):
            for level in range(2):
                for row in range(6):
                    for column in range(3):
                        inner = level * 18 + row * 3 + column
                        at = quadrant * QUARTER + inner
                        token = window * LENGTH + at
                        lat = quadrant // 2 * 6 + row
                        lon = quadrant % 2 * 3 + column
                        source = (lat * 6 + lon) * 4 + 2 * window + level
                        place[token, source] = 1
                        sort[quadrant * PIECE + window * QUARTER + inner, token] = 1
                        where[at, 0] = lat
                        where[at, 1] = lon
    return place, sort, where


PLACE, SORT, WHERE = _tables()


def mm(left, right):
    return jnp.dot(left, right, preferred_element_type=F32)


def mm_t(left, right):
    return lax.dot_general(left, right, (((1,), (1,)), ((), ())), preferred_element_type=F32)


def normalise(inputs):
    centre = inputs - jnp.mean(inputs, axis=-1, keepdims=True)
    spread = jnp.mean(centre * centre, axis=-1, keepdims=True)
    scale = lax.rsqrt(spread + EPS)
    return centre * scale, scale


def lanes(shape):
    return lax.broadcasted_iota(jnp.int32, shape, 1)


def head_masks():
    lane = lanes((1, GROUP))
    return [
        ((lane >= h * HEAD) & (lane < (h + 1) * HEAD)).astype(F32).astype(BF16)
        for h in range(PER_GROUP)
    ]


def bias_features(ids_ref, where_ref, table_ref, spare_ref, shift, last):
    lat_at = lax.axis_index("lat")
    lon_at = lax.axis_index("lon")
    rows, columns = ids_ref.shape
    row = where_ref[:, 0:1]
    column = where_ref[:, 1:2] + (lon_at * 6 + shift // 2)
    at = row + (lat_at * 12 + shift)
    at = jnp.where(at >= rows, at - rows, at)
    column = jnp.where(column >= columns, column - columns, column)
    pick = (lanes((LENGTH, rows)) == at).astype(F32).astype(BF16)
    found = mm(pick, ids_ref[...].astype(F32).astype(BF16))
    found = jnp.where(lanes((LENGTH, columns)) == column, found, 0.0)
    kind = jnp.sum(found, axis=1, keepdims=True).astype(jnp.int32)
    lane = lanes((LENGTH, GROUP))
    third = (lane >= 3).astype(jnp.int32) + (lane >= 6).astype(jnp.int32)
    query = ((lane < 9) & (third == kind)).astype(F32)
    key = ((lane < 3) & (lane == kind)).astype(F32)
    if last:
        flag = ((row >= 6) & (lat_at == lax.axis_size("lat") - 1)).astype(F32)
        query = jnp.where(lane == 9, flag, jnp.where(lane == 10, 1.0 - flag, query))
        key = jnp.where(lane == 3, 1.0 - flag, jnp.where(lane == 4, flag, key))
    small = (16, GROUP)
    lane = lanes(small)
    sub = lax.broadcasted_iota(jnp.int32, small, 0)
    third = (lane >= 3).astype(jnp.int32) + (lane >= 6).astype(jnp.int32)
    part = lane - 3 * third
    spots = {
        (first, second): (lane < 9) & (third == first) & (sub == second)
        for first in range(3)
        for second in range(3)
    }
    fixed = jnp.where(((sub == 3) & (lane == 9)) | ((sub == 4) & (lane == 10)), NEG * ROOT, 0.0)
    for head in range(HEADS):
        entry = fixed
        for (first, second), spot in spots.items():
            entry = jnp.where(spot, table_ref[first, second, head] * ROOT, entry)
        high = entry.astype(BF16).astype(F32)
        middle = (entry - high).astype(BF16).astype(F32)
        low = entry - high - middle
        entry = jnp.where(part == 0, high, jnp.where(part == 1, middle, low))
        entry = jnp.where(lane >= 9, high, entry)
        spare_ref[:, head * GROUP : (head + 1) * GROUP] = entry.astype(BF16)
    features = mm(key.astype(BF16)[:, :16], spare_ref[...])
    return query.astype(BF16), features.astype(BF16)


def forward_core(
    inputs, gain, qkv_ref, out_ref, query_features, key_ref, packed_ref, probs_ref, mixed_t_ref, scores_ref
):
    hat, _ = normalise(inputs)
    normed = (hat * gain).astype(BF16)
    packed_ref[...] = mm(normed, qkv_ref[...]).astype(BF16)
    masks = head_masks()
    factor = F32(1.0 / ROOT * np.log2(np.e))
    for window, group, rows, at in sections():
        query = packed_ref[rows, at : at + GROUP]
        keys = packed_ref[rows, WIDTH + at : WIDTH + at + GROUP]
        for h in range(PER_GROUP):
            head = group * PER_GROUP + h
            left = jnp.concatenate([keys, key_ref[:, head * GROUP : (head + 1) * GROUP]], axis=1)
            right = jnp.concatenate([query * masks[h], query_features], axis=1)
            scores_ref[window * HEADS + head] = mm_t(left, right)
    for item in range(WINDOWS * HEADS):
        scores = scores_ref[item]
        top = jnp.max(scores, axis=0, keepdims=True)
        raised = jnp.exp2((scores - top) * factor)
        total = jnp.sum(raised, axis=0, keepdims=True)
        probs_ref[item] = (raised * (1.0 / total)).astype(BF16)
    for window, group, rows, at in sections():
        values_t = packed_ref[rows, 2 * WIDTH + at : 2 * WIDTH + at + GROUP].T
        for h in range(PER_GROUP):
            head = group * PER_GROUP + h
            mixed = mm(values_t[h * HEAD : (h + 1) * HEAD], probs_ref[window * HEADS + head])
            mixed_t_ref[window, head * HEAD : (head + 1) * HEAD, :] = mixed.astype(BF16)
    parts = [mm(mixed_t_ref[window].T, out_ref[...]) for window in range(WINDOWS)]
    return normed, jnp.concatenate(parts, axis=0)


def sections():
    for window in range(WINDOWS):
        for group in range(GROUPS):
            rows = slice(window * LENGTH, (window + 1) * LENGTH)
            yield window, group, rows, group * GROUP


def backward_core(
    upstream, out_ref, packed_ref, probs_ref, mixed_t_ref, d_packed_ref, d_probs_ref, d_scores_ref
):
    masks = head_masks()
    d_mixed = mm_t(upstream, out_ref[...]).astype(BF16)
    for window, group, rows, at in sections():
        values = packed_ref[rows, 2 * WIDTH + at : 2 * WIDTH + at + GROUP]
        up = d_mixed[rows, at : at + GROUP]
        for h in range(PER_GROUP):
            d_probs_ref[window * HEADS + group * PER_GROUP + h] = mm_t(values, up * masks[h])
    for window in range(WINDOWS):
        here = upstream[window * LENGTH : (window + 1) * LENGTH]
        d_mixed_t = mm_t(out_ref[...], here).astype(BF16)
        dots = d_mixed_t.astype(F32) * mixed_t_ref[window].astype(F32)
        for head in range(HEADS):
            item = window * HEADS + head
            inner = jnp.sum(dots[head * HEAD : (head + 1) * HEAD], axis=0, keepdims=True)
            d_scores = (d_probs_ref[item] - inner) * F32(1.0 / ROOT)
            d_scores_ref[item] = (probs_ref[item].astype(F32) * d_scores).astype(BF16)
    for window, group, rows, at in sections():
        query = packed_ref[rows, at : at + GROUP]
        keys_t = packed_ref[rows, WIDTH + at : WIDTH + at + GROUP].T
        up = d_mixed[rows, at : at + GROUP]
        d_values = None
        d_keys = None
        d_query = []
        for h in range(PER_GROUP):
            item = window * HEADS + group * PER_GROUP + h
            d_value = mm(probs_ref[item], up * masks[h])
            d_key = mm(d_scores_ref[item], query * masks[h])
            d_values = d_value if d_values is None else d_values + d_value
            d_keys = d_key if d_keys is None else d_keys + d_key
            d_query.append(mm(keys_t[h * HEAD : (h + 1) * HEAD], d_scores_ref[item]))
        d_query = jnp.concatenate(d_query, axis=0).T
        d_packed_ref[rows, at : at + GROUP] = d_query.astype(BF16)
        d_packed_ref[rows, WIDTH + at : WIDTH + at + GROUP] = d_keys.astype(BF16)
        d_packed_ref[rows, 2 * WIDTH + at : 2 * WIDTH + at + GROUP] = d_values.astype(BF16)


def norm_backward(inputs, gain, d_packed, qkv_ref):
    d_normed = mm_t(d_packed, qkv_ref[...]).astype(BF16).astype(F32)
    hat, scale = normalise(inputs)
    d_hat = d_normed * gain
    mean = jnp.mean(d_hat, axis=-1, keepdims=True)
    along = jnp.mean(d_hat * hat, axis=-1, keepdims=True)
    return scale * (d_hat - mean - hat * along)


def grads_half(half, normed_t_ref, mixed_t_ref, upstream, d_packed_ref, result_ref):
    def blocks(ref, *first):
        return [
            ref[(*first, pl.ds(pl.multiple_of((2 * block + half) * 32, 32), 32), slice(None))]
            for block in range(8)
        ]

    left = jnp.concatenate(blocks(normed_t_ref), axis=0)
    result_ref[:, : 3 * WIDTH] = mm(left, d_packed_ref[...]).astype(BF16)
    total = None
    for window in range(WINDOWS):
        left = jnp.concatenate(blocks(mixed_t_ref, window), axis=0)
        part = mm(left, upstream[window * LENGTH : (window + 1) * LENGTH])
        total = part if total is None else total + part
    result_ref[:, 3 * WIDTH :] = total.astype(BF16)


def load_grid(ref, place, spare_ref):
    for row in range(12):
        for column in range(6):
            at = (row * 6 + column) * 4
            spare_ref[at : at + 4, :] = ref[row, column].astype(F32)
    return mm(place, spare_ref[...].astype(BF16))


def store_grid(ref, place_t, tokens):
    spread = mm(place_t, tokens)
    for row in range(12):
        for column in range(6):
            at = (row * 6 + column) * 4
            ref[row, column] = spread[at : at + 4].astype(BF16)


def split_pieces(sort, tokens, refs):
    tokens = mm(sort, tokens)
    for at, ref in enumerate(refs):
        ref[...] = tokens[at * PIECE : (at + 1) * PIECE].astype(BF16)


def join_pieces(sort_t, refs):
    tokens = jnp.concatenate([ref[...].astype(F32) for ref in refs], axis=0)
    return mm(sort_t, tokens.astype(BF16))


def fetch(pairs, sems):
    copies = [
        pltpu.make_async_copy(source, target, sems.at[at])
        for at, (source, target) in enumerate(pairs)
    ]
    for copy in copies:
        copy.start()
    return copies


def kernel_forward_a(
    fields_hbm, ids_hbm, gain_hbm, table, qkv_hbm, out_hbm, place_hbm, sort_hbm, where_hbm,
    piece0, piece1, piece2, piece3, inputs_out, middle_out, normed_out, packed, probs, mixed_t,
    fields, ids, gain, qkv, out, place, sort, where, grid, spare, key_features, scores, sems,
):
    ids_in, where_in, fields_in, place_in, gain_in, qkv_in, out_in, sort_in = fetch(
        (
            (ids_hbm, ids), (where_hbm, where), (fields_hbm, fields), (place_hbm, place),
            (gain_hbm, gain), (qkv_hbm, qkv), (out_hbm, out), (sort_hbm, sort),
        ),
        sems,
    )
    ids_in.wait()
    where_in.wait()
    query_features, features = bias_features(ids, where, table, spare, 0, False)
    key_features[...] = features
    fields_in.wait()
    place_in.wait()
    inputs = load_grid(fields, place[...], grid)
    inputs_out[...] = inputs.astype(BF16)
    gain_in.wait()
    qkv_in.wait()
    out_in.wait()
    normed, delta = forward_core(
        inputs, gain[...].reshape(1, WIDTH), qkv, out, query_features, key_features,
        packed, probs, mixed_t, scores,
    )
    normed_out[...] = normed
    middle = (inputs + delta).astype(BF16)
    middle_out[...] = middle
    sort_in.wait()
    split_pieces(sort[...], middle, (piece0, piece1, piece2, piece3))


def kernel_cotangent(
    cotangent_hbm, place, sort, normed, ids, table, where,
    piece0, piece1, piece2, piece3, upstream_out, normed_t, query_out, key_out,
    cotangent, grid, spare, sems,
):
    (cotangent_in,) = fetch(((cotangent_hbm, cotangent),), sems)
    normed_t[...] = normed[...].T
    query, keys = bias_features(ids, where, table, spare, 6, True)
    query_out[...] = query
    key_out[...] = keys
    cotangent_in.wait()
    upstream = load_grid(cotangent, place[...], grid).astype(BF16)
    upstream_out[...] = upstream
    split_pieces(sort[...], upstream, (piece0, piece1, piece2, piece3))


def kernel_forward_b(
    piece0, piece1, piece2, piece3, query_features, key_features, gain, qkv, out, sort, sort_t,
    back0, back1, back2, back3, inputs_out, normed_out, packed, probs, mixed_t,
    scores,
):
    inputs = join_pieces(sort_t[...], (piece0, piece1, piece2, piece3))
    inputs_out[...] = inputs.astype(BF16)
    normed, delta = forward_core(
        inputs, gain[...].reshape(1, WIDTH), qkv, out, query_features[...], key_features,
        packed, probs, mixed_t, scores,
    )
    normed_out[...] = normed
    split_pieces(sort[...], delta.astype(BF16), (back0, back1, back2, back3))


def kernel_backward_b(
    piece0, piece1, piece2, piece3, inputs, gain, qkv, out, packed, probs, mixed_t, sort, sort_t,
    back0, back1, back2, back3, upstream_out, d_packed,
    d_probs, d_scores,
):
    upstream = join_pieces(sort_t[...], (piece0, piece1, piece2, piece3)).astype(BF16)
    upstream_out[...] = upstream
    backward_core(upstream, out, packed, probs, mixed_t, d_packed, d_probs, d_scores)
    d_inputs = norm_backward(
        inputs[...].astype(F32), gain[...].reshape(1, WIDTH), d_packed[...], qkv
    )
    split_pieces(sort[...], d_inputs.astype(BF16), (back0, back1, back2, back3))


def kernel_grads_b(normed, mixed_t, upstream, d_packed, send, keep, normed_t):
    normed_t[...] = normed[...].T
    core = lax.axis_index("lat") % 2
    grads_half(1 - core, normed_t, mixed_t, upstream[...], d_packed, send)
    grads_half(core, normed_t, mixed_t, upstream[...], d_packed, keep)


def kernel_backward_a(
    back0, back1, back2, back3, upstream, out, packed, probs, mixed_t, normed_t, sort_t,
    grad_middle_out, d_packed, send,
    d_probs, d_scores,
):
    d_inputs = join_pieces(sort_t[...], (back0, back1, back2, back3))
    grad_middle = (upstream[...].astype(F32) + d_inputs).astype(BF16)
    grad_middle_out[...] = grad_middle
    backward_core(grad_middle, out, packed, probs, mixed_t, d_packed, d_probs, d_scores)
    core = lax.axis_index("lat") % 2
    grads_half(1 - core, normed_t, mixed_t, grad_middle, d_packed, send)


def kernel_finish_a(
    back0, back1, back2, back3, inputs, middle, grad_middle, gain, qkv, d_packed, normed_t,
    mixed_t, place_t, sort_t,
    keep, advanced, grad_fields,
):
    core = lax.axis_index("lat") % 2
    grads_half(core, normed_t, mixed_t, grad_middle[...], d_packed, keep)
    delta = join_pieces(sort_t[...], (back0, back1, back2, back3))
    store_grid(advanced, place_t[...], (middle[...].astype(F32) + delta).astype(BF16))
    d_inputs = norm_backward(
        inputs[...].astype(F32), gain[...].reshape(1, WIDTH), d_packed[...], qkv
    )
    total = (grad_middle[...].astype(F32) + d_inputs).astype(BF16)
    store_grid(grad_fields, place_t[...], total)


def kernel_columns(keep_a, got_a, keep_b, got_b, result):
    for at, (keep, got) in enumerate(((keep_a, got_a), (keep_b, got_b))):
        total = keep[...].astype(F32) + got[...].astype(F32)
        for block in range(16):
            qkv = total[:, block * 96 : (block + 1) * 96]
            out = total[:, 3 * WIDTH + block * 32 : 3 * WIDTH + (block + 1) * 32]
            result[block, at] = jnp.concatenate([qkv, out], axis=1).astype(BF16)


def kernel_total(parts, qkv_a, out_a, qkv_b, out_b):
    total = parts[0].astype(F32)
    for at in range(1, 16):
        total = total + parts[at].astype(F32)
    for at, (qkv, out) in enumerate(((qkv_a, out_a), (qkv_b, out_b))):
        qkv[...] = total[at, :, :96]
        out[...] = total[at, :, 96:]


def call(kernel, outs, scratch, args, smem=(), hbm=(), copies=0, cost=None):
    def space(at):
        return pltpu.SMEM if at in smem else pl.ANY if at in hbm else pltpu.VMEM

    shapes = [pltpu.VMEM(shape, kind) for shape, kind in scratch]
    if copies:
        shapes.append(pltpu.SemaphoreType.DMA((copies,)))
    return pl.pallas_call(
        kernel,
        out_shape=tuple(jax.ShapeDtypeStruct(shape, kind) for shape, kind in outs),
        in_specs=[pl.BlockSpec(memory_space=space(at)) for at in range(len(args))],
        out_specs=tuple(pl.BlockSpec(memory_space=pltpu.VMEM) for _ in outs),
        scratch_shapes=shapes,
        cost_estimate=cost,
        compiler_params=pltpu.CompilerParams(vmem_limit_bytes=VMEM_LIMIT),
    )(*args)


def permute(array, axis, target):
    length = lax.axis_size(axis)
    return lax.ppermute(array, axis, [(i, target(i) % length) for i in range(length)])


def permute_both(array, by):
    lons, lats = lax.axis_size("lon"), lax.axis_size("lat")
    pairs = [
        (lon * lats + lat, (lon + by) % lons * lats + (lat + by) % lats)
        for lon in range(lons)
        for lat in range(lats)
    ]
    return lax.ppermute(array, ("lon", "lat"), pairs)


def pick(array, at):
    return lax.dynamic_index_in_dim(array, at, 0, keepdims=False)


def add(*parts):
    return sum(part.astype(F32) for part in parts).astype(BF16)


def reduce_rows(send, keep):
    y = lax.axis_index("lat") // 4
    whole = add(keep, permute(send, "lat", lambda i: i ^ 1)).reshape(4, 2, 32, 4 * WIDTH)
    half = 2 * WIDTH
    one, two = whole[..., :half], whole[..., half:]
    got_one = permute(jnp.stack([pick(one, y ^ 1), pick(one, y ^ 2)]), "lat", lambda i: i ^ 4)
    got_two = permute(jnp.stack([pick(two, y ^ 3), pick(two, y ^ 2)]), "lat", lambda i: i ^ 12)
    keep_one = add(pick(one, y), got_one[0])
    send_one = add(pick(one, y ^ 3), got_one[1])
    keep_two = add(pick(two, y), got_two[0])
    send_two = add(pick(two, y ^ 1), got_two[1])
    last_one = permute(send_one, "lat", lambda i: i ^ 12)
    last_two = permute(send_two, "lat", lambda i: i ^ 4)
    both = jnp.concatenate([add(keep_one, last_one), add(keep_two, last_two)], axis=-1)
    near = lax.axis_index("lat") // 2 % 2
    return pick(both, near), permute(pick(both, 1 - near), "lat", lambda i: i ^ 2)


def body(
    fields, cotangent, land_ids, gain_a, table_a, qkv_weight_a, out_weight_a,
    gain_b, table_b, qkv_weight_b, out_weight_b,
):
    place = jnp.asarray(PLACE, BF16)
    place_t = jnp.asarray(PLACE.T, BF16)
    sort = jnp.asarray(SORT, BF16)
    sort_t = jnp.asarray(SORT.T, BF16)
    where = jnp.asarray(WHERE)
    fields = fields.transpose(1, 2, 0, 3)
    cotangent = cotangent.transpose(1, 2, 0, 3)
    table_a = table_a.transpose(1, 2, 0)
    table_b = table_b.transpose(1, 2, 0)
    grid = (fields.shape, BF16)
    piece = ((PIECE, WIDTH), BF16)
    token = ((TOKENS, WIDTH), BF16)
    token_wide = ((TOKENS, WIDTH), F32)
    packed = ((TOKENS, 3 * WIDTH), BF16)
    probs = ((WINDOWS * HEADS, LENGTH, LENGTH), BF16)
    scores = ((WINDOWS * HEADS, LENGTH, LENGTH), F32)
    mixed_t = ((WINDOWS, WIDTH, LENGTH), BF16)
    half_grads = ((WIDTH // 2, 4 * WIDTH), BF16)
    normed_t = ((WIDTH, TOKENS), BF16)
    square = ((TOKENS, TOKENS), BF16)
    spare = ((16, HEADS * GROUP), BF16)
    query = ((LENGTH, GROUP), BF16)
    keys = ((LENGTH, HEADS * GROUP), BF16)
    ids = (land_ids.shape, jnp.int32)
    place_of = (where.shape, jnp.int32)
    vector = ((WIDTH,), F32)
    qkv_shape = ((WIDTH, 3 * WIDTH), BF16)
    out_shape = ((WIDTH, WIDTH), BF16)

    p0, p1, p2, p3, inputs_a, middle_a, normed_a, packed_a, probs_a, mixed_a = call(
        kernel_forward_a,
        [piece] * 4 + [token] * 3 + [packed, probs, mixed_t],
        [grid, ids, vector, qkv_shape, out_shape, square, square, place_of, token_wide, spare, keys, scores],
        (fields, land_ids, gain_a, table_a, qkv_weight_a, out_weight_a, place, sort, where),
        smem=(3,), hbm=(0, 1, 2, 4, 5, 6, 7, 8), copies=8,
    )
    diagonal = permute_both(p0, -1)
    below = permute(p1, "lat", lambda i: i - 1)
    eastern = permute(p2, "lon", lambda i: i - 1)
    c0, c1, c2, c3, upstream_a, normed_a_t, query_b, keys_b = call(
        kernel_cotangent,
        [piece] * 4 + [token, normed_t, query, keys],
        [grid, token_wide, spare],
        (cotangent, place, sort, normed_a, land_ids, table_b, where),
        smem=(5,), hbm=(0,), copies=1,
    )
    c_diagonal = permute_both(c0, -1)
    c_below = permute(c1, "lat", lambda i: i - 1)
    c_eastern = permute(c2, "lon", lambda i: i - 1)
    b0, b1, b2, b3, inputs_b, normed_b, packed_b, probs_b, mixed_b = call(
        kernel_forward_b,
        [piece] * 4 + [token] * 2 + [packed, probs, mixed_t],
        [scores],
        (p3, eastern, below, diagonal, query_b, keys_b, gain_b, qkv_weight_b, out_weight_b, sort, sort_t),
    )
    delta_diagonal = permute_both(b3, 1)
    delta_above = permute(b2, "lat", lambda i: i + 1)
    delta_western = permute(b1, "lon", lambda i: i + 1)
    d0, d1, d2, d3, upstream_b, d_packed_b = call(
        kernel_backward_b,
        [piece] * 4 + [token, packed],
        [scores, probs],
        (
            c3, c_eastern, c_below, c_diagonal, inputs_b, gain_b, qkv_weight_b, out_weight_b,
            packed_b, probs_b, mixed_b, sort, sort_t,
        ),
    )
    d_diagonal = permute_both(d3, 1)
    d_above = permute(d2, "lat", lambda i: i + 1)
    d_western = permute(d1, "lon", lambda i: i + 1)
    send_b, keep_b = call(
        kernel_grads_b, [half_grads] * 2, [normed_t], (normed_b, mixed_b, upstream_b, d_packed_b)
    )
    grad_middle, d_packed_a, send_a = call(
        kernel_backward_a,
        [token, packed, half_grads],
        [scores, probs],
        (
            d_diagonal, d_above, d_western, d0, upstream_a, out_weight_a, packed_a, probs_a,
            mixed_a, normed_a_t, sort_t,
        ),
    )
    keep_a, advanced, grad_fields = call(
        kernel_finish_a,
        [half_grads, grid, grid],
        [],
        (
            delta_diagonal, delta_above, delta_western, b0, inputs_a, middle_a, grad_middle,
            gain_a, qkv_weight_a, d_packed_a, normed_a_t, mixed_a, place_t, sort_t,
        ),
    )
    blocks = call(
        kernel_columns,
        [((16, 2, 32, GROUP), BF16)],
        [],
        reduce_rows(send_a, keep_a) + reduce_rows(send_b, keep_b),
    )[0]
    blocks = lax.all_to_all(blocks, "lon", 0, 0, tiled=True)
    grads = call(
        kernel_total,
        [((32, 96), F32), ((32, 32), F32)] * 2,
        [],
        (blocks,),
    )
    return (advanced.transpose(2, 0, 1, 3), grad_fields.transpose(2, 0, 1, 3), *grads)


def solution(mesh):
    grid = P(None, "lat", "lon", None)
    return jax.shard_map(
        body,
        mesh=mesh,
        in_specs=(grid, grid) + (P(),) * 9,
        out_specs=(grid, grid) + (P("lat", "lon"),) * 4,
        check_vma=False,
    )
```

```python
import jax
import jax.numpy as jnp
import numpy as np
from jax import lax
from jax.experimental import pallas as pl
from jax.experimental.pallas import tpu as pltpu
from jax.sharding import PartitionSpec as P

WINDOWS = 2
LENGTH = 144
QUARTER = 36
TOKENS = WINDOWS * LENGTH
PIECE = WINDOWS * QUARTER
WIDTH = 512
HEADS = 16
HEAD = 32
GROUP = 128
GROUPS = WIDTH // GROUP
PER_GROUP = GROUP // HEAD
ROOT = HEAD**0.5
EPS = 1e-05
NEG = -1000000000.0
VMEM_LIMIT = 24 * 1024 * 1024
F32 = jnp.float32
BF16 = jnp.bfloat16


def _tables():
    place = np.zeros((TOKENS, TOKENS), np.float32)
    sort = np.zeros((TOKENS, TOKENS), np.float32)
    where = np.zeros((LENGTH, 8), np.int32)
    for window in range(WINDOWS):
        for quadrant in range(4):
            for level in range(2):
                for row in range(6):
                    for column in range(3):
                        inner = level * 18 + row * 3 + column
                        at = quadrant * QUARTER + inner
                        token = window * LENGTH + at
                        lat = quadrant // 2 * 6 + row
                        lon = quadrant % 2 * 3 + column
                        source = (lat * 6 + lon) * 4 + 2 * window + level
                        place[token, source] = 1
                        sort[quadrant * PIECE + window * QUARTER + inner, token] = 1
                        where[at, 0] = lat
                        where[at, 1] = lon
    return place, sort, where


PLACE, SORT, WHERE = _tables()


def mm(left, right):
    return jnp.dot(left, right, preferred_element_type=F32)


def mm_t(left, right):
    return lax.dot_general(left, right, (((1,), (1,)), ((), ())), preferred_element_type=F32)


def normalise(inputs):
    centre = inputs - jnp.mean(inputs, axis=-1, keepdims=True)
    spread = jnp.mean(centre * centre, axis=-1, keepdims=True)
    scale = lax.rsqrt(spread + EPS)
    return centre * scale, scale


def lanes(shape):
    return lax.broadcasted_iota(jnp.int32, shape, 1)


def head_masks():
    lane = lanes((1, GROUP))
    return [
        ((lane >= h * HEAD) & (lane < (h + 1) * HEAD)).astype(F32).astype(BF16)
        for h in range(PER_GROUP)
    ]


def bias_features(ids_ref, where_ref, table_ref, spare_ref, shift, last):
    lat_at = lax.axis_index("lat")
    lon_at = lax.axis_index("lon")
    rows, columns = ids_ref.shape
    row = where_ref[:, 0:1]
    column = where_ref[:, 1:2] + (lon_at * 6 + shift // 2)
    at = row + (lat_at * 12 + shift)
    at = jnp.where(at >= rows, at - rows, at)
    column = jnp.where(column >= columns, column - columns, column)
    pick = (lanes((LENGTH, rows)) == at).astype(F32).astype(BF16)
    found = mm(pick, ids_ref[...].astype(F32).astype(BF16))
    found = jnp.where(lanes((LENGTH, columns)) == column, found, 0.0)
    kind = jnp.sum(found, axis=1, keepdims=True).astype(jnp.int32)
    lane = lanes((LENGTH, GROUP))
    third = (lane >= 3).astype(jnp.int32) + (lane >= 6).astype(jnp.int32)
    query = ((lane < 9) & (third == kind)).astype(F32)
    key = ((lane < 3) & (lane == kind)).astype(F32)
    if last:
        flag = ((row >= 6) & (lat_at == lax.axis_size("lat") - 1)).astype(F32)
        query = jnp.where(lane == 9, flag, jnp.where(lane == 10, 1.0 - flag, query))
        key = jnp.where(lane == 3, 1.0 - flag, jnp.where(lane == 4, flag, key))
    small = (16, GROUP)
    lane = lanes(small)
    sub = lax.broadcasted_iota(jnp.int32, small, 0)
    third = (lane >= 3).astype(jnp.int32) + (lane >= 6).astype(jnp.int32)
    part = lane - 3 * third
    spots = {
        (first, second): (lane < 9) & (third == first) & (sub == second)
        for first in range(3)
        for second in range(3)
    }
    fixed = jnp.where(((sub == 3) & (lane == 9)) | ((sub == 4) & (lane == 10)), NEG * ROOT, 0.0)
    for head in range(HEADS):
        entry = fixed
        for (first, second), spot in spots.items():
            entry = jnp.where(spot, table_ref[first, second, head] * ROOT, entry)
        high = entry.astype(BF16).astype(F32)
        middle = (entry - high).astype(BF16).astype(F32)
        low = entry - high - middle
        entry = jnp.where(part == 0, high, jnp.where(part == 1, middle, low))
        entry = jnp.where(lane >= 9, high, entry)
        spare_ref[:, head * GROUP : (head + 1) * GROUP] = entry.astype(BF16)
    features = mm(key.astype(BF16)[:, :16], spare_ref[...])
    return query.astype(BF16), features.astype(BF16)


def forward_core(
    inputs, gain, qkv_ref, out_ref, query_features, key_ref, packed_ref, probs_ref, mixed_t_ref, scores_ref
):
    hat, _ = normalise(inputs)
    normed = (hat * gain).astype(BF16)
    packed_ref[...] = mm(normed, qkv_ref[...]).astype(BF16)
    masks = head_masks()
    factor = F32(1.0 / ROOT * np.log2(np.e))
    for window, group, rows, at in sections():
        query = packed_ref[rows, at : at + GROUP]
        keys = packed_ref[rows, WIDTH + at : WIDTH + at + GROUP]
        for h in range(PER_GROUP):
            head = group * PER_GROUP + h
            left = jnp.concatenate([keys, key_ref[:, head * GROUP : (head + 1) * GROUP]], axis=1)
            right = jnp.concatenate([query * masks[h], query_features], axis=1)
            scores_ref[window * HEADS + head] = mm_t(left, right)
    for item in range(WINDOWS * HEADS):
        scores = scores_ref[item]
        top = jnp.max(scores, axis=0, keepdims=True)
        raised = jnp.exp2((scores - top) * factor)
        total = jnp.sum(raised, axis=0, keepdims=True)
        probs_ref[item] = (raised * (1.0 / total)).astype(BF16)
    for window, group, rows, at in sections():
        values_t = packed_ref[rows, 2 * WIDTH + at : 2 * WIDTH + at + GROUP].T
        for h in range(PER_GROUP):
            head = group * PER_GROUP + h
            mixed = mm(values_t[h * HEAD : (h + 1) * HEAD], probs_ref[window * HEADS + head])
            mixed_t_ref[window, head * HEAD : (head + 1) * HEAD, :] = mixed.astype(BF16)
    parts = [mm(mixed_t_ref[window].T, out_ref[...]) for window in range(WINDOWS)]
    return normed, jnp.concatenate(parts, axis=0)


def sections():
    for window in range(WINDOWS):
        for group in range(GROUPS):
            rows = slice(window * LENGTH, (window + 1) * LENGTH)
            yield window, group, rows, group * GROUP


def backward_core(
    upstream, out_ref, packed_ref, probs_ref, mixed_t_ref, d_packed_ref, d_probs_ref, d_scores_ref
):
    masks = head_masks()
    d_mixed = mm_t(upstream, out_ref[...]).astype(BF16)
    for window, group, rows, at in sections():
        values = packed_ref[rows, 2 * WIDTH + at : 2 * WIDTH + at + GROUP]
        up = d_mixed[rows, at : at + GROUP]
        for h in range(PER_GROUP):
            d_probs_ref[window * HEADS + group * PER_GROUP + h] = mm_t(values, up * masks[h])
    for window in range(WINDOWS):
        here = upstream[window * LENGTH : (window + 1) * LENGTH]
        d_mixed_t = mm_t(out_ref[...], here).astype(BF16)
        dots = d_mixed_t.astype(F32) * mixed_t_ref[window].astype(F32)
        for head in range(HEADS):
            item = window * HEADS + head
            inner = jnp.sum(dots[head * HEAD : (head + 1) * HEAD], axis=0, keepdims=True)
            d_scores = (d_probs_ref[item] - inner) * F32(1.0 / ROOT)
            d_scores_ref[item] = (probs_ref[item].astype(F32) * d_scores).astype(BF16)
    for window, group, rows, at in sections():
        query = packed_ref[rows, at : at + GROUP]
        keys_t = packed_ref[rows, WIDTH + at : WIDTH + at + GROUP].T
        up = d_mixed[rows, at : at + GROUP]
        d_values = None
        d_keys = None
        d_query = []
        for h in range(PER_GROUP):
            item = window * HEADS + group * PER_GROUP + h
            d_value = mm(probs_ref[item], up * masks[h])
            d_key = mm(d_scores_ref[item], query * masks[h])
            d_values = d_value if d_values is None else d_values + d_value
            d_keys = d_key if d_keys is None else d_keys + d_key
            d_query.append(mm(keys_t[h * HEAD : (h + 1) * HEAD], d_scores_ref[item]))
        d_query = jnp.concatenate(d_query, axis=0).T
        d_packed_ref[rows, at : at + GROUP] = d_query.astype(BF16)
        d_packed_ref[rows, WIDTH + at : WIDTH + at + GROUP] = d_keys.astype(BF16)
        d_packed_ref[rows, 2 * WIDTH + at : 2 * WIDTH + at + GROUP] = d_values.astype(BF16)


def norm_backward(inputs, gain, d_packed, qkv_ref):
    d_normed = mm_t(d_packed, qkv_ref[...]).astype(BF16).astype(F32)
    hat, scale = normalise(inputs)
    d_hat = d_normed * gain
    mean = jnp.mean(d_hat, axis=-1, keepdims=True)
    along = jnp.mean(d_hat * hat, axis=-1, keepdims=True)
    return scale * (d_hat - mean - hat * along)


def grads_half(half, normed_t_ref, mixed_t_ref, upstream, d_packed_ref, result_ref):
    def blocks(ref, *first):
        return [
            ref[(*first, pl.ds(pl.multiple_of((2 * block + half) * 32, 32), 32), slice(None))]
            for block in range(8)
        ]

    left = jnp.concatenate(blocks(normed_t_ref), axis=0)
    result_ref[:, : 3 * WIDTH] = mm(left, d_packed_ref[...]).astype(BF16)
    total = None
    for window in range(WINDOWS):
        left = jnp.concatenate(blocks(mixed_t_ref, window), axis=0)
        part = mm(left, upstream[window * LENGTH : (window + 1) * LENGTH])
        total = part if total is None else total + part
    result_ref[:, 3 * WIDTH :] = total.astype(BF16)


def load_grid(ref, place, spare_ref):
    for row in range(12):
        for column in range(6):
            at = (row * 6 + column) * 4
            spare_ref[at : at + 4, :] = ref[row, column].astype(F32)
    return mm(place, spare_ref[...].astype(BF16))


def store_grid(ref, place_t, tokens):
    spread = mm(place_t, tokens)
    for row in range(12):
        for column in range(6):
            at = (row * 6 + column) * 4
            ref[row, column] = spread[at : at + 4].astype(BF16)


def split_pieces(sort, tokens, refs):
    tokens = mm(sort, tokens)
    for at, ref in enumerate(refs):
        ref[...] = tokens[at * PIECE : (at + 1) * PIECE].astype(BF16)


def join_pieces(sort_t, refs):
    tokens = jnp.concatenate([ref[...].astype(F32) for ref in refs], axis=0)
    return mm(sort_t, tokens.astype(BF16))


def fetch(pairs, sems):
    copies = [
        pltpu.make_async_copy(source, target, sems.at[at])
        for at, (source, target) in enumerate(pairs)
    ]
    for copy in copies:
        copy.start()
    return copies


def kernel_forward_a(
    fields_hbm, ids_hbm, gain_hbm, table, qkv_hbm, out_hbm, place_hbm, sort_hbm, where_hbm,
    piece0, piece1, piece2, piece3, inputs_out, middle_out, normed_out, packed, probs, mixed_t,
    fields, ids, gain, qkv, out, place, sort, where, grid, spare, key_features, scores, sems,
):
    ids_in, where_in, fields_in, place_in, gain_in, qkv_in, out_in, sort_in = fetch(
        (
            (ids_hbm, ids), (where_hbm, where), (fields_hbm, fields), (place_hbm, place),
            (gain_hbm, gain), (qkv_hbm, qkv), (out_hbm, out), (sort_hbm, sort),
        ),
        sems,
    )
    ids_in.wait()
    where_in.wait()
    query_features, features = bias_features(ids, where, table, spare, 0, False)
    key_features[...] = features
    fields_in.wait()
    place_in.wait()
    inputs = load_grid(fields, place[...], grid)
    inputs_out[...] = inputs.astype(BF16)
    gain_in.wait()
    qkv_in.wait()
    out_in.wait()
    normed, delta = forward_core(
        inputs, gain[...].reshape(1, WIDTH), qkv, out, query_features, key_features,
        packed, probs, mixed_t, scores,
    )
    normed_out[...] = normed
    middle = (inputs + delta).astype(BF16)
    middle_out[...] = middle
    sort_in.wait()
    split_pieces(sort[...], middle, (piece0, piece1, piece2, piece3))


def kernel_cotangent(
    cotangent_hbm, place, sort, normed, ids, table, where,
    piece0, piece1, piece2, piece3, upstream_out, normed_t, query_out, key_out,
    cotangent, grid, spare, sems,
):
    (cotangent_in,) = fetch(((cotangent_hbm, cotangent),), sems)
    normed_t[...] = normed[...].T
    query, keys = bias_features(ids, where, table, spare, 6, True)
    query_out[...] = query
    key_out[...] = keys
    cotangent_in.wait()
    upstream = load_grid(cotangent, place[...], grid).astype(BF16)
    upstream_out[...] = upstream
    split_pieces(sort[...], upstream, (piece0, piece1, piece2, piece3))


def kernel_forward_b(
    piece0, piece1, piece2, piece3, query_features, key_features, gain, qkv, out, sort, sort_t,
    back0, back1, back2, back3, inputs_out, normed_out, packed, probs, mixed_t,
    scores,
):
    inputs = join_pieces(sort_t[...], (piece0, piece1, piece2, piece3))
    inputs_out[...] = inputs.astype(BF16)
    normed, delta = forward_core(
        inputs, gain[...].reshape(1, WIDTH), qkv, out, query_features[...], key_features,
        packed, probs, mixed_t, scores,
    )
    normed_out[...] = normed
    split_pieces(sort[...], delta.astype(BF16), (back0, back1, back2, back3))


def kernel_backward_b(
    piece0, piece1, piece2, piece3, inputs, gain, qkv, out, packed, probs, mixed_t, sort, sort_t,
    back0, back1, back2, back3, upstream_out, d_packed,
    d_probs, d_scores,
):
    upstream = join_pieces(sort_t[...], (piece0, piece1, piece2, piece3)).astype(BF16)
    upstream_out[...] = upstream
    backward_core(upstream, out, packed, probs, mixed_t, d_packed, d_probs, d_scores)
    d_inputs = norm_backward(
        inputs[...].astype(F32), gain[...].reshape(1, WIDTH), d_packed[...], qkv
    )
    split_pieces(sort[...], d_inputs.astype(BF16), (back0, back1, back2, back3))


def kernel_grads_b(normed, mixed_t, upstream, d_packed, send, keep, normed_t):
    normed_t[...] = normed[...].T
    core = lax.axis_index("lat") % 2
    grads_half(1 - core, normed_t, mixed_t, upstream[...], d_packed, send)
    grads_half(core, normed_t, mixed_t, upstream[...], d_packed, keep)


def kernel_backward_a(
    back0, back1, back2, back3, upstream, out, packed, probs, mixed_t, normed_t, sort_t,
    grad_middle_out, d_packed, send,
    d_probs, d_scores,
):
    d_inputs = join_pieces(sort_t[...], (back0, back1, back2, back3))
    grad_middle = (upstream[...].astype(F32) + d_inputs).astype(BF16)
    grad_middle_out[...] = grad_middle
    backward_core(grad_middle, out, packed, probs, mixed_t, d_packed, d_probs, d_scores)
    core = lax.axis_index("lat") % 2
    grads_half(1 - core, normed_t, mixed_t, grad_middle, d_packed, send)


def kernel_finish_a(
    inputs, grad_middle, gain, qkv_hbm, d_packed, normed_t, mixed_t, place_t,
    keep, grad_fields,
    qkv, sems,
):
    (qkv_in,) = fetch(((qkv_hbm, qkv),), sems)
    core = lax.axis_index("lat") % 2
    grads_half(core, normed_t, mixed_t, grad_middle[...], d_packed, keep)
    qkv_in.wait()
    d_inputs = norm_backward(
        inputs[...].astype(F32), gain[...].reshape(1, WIDTH), d_packed[...], qkv
    )
    total = (grad_middle[...].astype(F32) + d_inputs).astype(BF16)
    store_grid(grad_fields, place_t[...], total)


def kernel_advanced(back0, back1, back2, back3, middle, place_t, sort_t, advanced):
    delta = join_pieces(sort_t[...], (back0, back1, back2, back3))
    store_grid(advanced, place_t[...], (middle[...].astype(F32) + delta).astype(BF16))


def kernel_first_sum(keep, got, send_one, send_two, keep_one, keep_two):
    y = lax.axis_index("lat") // 4
    half = 2 * WIDTH

    def put(target, place, block, columns):
        rows = pl.ds(pl.multiple_of(block * 64, 64), 64)
        target[place] = keep[rows, columns] + got[rows, columns]

    one, two = slice(0, half), slice(half, 2 * half)
    put(send_one, 0, y ^ 1, one)
    put(send_one, 1, y ^ 2, one)
    put(send_two, 0, y ^ 3, two)
    put(send_two, 1, y ^ 2, two)
    put(keep_one, 0, y, one)
    put(keep_one, 1, y ^ 3, one)
    put(keep_two, 0, y, two)
    put(keep_two, 1, y ^ 1, two)


def kernel_second_sum(keep_one, got_one, keep_two, got_two, send_one, send_two, held_one, held_two):
    send_one[...] = keep_one[1] + got_one[1]
    send_two[...] = keep_two[1] + got_two[1]
    held_one[...] = keep_one[0] + got_one[0]
    held_two[...] = keep_two[0] + got_two[0]


def kernel_third_sum(held_one, got_one, held_two, got_two, send, keep):
    near = lax.axis_index("lat") // 2 % 2
    half = 2 * WIDTH
    for target, place in ((send, 1 - near), (keep, near)):
        rows = pl.ds(pl.multiple_of(place * 32, 32), 32)
        target[:, :half] = held_one[rows] + got_one[rows]
        target[:, half:] = held_two[rows] + got_two[rows]


def kernel_columns(keep_a, got_a, keep_b, got_b, result):
    for at, (keep, got) in enumerate(((keep_a, got_a), (keep_b, got_b))):
        total = keep[...].astype(F32) + got[...].astype(F32)
        for block in range(16):
            qkv = total[:, block * 96 : (block + 1) * 96]
            out = total[:, 3 * WIDTH + block * 32 : 3 * WIDTH + (block + 1) * 32]
            result[block, at] = jnp.concatenate([qkv, out], axis=1).astype(BF16)


def kernel_total(parts, qkv_a, out_a, qkv_b, out_b):
    total = parts[0].astype(F32)
    for at in range(1, 16):
        total = total + parts[at].astype(F32)
    for at, (qkv, out) in enumerate(((qkv_a, out_a), (qkv_b, out_b))):
        qkv[...] = total[at, :, :96]
        out[...] = total[at, :, 96:]


def call(kernel, outs, scratch, args, smem=(), hbm=(), copies=0, flops=0, final=()):
    def space(at):
        return pltpu.SMEM if at in smem else pltpu.HBM if at in hbm else pltpu.VMEM

    cost = pl.CostEstimate(flops=flops, bytes_accessed=1 << 20, transcendentals=0) if flops else None
    args = [
        pltpu.with_memory_space_constraint(arg, pltpu.HBM) if at in hbm or at in smem else arg
        for at, arg in enumerate(args)
    ]
    shapes = [pltpu.VMEM(shape, kind) for shape, kind in scratch]
    if copies:
        shapes.append(pltpu.SemaphoreType.DMA((copies,)))
    return pl.pallas_call(
        kernel,
        out_shape=tuple(
            jax.ShapeDtypeStruct(shape, kind) if at in final else pltpu.VMEM(shape, kind)
            for at, (shape, kind) in enumerate(outs)
        ),
        in_specs=[pl.BlockSpec(memory_space=space(at)) for at in range(len(args))],
        out_specs=tuple(pl.BlockSpec(memory_space=pltpu.VMEM) for _ in outs),
        scratch_shapes=shapes,
        cost_estimate=cost,
        compiler_params=pltpu.CompilerParams(vmem_limit_bytes=VMEM_LIMIT),
    )(*args)


def permute(array, axis, target):
    length = lax.axis_size(axis)
    return lax.ppermute(array, axis, [(i, target(i) % length) for i in range(length)])


def permute_both(array, by):
    lons, lats = lax.axis_size("lon"), lax.axis_size("lat")
    pairs = [
        (lon * lats + lat, (lon + by) % lons * lats + (lat + by) % lats)
        for lon in range(lons)
        for lat in range(lats)
    ]
    return lax.ppermute(array, ("lon", "lat"), pairs)


def first_round(send, keep):
    return keep, permute(send, "lat", lambda i: i ^ 1)


def first_sum(keep, got):
    return call(kernel_first_sum, [((2, 64, 2 * WIDTH), BF16)] * 4, [], (keep, got))


def second_round(send_one, send_two, keep_one, keep_two):
    got_one = permute(send_one, "lat", lambda i: i ^ 4)
    got_two = permute(send_two, "lat", lambda i: i ^ 12)
    return keep_one, got_one, keep_two, got_two


def second_sum(*parts):
    return call(kernel_second_sum, [((64, 2 * WIDTH), BF16)] * 4, [], parts)


def third_round(send_one, send_two, held_one, held_two):
    got_one = permute(send_one, "lat", lambda i: i ^ 12)
    got_two = permute(send_two, "lat", lambda i: i ^ 4)
    return held_one, got_one, held_two, got_two


def fourth_round(*parts):
    rows = ((32, 4 * WIDTH), BF16)
    send, keep = call(kernel_third_sum, [rows] * 2, [], parts)
    return keep, permute(send, "lat", lambda i: i ^ 2)


def body(
    fields, cotangent, land_ids, gain_a, table_a, qkv_weight_a, out_weight_a,
    gain_b, table_b, qkv_weight_b, out_weight_b,
):
    place = jnp.asarray(PLACE, BF16)
    place_t = jnp.asarray(PLACE.T, BF16)
    sort = jnp.asarray(SORT, BF16)
    sort_t = jnp.asarray(SORT.T, BF16)
    where = jnp.asarray(WHERE)
    fields = fields.transpose(1, 2, 0, 3)
    cotangent = cotangent.transpose(1, 2, 0, 3)
    table_a = table_a.transpose(1, 2, 0)
    table_b = table_b.transpose(1, 2, 0)
    grid = (fields.shape, BF16)
    piece = ((PIECE, WIDTH), BF16)
    token = ((TOKENS, WIDTH), BF16)
    token_wide = ((TOKENS, WIDTH), F32)
    packed = ((TOKENS, 3 * WIDTH), BF16)
    probs = ((WINDOWS * HEADS, LENGTH, LENGTH), BF16)
    scores = ((WINDOWS * HEADS, LENGTH, LENGTH), F32)
    mixed_t = ((WINDOWS, WIDTH, LENGTH), BF16)
    half_grads = ((WIDTH // 2, 4 * WIDTH), BF16)
    normed_t = ((WIDTH, TOKENS), BF16)
    square = ((TOKENS, TOKENS), BF16)
    spare = ((16, HEADS * GROUP), BF16)
    query = ((LENGTH, GROUP), BF16)
    keys = ((LENGTH, HEADS * GROUP), BF16)
    ids = (land_ids.shape, jnp.int32)
    place_of = (where.shape, jnp.int32)
    vector = ((WIDTH,), F32)
    qkv_shape = ((WIDTH, 3 * WIDTH), BF16)
    out_shape = ((WIDTH, WIDTH), BF16)

    p0, p1, p2, p3, inputs_a, middle_a, normed_a, packed_a, probs_a, mixed_a = call(
        kernel_forward_a,
        [piece] * 4 + [token] * 3 + [packed, probs, mixed_t],
        [grid, ids, vector, qkv_shape, out_shape, square, square, place_of, token_wide, spare, keys, scores],
        (fields, land_ids, gain_a, table_a, qkv_weight_a, out_weight_a, place, sort, where),
        smem=(3,), hbm=(0, 1, 2, 4, 5, 6, 7, 8), copies=8, flops=7 * 10**9,
    )
    diagonal = permute_both(p0, -1)
    below = permute(p1, "lat", lambda i: i - 1)
    eastern = permute(p2, "lon", lambda i: i - 1)
    c0, c1, c2, c3, upstream_a, normed_a_t, query_b, keys_b = call(
        kernel_cotangent,
        [piece] * 4 + [token, normed_t, query, keys],
        [grid, token_wide, spare],
        (cotangent, place, sort, normed_a, land_ids, table_b, where),
        smem=(5,), hbm=(0,), copies=1, flops=2 * 10**9,
    )
    c_diagonal = permute_both(c0, -1)
    c_below = permute(c1, "lat", lambda i: i - 1)
    c_eastern = permute(c2, "lon", lambda i: i - 1)
    b0, b1, b2, b3, inputs_b, normed_b, packed_b, probs_b, mixed_b = call(
        kernel_forward_b,
        [piece] * 4 + [token] * 2 + [packed, probs, mixed_t],
        [scores],
        (p3, eastern, below, diagonal, query_b, keys_b, gain_b, qkv_weight_b, out_weight_b, sort, sort_t),
        flops=5 * 10**9,
    )
    d0, d1, d2, d3, upstream_b, d_packed_b = call(
        kernel_backward_b,
        [piece] * 4 + [token, packed],
        [scores, probs],
        (
            c3, c_eastern, c_below, c_diagonal, inputs_b, gain_b, qkv_weight_b, out_weight_b,
            packed_b, probs_b, mixed_b, sort, sort_t,
        ),
        flops=5 * 10**9,
    )
    d_diagonal = permute_both(d3, 1)
    d_above = permute(d2, "lat", lambda i: i + 1)
    d_western = permute(d1, "lon", lambda i: i + 1)
    send_b, keep_b = call(
        kernel_grads_b, [half_grads] * 2, [normed_t], (normed_b, mixed_b, upstream_b, d_packed_b),
        flops=2 * 10**9,
    )
    sums_b = first_sum(*first_round(send_b, keep_b))
    rounds_b = second_round(*sums_b)
    grad_middle, d_packed_a, send_a = call(
        kernel_backward_a,
        [token, packed, half_grads],
        [scores, probs],
        (
            d_diagonal, d_above, d_western, d0, upstream_a, out_weight_a, packed_a, probs_a,
            mixed_a, normed_a_t, sort_t,
        ),
        flops=5 * 10**9,
    )
    sums_b = second_sum(*rounds_b)
    rounds_b = third_round(*sums_b)
    keep_a, grad_fields = call(
        kernel_finish_a,
        [half_grads, grid],
        [qkv_shape],
        (inputs_a, grad_middle, gain_a, qkv_weight_a, d_packed_a, normed_a_t, mixed_a, place_t),
        hbm=(3,), copies=1, flops=4 * 10**9, final=(1,),
    )
    sums_a = first_sum(*first_round(send_a, keep_a))
    sums_a, b1, b2, b3 = lax.optimization_barrier((sums_a, b1, b2, b3))
    rounds_a = second_round(*sums_a)
    delta_diagonal = permute_both(b3, 1)
    delta_above = permute(b2, "lat", lambda i: i + 1)
    delta_western = permute(b1, "lon", lambda i: i + 1)
    rounds_b = fourth_round(*rounds_b)
    sums_a = second_sum(*rounds_a)
    sums_a, b0 = lax.optimization_barrier((sums_a, b0))
    advanced = call(
        kernel_advanced,
        [grid],
        [],
        (delta_diagonal, delta_above, delta_western, b0, middle_a, place_t, sort_t),
        flops=10**9, final=(0,),
    )[0]
    rounds_a = fourth_round(*third_round(*sums_a))
    blocks = call(
        kernel_columns, [((16, 2, 32, GROUP), BF16)], [], rounds_a + rounds_b, final=(0,)
    )[0]
    blocks = lax.all_to_all(blocks, "lon", 0, 0, tiled=True)
    grads = call(
        kernel_total,
        [((32, 96), F32), ((32, 32), F32)] * 2,
        [],
        (blocks,),
        final=(0, 1, 2, 3),
    )
    return (advanced.transpose(2, 0, 1, 3), grad_fields.transpose(2, 0, 1, 3), *grads)


def solution(mesh):
    grid = P(None, "lat", "lon", None)
    return jax.shard_map(
        body,
        mesh=mesh,
        in_specs=(grid, grid) + (P(),) * 9,
        out_specs=(grid, grid) + (P("lat", "lon"),) * 4,
        check_vma=False,
    )
```

```python
import jax
import jax.numpy as jnp
import numpy as np
from jax import lax
from jax.experimental import pallas as pl
from jax.experimental.pallas import tpu as pltpu
from jax.sharding import PartitionSpec as P

WINDOWS = 2
LENGTH = 144
QUARTER = 36
TOKENS = WINDOWS * LENGTH
PIECE = WINDOWS * QUARTER
WIDTH = 512
HEADS = 16
HEAD = 32
GROUP = 128
GROUPS = WIDTH // GROUP
PER_GROUP = GROUP // HEAD
ROOT = HEAD**0.5
EPS = 1e-05
NEG = -1000000000.0
VMEM_LIMIT = 24 * 1024 * 1024
F32 = jnp.float32
BF16 = jnp.bfloat16


def _tables():
    place = np.zeros((TOKENS, TOKENS), np.float32)
    sort = np.zeros((TOKENS, TOKENS), np.float32)
    where = np.zeros((LENGTH, 8), np.int32)
    for window in range(WINDOWS):
        for quadrant in range(4):
            for level in range(2):
                for row in range(6):
                    for column in range(3):
                        inner = level * 18 + row * 3 + column
                        at = quadrant * QUARTER + inner
                        token = window * LENGTH + at
                        lat = quadrant // 2 * 6 + row
                        lon = quadrant % 2 * 3 + column
                        source = (lat * 6 + lon) * 4 + 2 * window + level
                        place[token, source] = 1
                        sort[quadrant * PIECE + window * QUARTER + inner, token] = 1
                        where[at, 0] = lat
                        where[at, 1] = lon
    return place, sort, where


PLACE, SORT, WHERE = _tables()


def mm(left, right):
    return jnp.dot(left, right, preferred_element_type=F32)


def mm_t(left, right):
    return lax.dot_general(left, right, (((1,), (1,)), ((), ())), preferred_element_type=F32)


def normalise(inputs):
    centre = inputs - jnp.mean(inputs, axis=-1, keepdims=True)
    spread = jnp.mean(centre * centre, axis=-1, keepdims=True)
    scale = lax.rsqrt(spread + EPS)
    return centre * scale, scale


def lanes(shape):
    return lax.broadcasted_iota(jnp.int32, shape, 1)


def head_masks():
    lane = lanes((1, GROUP))
    return [
        ((lane >= h * HEAD) & (lane < (h + 1) * HEAD)).astype(F32).astype(BF16)
        for h in range(PER_GROUP)
    ]


def bias_features(ids_ref, where_ref, table_ref, spare_ref, shift, last):
    lat_at = lax.axis_index("lat")
    lon_at = lax.axis_index("lon")
    rows, columns = ids_ref.shape
    row = where_ref[:, 0:1]
    column = where_ref[:, 1:2] + (lon_at * 6 + shift // 2)
    at = row + (lat_at * 12 + shift)
    at = jnp.where(at >= rows, at - rows, at)
    column = jnp.where(column >= columns, column - columns, column)
    pick = (lanes((LENGTH, rows)) == at).astype(F32).astype(BF16)
    found = mm(pick, ids_ref[...].astype(F32).astype(BF16))
    found = jnp.where(lanes((LENGTH, columns)) == column, found, 0.0)
    kind = jnp.sum(found, axis=1, keepdims=True).astype(jnp.int32)
    lane = lanes((LENGTH, GROUP))
    third = (lane >= 3).astype(jnp.int32) + (lane >= 6).astype(jnp.int32)
    query = ((lane < 9) & (third == kind)).astype(F32)
    key = ((lane < 3) & (lane == kind)).astype(F32)
    if last:
        flag = ((row >= 6) & (lat_at == lax.axis_size("lat") - 1)).astype(F32)
        query = jnp.where(lane == 9, flag, jnp.where(lane == 10, 1.0 - flag, query))
        key = jnp.where(lane == 3, 1.0 - flag, jnp.where(lane == 4, flag, key))
    small = (16, GROUP)
    lane = lanes(small)
    sub = lax.broadcasted_iota(jnp.int32, small, 0)
    third = (lane >= 3).astype(jnp.int32) + (lane >= 6).astype(jnp.int32)
    part = lane - 3 * third
    spots = {
        (first, second): (lane < 9) & (third == first) & (sub == second)
        for first in range(3)
        for second in range(3)
    }
    fixed = jnp.where(((sub == 3) & (lane == 9)) | ((sub == 4) & (lane == 10)), NEG * ROOT, 0.0)
    for head in range(HEADS):
        entry = fixed
        for (first, second), spot in spots.items():
            entry = jnp.where(spot, table_ref[first, second, head] * ROOT, entry)
        high = entry.astype(BF16).astype(F32)
        middle = (entry - high).astype(BF16).astype(F32)
        low = entry - high - middle
        entry = jnp.where(part == 0, high, jnp.where(part == 1, middle, low))
        entry = jnp.where(lane >= 9, high, entry)
        spare_ref[:, head * GROUP : (head + 1) * GROUP] = entry.astype(BF16)
    features = mm(key.astype(BF16)[:, :16], spare_ref[...])
    return query.astype(BF16), features.astype(BF16)


def forward_core(
    inputs, gain, qkv_ref, out_ref, query_features, key_ref, packed_ref, probs_ref, mixed_t_ref, scores_ref
):
    hat, _ = normalise(inputs)
    normed = (hat * gain).astype(BF16)
    packed_ref[...] = mm(normed, qkv_ref[...]).astype(BF16)
    masks = head_masks()
    factor = F32(1.0 / ROOT * np.log2(np.e))
    for window, group, rows, at in sections():
        query = packed_ref[rows, at : at + GROUP]
        keys = packed_ref[rows, WIDTH + at : WIDTH + at + GROUP]
        for h in range(PER_GROUP):
            head = group * PER_GROUP + h
            left = jnp.concatenate([keys, key_ref[:, head * GROUP : (head + 1) * GROUP]], axis=1)
            right = jnp.concatenate([query * masks[h], query_features], axis=1)
            scores_ref[window * HEADS + head] = mm_t(left, right)
    for item in range(WINDOWS * HEADS):
        scores = scores_ref[item]
        top = jnp.max(scores, axis=0, keepdims=True)
        raised = jnp.exp2((scores - top) * factor)
        total = jnp.sum(raised, axis=0, keepdims=True)
        probs_ref[item] = (raised * (1.0 / total)).astype(BF16)
    for window, group, rows, at in sections():
        values_t = packed_ref[rows, 2 * WIDTH + at : 2 * WIDTH + at + GROUP].T
        for h in range(PER_GROUP):
            head = group * PER_GROUP + h
            mixed = mm(values_t[h * HEAD : (h + 1) * HEAD], probs_ref[window * HEADS + head])
            mixed_t_ref[window, head * HEAD : (head + 1) * HEAD, :] = mixed.astype(BF16)
    parts = [mm(mixed_t_ref[window].T, out_ref[...]) for window in range(WINDOWS)]
    return normed, jnp.concatenate(parts, axis=0)


def sections():
    for window in range(WINDOWS):
        for group in range(GROUPS):
            rows = slice(window * LENGTH, (window + 1) * LENGTH)
            yield window, group, rows, group * GROUP


def backward_core(
    upstream, out_ref, packed_ref, probs_ref, mixed_t_ref, d_packed_ref, d_probs_ref, d_scores_ref
):
    masks = head_masks()
    d_mixed = mm_t(upstream, out_ref[...]).astype(BF16)
    for window, group, rows, at in sections():
        values = packed_ref[rows, 2 * WIDTH + at : 2 * WIDTH + at + GROUP]
        up = d_mixed[rows, at : at + GROUP]
        for h in range(PER_GROUP):
            d_probs_ref[window * HEADS + group * PER_GROUP + h] = mm_t(values, up * masks[h])
    for window in range(WINDOWS):
        here = upstream[window * LENGTH : (window + 1) * LENGTH]
        d_mixed_t = mm_t(out_ref[...], here).astype(BF16)
        dots = d_mixed_t.astype(F32) * mixed_t_ref[window].astype(F32)
        for head in range(HEADS):
            item = window * HEADS + head
            inner = jnp.sum(dots[head * HEAD : (head + 1) * HEAD], axis=0, keepdims=True)
            d_scores = (d_probs_ref[item] - inner) * F32(1.0 / ROOT)
            d_scores_ref[item] = (probs_ref[item].astype(F32) * d_scores).astype(BF16)
    for window, group, rows, at in sections():
        query = packed_ref[rows, at : at + GROUP]
        keys_t = packed_ref[rows, WIDTH + at : WIDTH + at + GROUP].T
        up = d_mixed[rows, at : at + GROUP]
        d_values = None
        d_keys = None
        d_query = []
        for h in range(PER_GROUP):
            item = window * HEADS + group * PER_GROUP + h
            d_value = mm(probs_ref[item], up * masks[h])
            d_key = mm(d_scores_ref[item], query * masks[h])
            d_values = d_value if d_values is None else d_values + d_value
            d_keys = d_key if d_keys is None else d_keys + d_key
            d_query.append(mm(keys_t[h * HEAD : (h + 1) * HEAD], d_scores_ref[item]))
        d_query = jnp.concatenate(d_query, axis=0).T
        d_packed_ref[rows, at : at + GROUP] = d_query.astype(BF16)
        d_packed_ref[rows, WIDTH + at : WIDTH + at + GROUP] = d_keys.astype(BF16)
        d_packed_ref[rows, 2 * WIDTH + at : 2 * WIDTH + at + GROUP] = d_values.astype(BF16)


def norm_backward(inputs, gain, d_packed, qkv_ref):
    d_normed = mm_t(d_packed, qkv_ref[...]).astype(BF16).astype(F32)
    hat, scale = normalise(inputs)
    d_hat = d_normed * gain
    mean = jnp.mean(d_hat, axis=-1, keepdims=True)
    along = jnp.mean(d_hat * hat, axis=-1, keepdims=True)
    return scale * (d_hat - mean - hat * along)


def grads_half(half, normed_t_ref, mixed_t_ref, upstream, d_packed_ref, result_ref):
    def blocks(ref, *first):
        return [
            ref[(*first, pl.ds(pl.multiple_of((2 * block + half) * 32, 32), 32), slice(None))]
            for block in range(8)
        ]

    left = jnp.concatenate(blocks(normed_t_ref), axis=0)
    result_ref[:, : 3 * WIDTH] = mm(left, d_packed_ref[...]).astype(BF16)
    total = None
    for window in range(WINDOWS):
        left = jnp.concatenate(blocks(mixed_t_ref, window), axis=0)
        part = mm(left, upstream[window * LENGTH : (window + 1) * LENGTH])
        total = part if total is None else total + part
    result_ref[:, 3 * WIDTH :] = total.astype(BF16)


def load_grid(ref, place, spare_ref):
    for row in range(12):
        for column in range(6):
            at = (row * 6 + column) * 4
            spare_ref[at : at + 4, :] = ref[row, column].astype(F32)
    return mm(place, spare_ref[...].astype(BF16))


def store_grid(ref, place_t, tokens):
    spread = mm(place_t, tokens)
    for row in range(12):
        for column in range(6):
            at = (row * 6 + column) * 4
            ref[row, column] = spread[at : at + 4].astype(BF16)


def split_pieces(sort, tokens, refs):
    tokens = mm(sort, tokens)
    for at, ref in enumerate(refs):
        ref[...] = tokens[at * PIECE : (at + 1) * PIECE].astype(BF16)


def join_pieces(sort_t, refs):
    tokens = jnp.concatenate([ref[...].astype(F32) for ref in refs], axis=0)
    return mm(sort_t, tokens.astype(BF16))


def fetch(pairs, sems):
    copies = [
        pltpu.make_async_copy(source, target, sems.at[at])
        for at, (source, target) in enumerate(pairs)
    ]
    for copy in copies:
        copy.start()
    return copies


def kernel_forward_a(
    fields_hbm, ids_hbm, gain_hbm, table, qkv_hbm, out_hbm, place_hbm, sort_hbm, where_hbm,
    piece0, piece1, piece2, piece3, inputs_out, middle_out, normed_out, packed, probs, mixed_t,
    fields, ids, gain, qkv, out, place, sort, where, grid, spare, key_features, scores, sems,
):
    ids_in, where_in, fields_in, place_in, gain_in, qkv_in, out_in, sort_in = fetch(
        (
            (ids_hbm, ids), (where_hbm, where), (fields_hbm, fields), (place_hbm, place),
            (gain_hbm, gain), (qkv_hbm, qkv), (out_hbm, out), (sort_hbm, sort),
        ),
        sems,
    )
    ids_in.wait()
    where_in.wait()
    query_features, features = bias_features(ids, where, table, spare, 0, False)
    key_features[...] = features
    fields_in.wait()
    place_in.wait()
    inputs = load_grid(fields, place[...], grid)
    inputs_out[...] = inputs.astype(BF16)
    gain_in.wait()
    qkv_in.wait()
    out_in.wait()
    normed, delta = forward_core(
        inputs, gain[...].reshape(1, WIDTH), qkv, out, query_features, key_features,
        packed, probs, mixed_t, scores,
    )
    normed_out[...] = normed
    middle = (inputs + delta).astype(BF16)
    middle_out[...] = middle
    sort_in.wait()
    split_pieces(sort[...], middle, (piece0, piece1, piece2, piece3))


def kernel_cotangent(
    cotangent_hbm, place, sort, normed, ids, table, where,
    piece0, piece1, piece2, piece3, upstream_out, normed_t, query_out, key_out,
    cotangent, grid, spare, sems,
):
    (cotangent_in,) = fetch(((cotangent_hbm, cotangent),), sems)
    normed_t[...] = normed[...].T
    query, keys = bias_features(ids, where, table, spare, 6, True)
    query_out[...] = query
    key_out[...] = keys
    cotangent_in.wait()
    upstream = load_grid(cotangent, place[...], grid).astype(BF16)
    upstream_out[...] = upstream
    split_pieces(sort[...], upstream, (piece0, piece1, piece2, piece3))


def kernel_forward_b(
    piece0, piece1, piece2, piece3, query_features, key_features, gain, qkv, out, sort, sort_t,
    back0, back1, back2, back3, inputs_out, normed_out, packed, probs, mixed_t,
    scores,
):
    inputs = join_pieces(sort_t[...], (piece0, piece1, piece2, piece3))
    inputs_out[...] = inputs.astype(BF16)
    normed, delta = forward_core(
        inputs, gain[...].reshape(1, WIDTH), qkv, out, query_features[...], key_features,
        packed, probs, mixed_t, scores,
    )
    normed_out[...] = normed
    split_pieces(sort[...], delta.astype(BF16), (back0, back1, back2, back3))


def kernel_backward_b(
    piece0, piece1, piece2, piece3, inputs, gain, qkv, out, packed, probs, mixed_t, sort, sort_t,
    back0, back1, back2, back3, upstream_out, d_packed,
    d_probs, d_scores,
):
    upstream = join_pieces(sort_t[...], (piece0, piece1, piece2, piece3)).astype(BF16)
    upstream_out[...] = upstream
    backward_core(upstream, out, packed, probs, mixed_t, d_packed, d_probs, d_scores)
    d_inputs = norm_backward(
        inputs[...].astype(F32), gain[...].reshape(1, WIDTH), d_packed[...], qkv
    )
    split_pieces(sort[...], d_inputs.astype(BF16), (back0, back1, back2, back3))


def kernel_grads_b(normed, mixed_t, upstream, d_packed, send, keep, normed_t):
    normed_t[...] = normed[...].T
    core = lax.axis_index("lat") % 2
    grads_half(1 - core, normed_t, mixed_t, upstream[...], d_packed, send)
    grads_half(core, normed_t, mixed_t, upstream[...], d_packed, keep)


def kernel_backward_a(
    back0, back1, back2, back3, upstream, out, packed, probs, mixed_t, normed_t, sort_t,
    grad_middle_out, d_packed, send,
    d_probs, d_scores,
):
    d_inputs = join_pieces(sort_t[...], (back0, back1, back2, back3))
    grad_middle = (upstream[...].astype(F32) + d_inputs).astype(BF16)
    grad_middle_out[...] = grad_middle
    backward_core(grad_middle, out, packed, probs, mixed_t, d_packed, d_probs, d_scores)
    core = lax.axis_index("lat") % 2
    grads_half(1 - core, normed_t, mixed_t, grad_middle, d_packed, send)


def kernel_keep_a(normed_t, mixed_t, grad_middle, d_packed, keep):
    core = lax.axis_index("lat") % 2
    grads_half(core, normed_t, mixed_t, grad_middle[...], d_packed, keep)


def kernel_finish_a(
    inputs, grad_middle, gain, qkv_hbm, d_packed, place_t, grad_fields, qkv, sems
):
    (qkv_in,) = fetch(((qkv_hbm, qkv),), sems)
    qkv_in.wait()
    d_inputs = norm_backward(
        inputs[...].astype(F32), gain[...].reshape(1, WIDTH), d_packed[...], qkv
    )
    total = (grad_middle[...].astype(F32) + d_inputs).astype(BF16)
    store_grid(grad_fields, place_t[...], total)


def kernel_advanced(back0, back1, back2, back3, middle, place_t, sort_t, advanced):
    delta = join_pieces(sort_t[...], (back0, back1, back2, back3))
    store_grid(advanced, place_t[...], (middle[...].astype(F32) + delta).astype(BF16))


def kernel_first_sum(keep, got, send_one, send_two, keep_one, keep_two):
    y = lax.axis_index("lat") // 4
    half = 2 * WIDTH

    def put(target, place, block, columns):
        rows = pl.ds(pl.multiple_of(block * 64, 64), 64)
        target[place] = keep[rows, columns] + got[rows, columns]

    one, two = slice(0, half), slice(half, 2 * half)
    put(send_one, 0, y ^ 1, one)
    put(send_one, 1, y ^ 2, one)
    put(send_two, 0, y ^ 3, two)
    put(send_two, 1, y ^ 2, two)
    put(keep_one, 0, y, one)
    put(keep_one, 1, y ^ 3, one)
    put(keep_two, 0, y, two)
    put(keep_two, 1, y ^ 1, two)


def kernel_second_sum(keep_one, got_one, keep_two, got_two, send_one, send_two, held_one, held_two):
    send_one[...] = keep_one[1] + got_one[1]
    send_two[...] = keep_two[1] + got_two[1]
    held_one[...] = keep_one[0] + got_one[0]
    held_two[...] = keep_two[0] + got_two[0]


def kernel_third_sum(held_one, got_one, held_two, got_two, send, keep):
    near = lax.axis_index("lat") // 2 % 2
    half = 2 * WIDTH
    for target, place in ((send, 1 - near), (keep, near)):
        rows = pl.ds(pl.multiple_of(place * 32, 32), 32)
        target[:, :half] = held_one[rows] + got_one[rows]
        target[:, half:] = held_two[rows] + got_two[rows]


def kernel_columns(keep_a, got_a, keep_b, got_b, result):
    for at, (keep, got) in enumerate(((keep_a, got_a), (keep_b, got_b))):
        total = keep[...].astype(F32) + got[...].astype(F32)
        for block in range(16):
            qkv = total[:, block * 96 : (block + 1) * 96]
            out = total[:, 3 * WIDTH + block * 32 : 3 * WIDTH + (block + 1) * 32]
            result[block, at] = jnp.concatenate([qkv, out], axis=1).astype(BF16)


def kernel_total(parts, qkv_a, out_a, qkv_b, out_b):
    total = parts[0].astype(F32)
    for at in range(1, 16):
        total = total + parts[at].astype(F32)
    for at, (qkv, out) in enumerate(((qkv_a, out_a), (qkv_b, out_b))):
        qkv[...] = total[at, :, :96]
        out[...] = total[at, :, 96:]


def call(kernel, outs, scratch, args, smem=(), hbm=(), copies=0, flops=0, final=()):
    def space(at):
        return pltpu.SMEM if at in smem else pltpu.HBM if at in hbm else pltpu.VMEM

    cost = pl.CostEstimate(flops=flops, bytes_accessed=1 << 20, transcendentals=0) if flops else None
    args = [
        pltpu.with_memory_space_constraint(arg, pltpu.HBM) if at in hbm or at in smem else arg
        for at, arg in enumerate(args)
    ]
    shapes = [pltpu.VMEM(shape, kind) for shape, kind in scratch]
    if copies:
        shapes.append(pltpu.SemaphoreType.DMA((copies,)))
    return pl.pallas_call(
        kernel,
        out_shape=tuple(
            jax.ShapeDtypeStruct(shape, kind) if at in final else pltpu.VMEM(shape, kind)
            for at, (shape, kind) in enumerate(outs)
        ),
        in_specs=[pl.BlockSpec(memory_space=space(at)) for at in range(len(args))],
        out_specs=tuple(pl.BlockSpec(memory_space=pltpu.VMEM) for _ in outs),
        scratch_shapes=shapes,
        cost_estimate=cost,
        compiler_params=pltpu.CompilerParams(vmem_limit_bytes=VMEM_LIMIT),
    )(*args)


def permute(array, axis, target):
    length = lax.axis_size(axis)
    return lax.ppermute(array, axis, [(i, target(i) % length) for i in range(length)])


def permute_both(array, by):
    lons, lats = lax.axis_size("lon"), lax.axis_size("lat")
    pairs = [
        (lon * lats + lat, (lon + by) % lons * lats + (lat + by) % lats)
        for lon in range(lons)
        for lat in range(lats)
    ]
    return lax.ppermute(array, ("lon", "lat"), pairs)


def first_round(send, keep):
    return keep, permute(send, "lat", lambda i: i ^ 1)


def first_sum(keep, got):
    return call(kernel_first_sum, [((2, 64, 2 * WIDTH), BF16)] * 4, [], (keep, got))


def second_round(send_one, send_two, keep_one, keep_two):
    got_one = permute(send_one, "lat", lambda i: i ^ 4)
    got_two = permute(send_two, "lat", lambda i: i ^ 12)
    return keep_one, got_one, keep_two, got_two


def second_sum(*parts):
    return call(kernel_second_sum, [((64, 2 * WIDTH), BF16)] * 4, [], parts)


def third_round(send_one, send_two, held_one, held_two):
    got_one = permute(send_one, "lat", lambda i: i ^ 12)
    got_two = permute(send_two, "lat", lambda i: i ^ 4)
    return held_one, got_one, held_two, got_two


def fourth_round(*parts):
    rows = ((32, 4 * WIDTH), BF16)
    send, keep = call(kernel_third_sum, [rows] * 2, [], parts)
    return keep, permute(send, "lat", lambda i: i ^ 2)


def body(
    fields, cotangent, land_ids, gain_a, table_a, qkv_weight_a, out_weight_a,
    gain_b, table_b, qkv_weight_b, out_weight_b,
):
    place = jnp.asarray(PLACE, BF16)
    place_t = jnp.asarray(PLACE.T, BF16)
    sort = jnp.asarray(SORT, BF16)
    sort_t = jnp.asarray(SORT.T, BF16)
    where = jnp.asarray(WHERE)
    fields = fields.transpose(1, 2, 0, 3)
    cotangent = cotangent.transpose(1, 2, 0, 3)
    table_a = table_a.transpose(1, 2, 0)
    table_b = table_b.transpose(1, 2, 0)
    grid = (fields.shape, BF16)
    piece = ((PIECE, WIDTH), BF16)
    token = ((TOKENS, WIDTH), BF16)
    token_wide = ((TOKENS, WIDTH), F32)
    packed = ((TOKENS, 3 * WIDTH), BF16)
    probs = ((WINDOWS * HEADS, LENGTH, LENGTH), BF16)
    scores = ((WINDOWS * HEADS, LENGTH, LENGTH), F32)
    mixed_t = ((WINDOWS, WIDTH, LENGTH), BF16)
    half_grads = ((WIDTH // 2, 4 * WIDTH), BF16)
    normed_t = ((WIDTH, TOKENS), BF16)
    square = ((TOKENS, TOKENS), BF16)
    spare = ((16, HEADS * GROUP), BF16)
    query = ((LENGTH, GROUP), BF16)
    keys = ((LENGTH, HEADS * GROUP), BF16)
    ids = (land_ids.shape, jnp.int32)
    place_of = (where.shape, jnp.int32)
    vector = ((WIDTH,), F32)
    qkv_shape = ((WIDTH, 3 * WIDTH), BF16)
    out_shape = ((WIDTH, WIDTH), BF16)

    p0, p1, p2, p3, inputs_a, middle_a, normed_a, packed_a, probs_a, mixed_a = call(
        kernel_forward_a,
        [piece] * 4 + [token] * 3 + [packed, probs, mixed_t],
        [grid, ids, vector, qkv_shape, out_shape, square, square, place_of, token_wide, spare, keys, scores],
        (fields, land_ids, gain_a, table_a, qkv_weight_a, out_weight_a, place, sort, where),
        smem=(3,), hbm=(0, 1, 2, 4, 5, 6, 7, 8), copies=8, flops=7 * 10**9,
    )
    diagonal = permute_both(p0, -1)
    below = permute(p1, "lat", lambda i: i - 1)
    eastern = permute(p2, "lon", lambda i: i - 1)
    c0, c1, c2, c3, upstream_a, normed_a_t, query_b, keys_b = call(
        kernel_cotangent,
        [piece] * 4 + [token, normed_t, query, keys],
        [grid, token_wide, spare],
        (cotangent, place, sort, normed_a, land_ids, table_b, where),
        smem=(5,), hbm=(0,), copies=1, flops=2 * 10**9,
    )
    c_diagonal = permute_both(c0, -1)
    c_below = permute(c1, "lat", lambda i: i - 1)
    c_eastern = permute(c2, "lon", lambda i: i - 1)
    b0, b1, b2, b3, inputs_b, normed_b, packed_b, probs_b, mixed_b = call(
        kernel_forward_b,
        [piece] * 4 + [token] * 2 + [packed, probs, mixed_t],
        [scores],
        (p3, eastern, below, diagonal, query_b, keys_b, gain_b, qkv_weight_b, out_weight_b, sort, sort_t),
        flops=5 * 10**9,
    )
    d0, d1, d2, d3, upstream_b, d_packed_b = call(
        kernel_backward_b,
        [piece] * 4 + [token, packed],
        [scores, probs],
        (
            c3, c_eastern, c_below, c_diagonal, inputs_b, gain_b, qkv_weight_b, out_weight_b,
            packed_b, probs_b, mixed_b, sort, sort_t,
        ),
        flops=5 * 10**9,
    )
    d_diagonal = permute_both(d3, 1)
    d_above = permute(d2, "lat", lambda i: i + 1)
    d_western = permute(d1, "lon", lambda i: i + 1)
    send_b, keep_b = call(
        kernel_grads_b, [half_grads] * 2, [normed_t], (normed_b, mixed_b, upstream_b, d_packed_b),
        flops=2 * 10**9,
    )
    sums_b = first_sum(*first_round(send_b, keep_b))
    sums_b, d0 = lax.optimization_barrier((sums_b, d0))
    rounds_b = second_round(*sums_b)
    grad_middle, d_packed_a, send_a = call(
        kernel_backward_a,
        [token, packed, half_grads],
        [scores, probs],
        (
            d_diagonal, d_above, d_western, d0, upstream_a, out_weight_a, packed_a, probs_a,
            mixed_a, normed_a_t, sort_t,
        ),
        flops=5 * 10**9,
    )
    rounds_b, send_a = lax.optimization_barrier((rounds_b, send_a))
    sums_b = second_sum(*rounds_b)
    rounds_b = third_round(*sums_b)
    keep_a = call(
        kernel_keep_a, [half_grads], [], (normed_a_t, mixed_a, grad_middle, d_packed_a),
        flops=10**9,
    )[0]
    sums_a = first_sum(*first_round(send_a, keep_a))
    sums_a, b1, b2, b3, d_packed_a = lax.optimization_barrier((sums_a, b1, b2, b3, d_packed_a))
    rounds_a = second_round(*sums_a)
    grad_fields = call(
        kernel_finish_a,
        [grid],
        [qkv_shape],
        (inputs_a, grad_middle, gain_a, qkv_weight_a, d_packed_a, place_t),
        hbm=(3,), copies=1, flops=4 * 10**9, final=(0,),
    )[0]
    delta_diagonal = permute_both(b3, 1)
    delta_above = permute(b2, "lat", lambda i: i + 1)
    delta_western = permute(b1, "lon", lambda i: i + 1)
    sums_a = second_sum(*rounds_a)
    sums_a, grad_fields = lax.optimization_barrier((sums_a, grad_fields))
    rounds_b = fourth_round(*rounds_b)
    rounds_a = fourth_round(*third_round(*sums_a))
    blocks = call(
        kernel_columns, [((16, 2, 32, GROUP), BF16)], [], rounds_a + rounds_b, final=(0,)
    )[0]
    blocks, delta_diagonal, delta_above, delta_western = lax.optimization_barrier(
        (blocks, delta_diagonal, delta_above, delta_western)
    )
    advanced = call(
        kernel_advanced,
        [grid],
        [],
        (delta_diagonal, delta_above, delta_western, b0, middle_a, place_t, sort_t),
        flops=10**9, final=(0,),
    )[0]
    blocks = lax.all_to_all(blocks, "lon", 0, 0, tiled=True)
    grads = call(
        kernel_total,
        [((32, 96), F32), ((32, 32), F32)] * 2,
        [],
        (blocks,),
        final=(0, 1, 2, 3),
    )
    return (advanced.transpose(2, 0, 1, 3), grad_fields.transpose(2, 0, 1, 3), *grads)


def solution(mesh):
    grid = P(None, "lat", "lon", None)
    return jax.shard_map(
        body,
        mesh=mesh,
        in_specs=(grid, grid) + (P(),) * 9,
        out_specs=(grid, grid) + (P("lat", "lon"),) * 4,
        check_vma=False,
    )
```

```python
import jax
import jax.numpy as jnp
import numpy as np
from jax import lax
from jax.experimental import pallas as pl
from jax.experimental.pallas import tpu as pltpu
from jax.sharding import PartitionSpec as P

WINDOWS = 2
LENGTH = 144
QUARTER = 36
TOKENS = WINDOWS * LENGTH
PIECE = WINDOWS * QUARTER
WIDTH = 512
HEADS = 16
HEAD = 32
GROUP = 128
GROUPS = WIDTH // GROUP
PER_GROUP = GROUP // HEAD
ROOT = HEAD**0.5
SIDE = 2 * WIDTH
EPS = 1e-05
NEG = -1000000000.0
VMEM_LIMIT = 24 * 1024 * 1024
F32 = jnp.float32
BF16 = jnp.bfloat16


def _tables():
    place = np.zeros((TOKENS, TOKENS), np.float32)
    sort = np.zeros((TOKENS, TOKENS), np.float32)
    where = np.zeros((LENGTH, 8), np.int32)
    for window in range(WINDOWS):
        for quadrant in range(4):
            for level in range(2):
                for row in range(6):
                    for column in range(3):
                        inner = level * 18 + row * 3 + column
                        at = quadrant * QUARTER + inner
                        token = window * LENGTH + at
                        lat = quadrant // 2 * 6 + row
                        lon = quadrant % 2 * 3 + column
                        source = (lat * 6 + lon) * 4 + 2 * window + level
                        place[token, source] = 1
                        sort[quadrant * PIECE + window * QUARTER + inner, token] = 1
                        where[at, 0] = lat
                        where[at, 1] = lon
    return place, sort, where


PLACE, SORT, WHERE = _tables()


def mm(left, right):
    return jnp.dot(left, right, preferred_element_type=F32)


def mm_t(left, right):
    return lax.dot_general(left, right, (((1,), (1,)), ((), ())), preferred_element_type=F32)


def normalise(inputs):
    centre = inputs - jnp.mean(inputs, axis=-1, keepdims=True)
    spread = jnp.mean(centre * centre, axis=-1, keepdims=True)
    scale = lax.rsqrt(spread + EPS)
    return centre * scale, scale


def lanes(shape):
    return lax.broadcasted_iota(jnp.int32, shape, 1)


def head_masks():
    lane = lanes((1, GROUP))
    return [
        ((lane >= h * HEAD) & (lane < (h + 1) * HEAD)).astype(F32).astype(BF16)
        for h in range(PER_GROUP)
    ]


def bias_features(ids_ref, where_ref, table_ref, spare_ref, shift, last):
    lat_at = lax.axis_index("lat")
    lon_at = lax.axis_index("lon")
    rows, columns = ids_ref.shape
    row = where_ref[:, 0:1]
    column = where_ref[:, 1:2] + (lon_at * 6 + shift // 2)
    at = row + (lat_at * 12 + shift)
    at = jnp.where(at >= rows, at - rows, at)
    column = jnp.where(column >= columns, column - columns, column)
    pick = (lanes((LENGTH, rows)) == at).astype(F32).astype(BF16)
    found = mm(pick, ids_ref[...].astype(F32).astype(BF16))
    found = jnp.where(lanes((LENGTH, columns)) == column, found, 0.0)
    kind = jnp.sum(found, axis=1, keepdims=True).astype(jnp.int32)
    lane = lanes((LENGTH, GROUP))
    third = (lane >= 3).astype(jnp.int32) + (lane >= 6).astype(jnp.int32)
    query = ((lane < 9) & (third == kind)).astype(F32)
    key = ((lane < 3) & (lane == kind)).astype(F32)
    if last:
        flag = ((row >= 6) & (lat_at == lax.axis_size("lat") - 1)).astype(F32)
        query = jnp.where(lane == 9, flag, jnp.where(lane == 10, 1.0 - flag, query))
        key = jnp.where(lane == 3, 1.0 - flag, jnp.where(lane == 4, flag, key))
    small = (16, GROUP)
    lane = lanes(small)
    sub = lax.broadcasted_iota(jnp.int32, small, 0)
    third = (lane >= 3).astype(jnp.int32) + (lane >= 6).astype(jnp.int32)
    part = lane - 3 * third
    spots = {
        (first, second): (lane < 9) & (third == first) & (sub == second)
        for first in range(3)
        for second in range(3)
    }
    fixed = jnp.where(((sub == 3) & (lane == 9)) | ((sub == 4) & (lane == 10)), NEG * ROOT, 0.0)
    for head in range(HEADS):
        entry = fixed
        for (first, second), spot in spots.items():
            entry = jnp.where(spot, table_ref[first, second, head] * ROOT, entry)
        high = entry.astype(BF16).astype(F32)
        middle = (entry - high).astype(BF16).astype(F32)
        low = entry - high - middle
        entry = jnp.where(part == 0, high, jnp.where(part == 1, middle, low))
        entry = jnp.where(lane >= 9, high, entry)
        spare_ref[:, head * GROUP : (head + 1) * GROUP] = entry.astype(BF16)
    features = mm(key.astype(BF16)[:, :16], spare_ref[...])
    return query.astype(BF16), features.astype(BF16)


def forward_core(
    inputs, gain, qkv_ref, out_ref, query_features, key_ref, packed_ref, probs_ref, mixed_t_ref, scores_ref
):
    hat, _ = normalise(inputs)
    normed = (hat * gain).astype(BF16)
    packed_ref[...] = mm(normed, qkv_ref[...]).astype(BF16)
    masks = head_masks()
    factor = F32(1.0 / ROOT * np.log2(np.e))
    for window, group, rows, at in sections():
        query = packed_ref[rows, at : at + GROUP]
        keys = packed_ref[rows, WIDTH + at : WIDTH + at + GROUP]
        for h in range(PER_GROUP):
            head = group * PER_GROUP + h
            left = jnp.concatenate([keys, key_ref[:, head * GROUP : (head + 1) * GROUP]], axis=1)
            right = jnp.concatenate([query * masks[h], query_features], axis=1)
            scores_ref[window * HEADS + head] = mm_t(left, right)
    for item in range(WINDOWS * HEADS):
        scores = scores_ref[item]
        top = jnp.max(scores, axis=0, keepdims=True)
        raised = jnp.exp2((scores - top) * factor)
        total = jnp.sum(raised, axis=0, keepdims=True)
        probs_ref[item] = (raised * (1.0 / total)).astype(BF16)
    for window, group, rows, at in sections():
        values_t = packed_ref[rows, 2 * WIDTH + at : 2 * WIDTH + at + GROUP].T
        for h in range(PER_GROUP):
            head = group * PER_GROUP + h
            mixed = mm(values_t[h * HEAD : (h + 1) * HEAD], probs_ref[window * HEADS + head])
            mixed_t_ref[window, head * HEAD : (head + 1) * HEAD, :] = mixed.astype(BF16)
    parts = [mm(mixed_t_ref[window].T, out_ref[...]) for window in range(WINDOWS)]
    return normed, jnp.concatenate(parts, axis=0)


def sections():
    for window in range(WINDOWS):
        for group in range(GROUPS):
            rows = slice(window * LENGTH, (window + 1) * LENGTH)
            yield window, group, rows, group * GROUP


def backward_core(
    upstream, out_ref, packed_ref, probs_ref, mixed_t_ref, d_packed_ref, d_probs_ref, d_scores_ref
):
    masks = head_masks()
    d_mixed = mm_t(upstream, out_ref[...]).astype(BF16)
    for window, group, rows, at in sections():
        values = packed_ref[rows, 2 * WIDTH + at : 2 * WIDTH + at + GROUP]
        up = d_mixed[rows, at : at + GROUP]
        for h in range(PER_GROUP):
            d_probs_ref[window * HEADS + group * PER_GROUP + h] = mm_t(values, up * masks[h])
    for window in range(WINDOWS):
        here = upstream[window * LENGTH : (window + 1) * LENGTH]
        d_mixed_t = mm_t(out_ref[...], here).astype(BF16)
        dots = d_mixed_t.astype(F32) * mixed_t_ref[window].astype(F32)
        for head in range(HEADS):
            item = window * HEADS + head
            inner = jnp.sum(dots[head * HEAD : (head + 1) * HEAD], axis=0, keepdims=True)
            d_scores = (d_probs_ref[item] - inner) * F32(1.0 / ROOT)
            d_scores_ref[item] = (probs_ref[item].astype(F32) * d_scores).astype(BF16)
    for window, group, rows, at in sections():
        query = packed_ref[rows, at : at + GROUP]
        keys_t = packed_ref[rows, WIDTH + at : WIDTH + at + GROUP].T
        up = d_mixed[rows, at : at + GROUP]
        d_values = None
        d_keys = None
        d_query = []
        for h in range(PER_GROUP):
            item = window * HEADS + group * PER_GROUP + h
            d_value = mm(probs_ref[item], up * masks[h])
            d_key = mm(d_scores_ref[item], query * masks[h])
            d_values = d_value if d_values is None else d_values + d_value
            d_keys = d_key if d_keys is None else d_keys + d_key
            d_query.append(mm(keys_t[h * HEAD : (h + 1) * HEAD], d_scores_ref[item]))
        d_query = jnp.concatenate(d_query, axis=0).T
        d_packed_ref[rows, at : at + GROUP] = d_query.astype(BF16)
        d_packed_ref[rows, WIDTH + at : WIDTH + at + GROUP] = d_keys.astype(BF16)
        d_packed_ref[rows, 2 * WIDTH + at : 2 * WIDTH + at + GROUP] = d_values.astype(BF16)


def norm_backward(inputs, gain, d_packed, qkv_ref):
    d_normed = mm_t(d_packed, qkv_ref[...]).astype(BF16).astype(F32)
    hat, scale = normalise(inputs)
    d_hat = d_normed * gain
    mean = jnp.mean(d_hat, axis=-1, keepdims=True)
    along = jnp.mean(d_hat * hat, axis=-1, keepdims=True)
    return scale * (d_hat - mean - hat * along)


def grads_half(half, normed_t_ref, mixed_t_ref, upstream, d_packed_ref, result_ref):
    def blocks(ref, *first):
        return [
            ref[(*first, pl.ds(pl.multiple_of((2 * block + half) * 32, 32), 32), slice(None))]
            for block in range(8)
        ]

    left = jnp.concatenate(blocks(normed_t_ref), axis=0)
    qkv = mm(left, d_packed_ref[...]).astype(BF16)
    total = None
    for window in range(WINDOWS):
        left = jnp.concatenate(blocks(mixed_t_ref, window), axis=0)
        part = mm(left, upstream[window * LENGTH : (window + 1) * LENGTH])
        total = part if total is None else total + part
    total = total.astype(BF16)
    result_ref[:, :768] = qkv[:, :768]
    result_ref[:, 768:SIDE] = total[:, :256]
    result_ref[:, SIDE : SIDE + 768] = qkv[:, 768:]
    result_ref[:, SIDE + 768 :] = total[:, 256:]


def load_grid(ref, place, spare_ref):
    for row in range(12):
        for column in range(6):
            at = (row * 6 + column) * 4
            spare_ref[at : at + 4, :] = ref[row, column].astype(F32)
    return mm(place, spare_ref[...].astype(BF16))


def store_grid(ref, place_t, tokens):
    spread = mm(place_t, tokens)
    for row in range(12):
        for column in range(6):
            at = (row * 6 + column) * 4
            ref[row, column] = spread[at : at + 4].astype(BF16)


def split_pieces(sort, tokens, refs):
    tokens = mm(sort, tokens)
    for at, ref in enumerate(refs):
        ref[...] = tokens[at * PIECE : (at + 1) * PIECE].astype(BF16)


def join_pieces(sort_t, refs):
    tokens = jnp.concatenate([ref[...].astype(F32) for ref in refs], axis=0)
    return mm(sort_t, tokens.astype(BF16))


def fetch(pairs, sems):
    copies = [
        pltpu.make_async_copy(source, target, sems.at[at])
        for at, (source, target) in enumerate(pairs)
    ]
    for copy in copies:
        copy.start()
    return copies


def kernel_forward_a(
    fields_hbm, ids_hbm, gain_hbm, table, qkv_hbm, out_hbm, place_hbm, sort_hbm, where_hbm,
    piece0, piece1, piece2, piece3, inputs_out, middle_out, normed_out, packed, probs, mixed_t,
    fields, ids, gain, qkv, out, place, sort, where, grid, spare, key_features, scores, sems,
):
    ids_in, where_in, fields_in, place_in, gain_in, qkv_in, out_in, sort_in = fetch(
        (
            (ids_hbm, ids), (where_hbm, where), (fields_hbm, fields), (place_hbm, place),
            (gain_hbm, gain), (qkv_hbm, qkv), (out_hbm, out), (sort_hbm, sort),
        ),
        sems,
    )
    ids_in.wait()
    where_in.wait()
    query_features, features = bias_features(ids, where, table, spare, 0, False)
    key_features[...] = features
    fields_in.wait()
    place_in.wait()
    inputs = load_grid(fields, place[...], grid)
    inputs_out[...] = inputs.astype(BF16)
    gain_in.wait()
    qkv_in.wait()
    out_in.wait()
    normed, delta = forward_core(
        inputs, gain[...].reshape(1, WIDTH), qkv, out, query_features, key_features,
        packed, probs, mixed_t, scores,
    )
    normed_out[...] = normed
    middle = (inputs + delta).astype(BF16)
    middle_out[...] = middle
    sort_in.wait()
    split_pieces(sort[...], middle, (piece0, piece1, piece2, piece3))


def kernel_cotangent(
    cotangent_hbm, place, sort, normed, ids, table, where,
    piece0, piece1, piece2, piece3, upstream_out, normed_t, query_out, key_out,
    cotangent, grid, spare, sems,
):
    (cotangent_in,) = fetch(((cotangent_hbm, cotangent),), sems)
    normed_t[...] = normed[...].T
    query, keys = bias_features(ids, where, table, spare, 6, True)
    query_out[...] = query
    key_out[...] = keys
    cotangent_in.wait()
    upstream = load_grid(cotangent, place[...], grid).astype(BF16)
    upstream_out[...] = upstream
    split_pieces(sort[...], upstream, (piece0, piece1, piece2, piece3))


def kernel_forward_b(
    piece0, piece1, piece2, piece3, query_features, key_features, gain, qkv, out, sort, sort_t,
    back0, back1, back2, back3, inputs_out, normed_out, packed, probs, mixed_t,
    scores,
):
    inputs = join_pieces(sort_t[...], (piece0, piece1, piece2, piece3))
    inputs_out[...] = inputs.astype(BF16)
    normed, delta = forward_core(
        inputs, gain[...].reshape(1, WIDTH), qkv, out, query_features[...], key_features,
        packed, probs, mixed_t, scores,
    )
    normed_out[...] = normed
    split_pieces(sort[...], delta.astype(BF16), (back0, back1, back2, back3))


def kernel_backward_b(
    piece0, piece1, piece2, piece3, inputs, gain, qkv, out, packed, probs, mixed_t, sort, sort_t,
    back0, back1, back2, back3, upstream_out, d_packed,
    d_probs, d_scores,
):
    upstream = join_pieces(sort_t[...], (piece0, piece1, piece2, piece3)).astype(BF16)
    upstream_out[...] = upstream
    backward_core(upstream, out, packed, probs, mixed_t, d_packed, d_probs, d_scores)
    d_inputs = norm_backward(
        inputs[...].astype(F32), gain[...].reshape(1, WIDTH), d_packed[...], qkv
    )
    split_pieces(sort[...], d_inputs.astype(BF16), (back0, back1, back2, back3))


def kernel_grads_b(normed, mixed_t, upstream, d_packed, send, keep, normed_t):
    normed_t[...] = normed[...].T
    core = lax.axis_index("lat") % 2
    grads_half(1 - core, normed_t, mixed_t, upstream[...], d_packed, send)
    grads_half(core, normed_t, mixed_t, upstream[...], d_packed, keep)


def kernel_backward_a(
    back0, back1, back2, back3, upstream, out, packed, probs, mixed_t, normed_t, sort_t,
    grad_middle_out, d_packed, send,
    d_probs, d_scores,
):
    d_inputs = join_pieces(sort_t[...], (back0, back1, back2, back3))
    grad_middle = (upstream[...].astype(F32) + d_inputs).astype(BF16)
    grad_middle_out[...] = grad_middle
    backward_core(grad_middle, out, packed, probs, mixed_t, d_packed, d_probs, d_scores)
    core = lax.axis_index("lat") % 2
    grads_half(1 - core, normed_t, mixed_t, grad_middle, d_packed, send)


def kernel_keep_a(normed_t, mixed_t, grad_middle, d_packed, keep):
    core = lax.axis_index("lat") % 2
    grads_half(core, normed_t, mixed_t, grad_middle[...], d_packed, keep)


def kernel_finish_a(
    inputs, grad_middle, gain, qkv_hbm, d_packed, place_t, grad_fields, qkv, sems
):
    (qkv_in,) = fetch(((qkv_hbm, qkv),), sems)
    qkv_in.wait()
    d_inputs = norm_backward(
        inputs[...].astype(F32), gain[...].reshape(1, WIDTH), d_packed[...], qkv
    )
    total = (grad_middle[...].astype(F32) + d_inputs).astype(BF16)
    store_grid(grad_fields, place_t[...], total)


def kernel_advanced(back0, back1, back2, back3, middle, place_t, sort_t, advanced):
    delta = join_pieces(sort_t[...], (back0, back1, back2, back3))
    store_grid(advanced, place_t[...], (middle[...].astype(F32) + delta).astype(BF16))


def rows_of(block, count):
    return pl.ds(pl.multiple_of(block * count, count), count)


def place_x():
    return lax.axis_index("lon") // 8 * 2 + lax.axis_index("lat") // 2 % 2


def place_y():
    return lax.axis_index("lat") // 4


def kernel_first_sum_a(keep, got, send_one, send_two, keep_one, keep_two):
    y = place_y()
    for side, first, send, kept in ((0, 1, send_one, keep_one), (1, 3, send_two, keep_two)):
        columns = slice(side * SIDE, (side + 1) * SIDE)
        for target, place, block in (
            (send, 0, y ^ first), (send, 1, y ^ 2), (kept, 0, y), (kept, 1, y ^ 2 ^ first)
        ):
            rows = rows_of(block, 64)
            target[place] = keep[rows, columns] + got[rows, columns]


def kernel_first_sum_b(keep, got, send_one, send_two, keep_one, keep_two):
    x = place_x()
    for part, first, send, kept in ((0, 1, send_one, keep_one), (1, 3, send_two, keep_two)):
        for target, place, block in (
            (send, 0, x ^ first), (send, 1, x ^ 2), (kept, 0, x), (kept, 1, x ^ 2 ^ first)
        ):
            columns = rows_of(block // 2, SIDE)
            for inner in range(2):
                rows = rows_of((part * 2 + inner) * 2 + block % 2, 32)
                target[place, inner * 32 : (inner + 1) * 32] = keep[rows, columns] + got[rows, columns]


def kernel_second_sum(keep_one, got_one, keep_two, got_two, send_one, send_two, held_one, held_two):
    send_one[...] = keep_one[1] + got_one[1]
    send_two[...] = keep_two[1] + got_two[1]
    held_one[...] = keep_one[0] + got_one[0]
    held_two[...] = keep_two[0] + got_two[0]


def third_sum(at, halves, send, keep):
    for target, place, block in ((send, 0, at ^ 1), (send, 1, at ^ 2), (keep, 0, at), (keep, 1, at ^ 3)):
        rows = rows_of(block % 2, 32)
        for half, (held, got) in enumerate(halves):

            @pl.when(block // 2 == half)
            def _(target=target, place=place, rows=rows, held=held, got=got):
                target[place] = held[rows, :] + got[rows, :]


def kernel_third_sum_a(held_one, got_one, held_two, got_two, send, keep):
    third_sum(place_x(), ((held_one, got_one), (held_two, got_two)), send, keep)


def kernel_third_sum_b(held_one, got_one, held_two, got_two, send, keep):
    third_sum(place_y(), ((held_one, got_one), (held_two, got_two)), send, keep)


def kernel_halve(keep, got, send, held):
    half = keep.shape[0] // 2
    held[...] = keep[:half] + got[:half]
    send[...] = keep[half:] + got[half:]


def z_partner(z, step):
    if step == 0:
        return z ^ 1
    if step == 1:
        return (z + 2 * (z & 1) + 7) & 7
    return z ^ (3 + 4 * (((z + 1) >> 1) & 1))


def z_blocks(z):
    other = z_partner(z, 1)
    return z, z_partner(z, 2), other, z_partner(other, 2)


def kernel_columns(keep_a, got_a, keep_b, got_b, send, keep, blocks):
    for at, (held, got) in enumerate(((keep_a, got_a), (keep_b, got_b))):
        total = held[0].astype(F32) + got[0].astype(F32)
        for block in range(8):
            qkv = total[:, block * 96 : (block + 1) * 96]
            out = total[:, 768 + block * 32 : 768 + (block + 1) * 32]
            blocks[block, at] = jnp.concatenate([qkv, out], axis=1).astype(BF16)
    z = lax.axis_index("lon") % 8
    for target, owner in ((send, z_partner(z, 0)), (keep, z)):
        for at, block in enumerate(z_blocks(owner)):
            target[at] = blocks[block]


def kernel_total(keep, got, qkv_a, out_a, qkv_b, out_b):
    total = keep[0].astype(F32) + got[0].astype(F32)
    for at, (qkv, out) in enumerate(((qkv_a, out_a), (qkv_b, out_b))):
        qkv[...] = total[at, :, :96]
        out[...] = total[at, :, 96:]


def call(kernel, outs, scratch, args, smem=(), hbm=(), copies=0, flops=0, final=()):
    def space(at):
        return pltpu.SMEM if at in smem else pltpu.HBM if at in hbm else pltpu.VMEM

    cost = pl.CostEstimate(flops=flops, bytes_accessed=1 << 20, transcendentals=0) if flops else None
    args = [
        pltpu.with_memory_space_constraint(arg, pltpu.HBM) if at in hbm or at in smem else arg
        for at, arg in enumerate(args)
    ]
    shapes = [pltpu.VMEM(shape, kind) for shape, kind in scratch]
    if copies:
        shapes.append(pltpu.SemaphoreType.DMA((copies,)))
    return pl.pallas_call(
        kernel,
        out_shape=tuple(
            jax.ShapeDtypeStruct(shape, kind) if at in final else pltpu.VMEM(shape, kind)
            for at, (shape, kind) in enumerate(outs)
        ),
        in_specs=[pl.BlockSpec(memory_space=space(at)) for at in range(len(args))],
        out_specs=tuple(pl.BlockSpec(memory_space=pltpu.VMEM) for _ in outs),
        scratch_shapes=shapes,
        cost_estimate=cost,
        compiler_params=pltpu.CompilerParams(vmem_limit_bytes=VMEM_LIMIT),
    )(*args)


def permute(array, axis, target):
    length = lax.axis_size(axis)
    return lax.ppermute(array, axis, [(i, target(i) % length) for i in range(length)])


def permute_both(array, by):
    lons, lats = lax.axis_size("lon"), lax.axis_size("lat")
    pairs = [
        (lon * lats + lat, (lon + by) % lons * lats + (lat + by) % lats)
        for lon in range(lons)
        for lat in range(lats)
    ]
    return lax.ppermute(array, ("lon", "lat"), pairs)


def to_core(array):
    return permute(array, "lat", lambda i: i ^ 1)


def to_y(array, by):
    return permute(array, "lat", lambda i: i ^ (4 * by))


def to_x(array, by):
    if by == 1:
        return permute(array, "lat", lambda i: i ^ 2)
    lons, lats = lax.axis_size("lon"), lax.axis_size("lat")
    pairs = [
        (lon * lats + lat, (lon ^ 8) * lats + (lat ^ 2)) for lon in range(lons) for lat in range(lats)
    ]
    return lax.ppermute(array, ("lon", "lat"), pairs)


def to_z(array, step):
    return permute(array, "lon", lambda i: i & 8 | z_partner(i & 7, step))


def quarters(kernel, keep, got):
    return call(kernel, [((2, 64, SIDE), BF16)] * 4, [], (keep, got))


def second_sum(parts):
    return call(kernel_second_sum, [((64, SIDE), BF16)] * 4, [], parts)


def halve(keep, got):
    shape = (keep.shape[0] // 2,) + keep.shape[1:]
    return call(kernel_halve, [(shape, BF16)] * 2, [], (keep, got))


def body(
    fields, cotangent, land_ids, gain_a, table_a, qkv_weight_a, out_weight_a,
    gain_b, table_b, qkv_weight_b, out_weight_b,
):
    place = jnp.asarray(PLACE, BF16)
    place_t = jnp.asarray(PLACE.T, BF16)
    sort = jnp.asarray(SORT, BF16)
    sort_t = jnp.asarray(SORT.T, BF16)
    where = jnp.asarray(WHERE)
    fields = fields.transpose(1, 2, 0, 3)
    cotangent = cotangent.transpose(1, 2, 0, 3)
    table_a = table_a.transpose(1, 2, 0)
    table_b = table_b.transpose(1, 2, 0)
    grid = (fields.shape, BF16)
    piece = ((PIECE, WIDTH), BF16)
    token = ((TOKENS, WIDTH), BF16)
    token_wide = ((TOKENS, WIDTH), F32)
    packed = ((TOKENS, 3 * WIDTH), BF16)
    probs = ((WINDOWS * HEADS, LENGTH, LENGTH), BF16)
    scores = ((WINDOWS * HEADS, LENGTH, LENGTH), F32)
    mixed_t = ((WINDOWS, WIDTH, LENGTH), BF16)
    half_grads = ((WIDTH // 2, 4 * WIDTH), BF16)
    normed_t = ((WIDTH, TOKENS), BF16)
    square = ((TOKENS, TOKENS), BF16)
    spare = ((16, HEADS * GROUP), BF16)
    query = ((LENGTH, GROUP), BF16)
    keys = ((LENGTH, HEADS * GROUP), BF16)
    ids = (land_ids.shape, jnp.int32)
    place_of = (where.shape, jnp.int32)
    vector = ((WIDTH,), F32)
    qkv_shape = ((WIDTH, 3 * WIDTH), BF16)
    out_shape = ((WIDTH, WIDTH), BF16)

    p0, p1, p2, p3, inputs_a, middle_a, normed_a, packed_a, probs_a, mixed_a = call(
        kernel_forward_a,
        [piece] * 4 + [token] * 3 + [packed, probs, mixed_t],
        [grid, ids, vector, qkv_shape, out_shape, square, square, place_of, token_wide, spare, keys, scores],
        (fields, land_ids, gain_a, table_a, qkv_weight_a, out_weight_a, place, sort, where),
        smem=(3,), hbm=(0, 1, 2, 4, 5, 6, 7, 8), copies=8, flops=7 * 10**9,
    )
    diagonal = permute_both(p0, -1)
    below = permute(p1, "lat", lambda i: i - 1)
    eastern = permute(p2, "lon", lambda i: i - 1)
    c0, c1, c2, c3, upstream_a, normed_a_t, query_b, keys_b = call(
        kernel_cotangent,
        [piece] * 4 + [token, normed_t, query, keys],
        [grid, token_wide, spare],
        (cotangent, place, sort, normed_a, land_ids, table_b, where),
        smem=(5,), hbm=(0,), copies=1, flops=2 * 10**9,
    )
    c_diagonal = permute_both(c0, -1)
    c_below = permute(c1, "lat", lambda i: i - 1)
    c_eastern = permute(c2, "lon", lambda i: i - 1)
    b0, b1, b2, b3, inputs_b, normed_b, packed_b, probs_b, mixed_b = call(
        kernel_forward_b,
        [piece] * 4 + [token] * 2 + [packed, probs, mixed_t],
        [scores],
        (p3, eastern, below, diagonal, query_b, keys_b, gain_b, qkv_weight_b, out_weight_b, sort, sort_t),
        flops=5 * 10**9,
    )
    d0, d1, d2, d3, upstream_b, d_packed_b = call(
        kernel_backward_b,
        [piece] * 4 + [token, packed],
        [scores, probs],
        (
            c3, c_eastern, c_below, c_diagonal, inputs_b, gain_b, qkv_weight_b, out_weight_b,
            packed_b, probs_b, mixed_b, sort, sort_t,
        ),
        flops=5 * 10**9,
    )
    d_diagonal = permute_both(d3, 1)
    d_above = permute(d2, "lat", lambda i: i + 1)
    d_western = permute(d1, "lon", lambda i: i + 1)
    send_b, keep_b = call(
        kernel_grads_b, [half_grads] * 2, [normed_t], (normed_b, mixed_b, upstream_b, d_packed_b),
        flops=2 * 10**9,
    )
    send_one_b, send_two_b, keep_one_b, keep_two_b = quarters(
        kernel_first_sum_b, keep_b, to_core(send_b)
    )
    send_one_b, send_two_b, d0 = lax.optimization_barrier((send_one_b, send_two_b, d0))
    parts_b = (keep_one_b, to_x(send_one_b, 1), keep_two_b, to_x(send_two_b, 3))
    grad_middle, d_packed_a, send_a = call(
        kernel_backward_a,
        [token, packed, half_grads],
        [scores, probs],
        (
            d_diagonal, d_above, d_western, d0, upstream_a, out_weight_a, packed_a, probs_a,
            mixed_a, normed_a_t, sort_t,
        ),
        flops=5 * 10**9,
    )
    parts_b, send_a = lax.optimization_barrier((parts_b, send_a))
    send_one_b, send_two_b, held_one_b, held_two_b = second_sum(parts_b)
    parts_b = (held_one_b, to_x(send_one_b, 3), held_two_b, to_x(send_two_b, 1))
    keep_a = call(
        kernel_keep_a, [half_grads], [], (normed_a_t, mixed_a, grad_middle, d_packed_a),
        flops=10**9,
    )[0]
    send_one_a, send_two_a, keep_one_a, keep_two_a = quarters(
        kernel_first_sum_a, keep_a, to_core(send_a)
    )
    send_one_a, send_two_a, d_packed_a = lax.optimization_barrier((send_one_a, send_two_a, d_packed_a))
    parts_a = (keep_one_a, to_y(send_one_a, 1), keep_two_a, to_y(send_two_a, 3))
    grad_fields = call(
        kernel_finish_a,
        [grid],
        [qkv_shape],
        (inputs_a, grad_middle, gain_a, qkv_weight_a, d_packed_a, place_t),
        hbm=(3,), copies=1, flops=4 * 10**9, final=(0,),
    )[0]
    pair = ((2, 32, SIDE), BF16)
    send_b, keep_b = call(kernel_third_sum_b, [pair] * 2, [], parts_b)
    got_b = to_y(send_b, 1)
    send_one_a, send_two_a, held_one_a, held_two_a = second_sum(parts_a)
    send_one_a, send_two_a, grad_fields, b1, b2, b3 = lax.optimization_barrier(
        (send_one_a, send_two_a, grad_fields, b1, b2, b3)
    )
    parts_a = (held_one_a, to_y(send_one_a, 3), held_two_a, to_y(send_two_a, 1))
    delta_diagonal = permute_both(b3, 1)
    delta_above = permute(b2, "lat", lambda i: i + 1)
    delta_western = permute(b1, "lon", lambda i: i + 1)
    send_a, keep_a = call(kernel_third_sum_a, [pair] * 2, [], parts_a)
    got_a = to_x(send_a, 1)
    send_b, keep_b = halve(keep_b, got_b)
    got_b = to_y(send_b, 3)
    send_a, keep_a = halve(keep_a, got_a)
    got_a = to_x(send_a, 3)
    four = ((4, 2, 32, GROUP), BF16)
    got_b, delta_diagonal, delta_above, delta_western = lax.optimization_barrier(
        (got_b, delta_diagonal, delta_above, delta_western)
    )
    send, keep = call(
        kernel_columns, [four] * 2, [((8, 2, 32, GROUP), BF16)], (keep_a, got_a, keep_b, got_b)
    )
    advanced = call(
        kernel_advanced,
        [grid],
        [],
        (delta_diagonal, delta_above, delta_western, b0, middle_a, place_t, sort_t),
        flops=10**9, final=(0,),
    )[0]
    send, keep = halve(keep, to_z(send, 0))
    send, keep = halve(keep, to_z(send, 1))
    grads = call(
        kernel_total,
        [((32, 96), F32), ((32, 32), F32)] * 2,
        [],
        (keep, to_z(send, 2)),
        final=(0, 1, 2, 3),
    )
    return (advanced.transpose(2, 0, 1, 3), grad_fields.transpose(2, 0, 1, 3), *grads)


def solution(mesh):
    grid = P(None, "lat", "lon", None)
    return jax.shard_map(
        body,
        mesh=mesh,
        in_specs=(grid, grid) + (P(),) * 9,
        out_specs=(grid, grid) + (P("lat", "lon"),) * 4,
        check_vma=False,
    )
```

```python
import jax
import jax.numpy as jnp
import numpy as np
from jax import lax
from jax.experimental import pallas as pl
from jax.experimental.pallas import tpu as pltpu
from jax.sharding import PartitionSpec as P

WINDOWS = 2
LENGTH = 144
QUARTER = 36
TOKENS = WINDOWS * LENGTH
PIECE = WINDOWS * QUARTER
WIDTH = 512
HEADS = 16
HEAD = 32
GROUP = 128
GROUPS = WIDTH // GROUP
PER_GROUP = GROUP // HEAD
ROOT = HEAD**0.5
SIDE = 2 * WIDTH
EPS = 1e-05
NEG = -1000000000.0
VMEM_LIMIT = 24 * 1024 * 1024
F32 = jnp.float32
BF16 = jnp.bfloat16


def _tables():
    place = np.zeros((TOKENS, TOKENS), np.float32)
    sort = np.zeros((TOKENS, TOKENS), np.float32)
    where = np.zeros((LENGTH, 8), np.int32)
    for window in range(WINDOWS):
        for quadrant in range(4):
            for level in range(2):
                for row in range(6):
                    for column in range(3):
                        inner = level * 18 + row * 3 + column
                        at = quadrant * QUARTER + inner
                        token = window * LENGTH + at
                        lat = quadrant // 2 * 6 + row
                        lon = quadrant % 2 * 3 + column
                        source = (lat * 6 + lon) * 4 + 2 * window + level
                        place[token, source] = 1
                        sort[quadrant * PIECE + window * QUARTER + inner, token] = 1
                        where[at, 0] = lat
                        where[at, 1] = lon
    return place, sort, where


PLACE, SORT, WHERE = _tables()


def mm(left, right):
    return jnp.dot(left, right, preferred_element_type=F32)


def mm_t(left, right):
    return lax.dot_general(left, right, (((1,), (1,)), ((), ())), preferred_element_type=F32)


def normalise(inputs):
    centre = inputs - jnp.mean(inputs, axis=-1, keepdims=True)
    spread = jnp.mean(centre * centre, axis=-1, keepdims=True)
    scale = lax.rsqrt(spread + EPS)
    return centre * scale, scale


def lanes(shape):
    return lax.broadcasted_iota(jnp.int32, shape, 1)


def head_masks():
    lane = lanes((1, GROUP))
    return [
        ((lane >= h * HEAD) & (lane < (h + 1) * HEAD)).astype(F32).astype(BF16)
        for h in range(PER_GROUP)
    ]


def bias_features(ids_ref, where_ref, table_ref, spare_ref, shift, last):
    lat_at = lax.axis_index("lat")
    lon_at = lax.axis_index("lon")
    rows, columns = ids_ref.shape
    row = where_ref[:, 0:1]
    column = where_ref[:, 1:2] + (lon_at * 6 + shift // 2)
    at = row + (lat_at * 12 + shift)
    at = jnp.where(at >= rows, at - rows, at)
    column = jnp.where(column >= columns, column - columns, column)
    pick = (lanes((LENGTH, rows)) == at).astype(F32).astype(BF16)
    found = mm(pick, ids_ref[...].astype(F32).astype(BF16))
    found = jnp.where(lanes((LENGTH, columns)) == column, found, 0.0)
    kind = jnp.sum(found, axis=1, keepdims=True).astype(jnp.int32)
    lane = lanes((LENGTH, GROUP))
    third = (lane >= 3).astype(jnp.int32) + (lane >= 6).astype(jnp.int32)
    query = ((lane < 9) & (third == kind)).astype(F32)
    key = ((lane < 3) & (lane == kind)).astype(F32)
    if last:
        flag = ((row >= 6) & (lat_at == lax.axis_size("lat") - 1)).astype(F32)
        query = jnp.where(lane == 9, flag, jnp.where(lane == 10, 1.0 - flag, query))
        key = jnp.where(lane == 3, 1.0 - flag, jnp.where(lane == 4, flag, key))
    small = (16, GROUP)
    lane = lanes(small)
    sub = lax.broadcasted_iota(jnp.int32, small, 0)
    third = (lane >= 3).astype(jnp.int32) + (lane >= 6).astype(jnp.int32)
    part = lane - 3 * third
    spots = {
        (first, second): (lane < 9) & (third == first) & (sub == second)
        for first in range(3)
        for second in range(3)
    }
    fixed = jnp.where(((sub == 3) & (lane == 9)) | ((sub == 4) & (lane == 10)), NEG * ROOT, 0.0)
    for head in range(HEADS):
        entry = fixed
        for (first, second), spot in spots.items():
            entry = jnp.where(spot, table_ref[first, second, head] * ROOT, entry)
        high = entry.astype(BF16).astype(F32)
        middle = (entry - high).astype(BF16).astype(F32)
        low = entry - high - middle
        entry = jnp.where(part == 0, high, jnp.where(part == 1, middle, low))
        entry = jnp.where(lane >= 9, high, entry)
        spare_ref[:, head * GROUP : (head + 1) * GROUP] = entry.astype(BF16)
    features = mm(key.astype(BF16)[:, :16], spare_ref[...])
    return query.astype(BF16), features.astype(BF16)


def forward_core(
    inputs, gain, qkv_ref, out_ref, query_features, key_ref, packed_ref, probs_ref, mixed_t_ref, scores_ref
):
    hat, _ = normalise(inputs)
    normed = (hat * gain).astype(BF16)
    packed_ref[...] = mm(normed, qkv_ref[...]).astype(BF16)
    masks = head_masks()
    factor = F32(1.0 / ROOT * np.log2(np.e))
    for window, group, rows, at in sections():
        query = packed_ref[rows, at : at + GROUP]
        keys = packed_ref[rows, WIDTH + at : WIDTH + at + GROUP]
        for h in range(PER_GROUP):
            head = group * PER_GROUP + h
            left = jnp.concatenate([keys, key_ref[:, head * GROUP : (head + 1) * GROUP]], axis=1)
            right = jnp.concatenate([query * masks[h], query_features], axis=1)
            scores_ref[window * HEADS + head] = mm_t(left, right)
    for item in range(WINDOWS * HEADS):
        scores = scores_ref[item]
        top = jnp.max(scores, axis=0, keepdims=True)
        raised = jnp.exp2((scores - top) * factor)
        total = jnp.sum(raised, axis=0, keepdims=True)
        probs_ref[item] = (raised * (1.0 / total)).astype(BF16)
    for window, group, rows, at in sections():
        values_t = packed_ref[rows, 2 * WIDTH + at : 2 * WIDTH + at + GROUP].T
        for h in range(PER_GROUP):
            head = group * PER_GROUP + h
            mixed = mm(values_t[h * HEAD : (h + 1) * HEAD], probs_ref[window * HEADS + head])
            mixed_t_ref[window, head * HEAD : (head + 1) * HEAD, :] = mixed.astype(BF16)
    parts = [mm(mixed_t_ref[window].T, out_ref[...]) for window in range(WINDOWS)]
    return normed, jnp.concatenate(parts, axis=0)


def sections():
    for window in range(WINDOWS):
        for group in range(GROUPS):
            rows = slice(window * LENGTH, (window + 1) * LENGTH)
            yield window, group, rows, group * GROUP


def backward_core(
    upstream, out_ref, packed_ref, probs_ref, mixed_t_ref, d_packed_ref, d_probs_ref, d_scores_ref
):
    masks = head_masks()
    d_mixed = mm_t(upstream, out_ref[...]).astype(BF16)
    for window, group, rows, at in sections():
        values = packed_ref[rows, 2 * WIDTH + at : 2 * WIDTH + at + GROUP]
        up = d_mixed[rows, at : at + GROUP]
        for h in range(PER_GROUP):
            d_probs_ref[window * HEADS + group * PER_GROUP + h] = mm_t(values, up * masks[h])
    for window in range(WINDOWS):
        here = upstream[window * LENGTH : (window + 1) * LENGTH]
        d_mixed_t = mm_t(out_ref[...], here).astype(BF16)
        dots = d_mixed_t.astype(F32) * mixed_t_ref[window].astype(F32)
        for head in range(HEADS):
            item = window * HEADS + head
            inner = jnp.sum(dots[head * HEAD : (head + 1) * HEAD], axis=0, keepdims=True)
            d_scores = (d_probs_ref[item] - inner) * F32(1.0 / ROOT)
            d_scores_ref[item] = (probs_ref[item].astype(F32) * d_scores).astype(BF16)
    for window, group, rows, at in sections():
        query = packed_ref[rows, at : at + GROUP]
        keys_t = packed_ref[rows, WIDTH + at : WIDTH + at + GROUP].T
        up = d_mixed[rows, at : at + GROUP]
        d_values = None
        d_keys = None
        d_query = []
        for h in range(PER_GROUP):
            item = window * HEADS + group * PER_GROUP + h
            d_value = mm(probs_ref[item], up * masks[h])
            d_key = mm(d_scores_ref[item], query * masks[h])
            d_values = d_value if d_values is None else d_values + d_value
            d_keys = d_key if d_keys is None else d_keys + d_key
            d_query.append(mm(keys_t[h * HEAD : (h + 1) * HEAD], d_scores_ref[item]))
        d_query = jnp.concatenate(d_query, axis=0).T
        d_packed_ref[rows, at : at + GROUP] = d_query.astype(BF16)
        d_packed_ref[rows, WIDTH + at : WIDTH + at + GROUP] = d_keys.astype(BF16)
        d_packed_ref[rows, 2 * WIDTH + at : 2 * WIDTH + at + GROUP] = d_values.astype(BF16)


def norm_backward(inputs, gain, d_packed, qkv_ref):
    d_normed = mm_t(d_packed, qkv_ref[...]).astype(BF16).astype(F32)
    hat, scale = normalise(inputs)
    d_hat = d_normed * gain
    mean = jnp.mean(d_hat, axis=-1, keepdims=True)
    along = jnp.mean(d_hat * hat, axis=-1, keepdims=True)
    return scale * (d_hat - mean - hat * along)


def grads_half(half, normed_t_ref, mixed_t_ref, upstream, d_packed_ref, result_ref):
    def blocks(ref, *first):
        return [
            ref[(*first, pl.ds(pl.multiple_of((2 * block + half) * 32, 32), 32), slice(None))]
            for block in range(8)
        ]

    left = jnp.concatenate(blocks(normed_t_ref), axis=0)
    qkv = mm(left, d_packed_ref[...]).astype(BF16)
    total = None
    for window in range(WINDOWS):
        left = jnp.concatenate(blocks(mixed_t_ref, window), axis=0)
        part = mm(left, upstream[window * LENGTH : (window + 1) * LENGTH])
        total = part if total is None else total + part
    total = total.astype(BF16)
    result_ref[:, :768] = qkv[:, :768]
    result_ref[:, 768:SIDE] = total[:, :256]
    result_ref[:, SIDE : SIDE + 768] = qkv[:, 768:]
    result_ref[:, SIDE + 768 :] = total[:, 256:]


def load_grid(ref, place, spare_ref):
    for row in range(12):
        for column in range(6):
            at = (row * 6 + column) * 4
            spare_ref[at : at + 4, :] = ref[row, column].astype(F32)
    return mm(place, spare_ref[...].astype(BF16))


def store_grid(ref, place_t, tokens):
    spread = mm(place_t, tokens)
    for row in range(12):
        for column in range(6):
            at = (row * 6 + column) * 4
            ref[row, column] = spread[at : at + 4].astype(BF16)


def split_pieces(sort, tokens, refs):
    tokens = mm(sort, tokens)
    for at, ref in enumerate(refs):
        ref[...] = tokens[at * PIECE : (at + 1) * PIECE].astype(BF16)


def join_pieces(sort_t, pieces):
    tokens = jnp.concatenate([piece.astype(F32) for piece in pieces], axis=0)
    return mm(sort_t, tokens.astype(BF16))


def fetch(pairs, sems):
    copies = [
        pltpu.make_async_copy(source, target, sems.at[at])
        for at, (source, target) in enumerate(pairs)
    ]
    for copy in copies:
        copy.start()
    return copies


def kernel_forward_a(
    fields_hbm, ids_hbm, gain_hbm, table, qkv_hbm, out_hbm, place_hbm, sort_hbm, where_hbm,
    piece0, piece1, piece2, piece3, inputs_out, middle_out, normed_out, packed, probs, mixed_t,
    fields, ids, gain, qkv, out, place, sort, where, grid, spare, key_features, scores, sems,
):
    ids_in, where_in, fields_in, place_in, gain_in, qkv_in, out_in, sort_in = fetch(
        (
            (ids_hbm, ids), (where_hbm, where), (fields_hbm, fields), (place_hbm, place),
            (gain_hbm, gain), (qkv_hbm, qkv), (out_hbm, out), (sort_hbm, sort),
        ),
        sems,
    )
    ids_in.wait()
    where_in.wait()
    query_features, features = bias_features(ids, where, table, spare, 0, False)
    key_features[...] = features
    fields_in.wait()
    place_in.wait()
    inputs = load_grid(fields, place[...], grid)
    inputs_out[...] = inputs.astype(BF16)
    gain_in.wait()
    qkv_in.wait()
    out_in.wait()
    normed, delta = forward_core(
        inputs, gain[...].reshape(1, WIDTH), qkv, out, query_features, key_features,
        packed, probs, mixed_t, scores,
    )
    normed_out[...] = normed
    middle = (inputs + delta).astype(BF16)
    middle_out[...] = middle
    sort_in.wait()
    split_pieces(sort[...], middle, (piece0, piece1, piece2, piece3))


def kernel_cotangent(
    cotangent_hbm, place, sort, normed, ids, table, where,
    piece0, piece1, piece2, piece3, upstream_out, normed_t, query_out, key_out,
    cotangent, grid, spare, sems,
):
    (cotangent_in,) = fetch(((cotangent_hbm, cotangent),), sems)
    normed_t[...] = normed[...].T
    query, keys = bias_features(ids, where, table, spare, 6, True)
    query_out[...] = query
    key_out[...] = keys
    cotangent_in.wait()
    upstream = load_grid(cotangent, place[...], grid).astype(BF16)
    upstream_out[...] = upstream
    split_pieces(sort[...], upstream, (piece0, piece1, piece2, piece3))


def kernel_forward_b(
    piece0, piece1, piece2, piece3, query_features, key_features, gain, qkv, out, sort, sort_t,
    back0, back1, back2, back3, inputs_out, normed_out, packed, probs, mixed_t,
    scores,
):
    inputs = join_pieces(sort_t[...], [ref[...] for ref in (piece0, piece1, piece2, piece3)])
    inputs_out[...] = inputs.astype(BF16)
    normed, delta = forward_core(
        inputs, gain[...].reshape(1, WIDTH), qkv, out, query_features[...], key_features,
        packed, probs, mixed_t, scores,
    )
    normed_out[...] = normed
    split_pieces(sort[...], delta.astype(BF16), (back0, back1, back2, back3))


def kernel_backward_b(
    piece0, piece1, piece2, piece3, delta0, delta1, delta2, delta3,
    inputs, gain, qkv, out, packed, probs, mixed_t, sort, sort_t,
    back0, back1, back2, back3, upstream_out, d_packed,
    d_probs, d_scores,
):
    pieces = [ref[...] for ref in (piece0, piece1, piece2, piece3)]
    upstream = join_pieces(sort_t[...], pieces).astype(BF16)
    upstream_out[...] = upstream
    backward_core(upstream, out, packed, probs, mixed_t, d_packed, d_probs, d_scores)
    d_inputs = norm_backward(
        inputs[...].astype(F32), gain[...].reshape(1, WIDTH), d_packed[...], qkv
    )
    backs = (back0, back1, back2, back3)
    split_pieces(sort[...], d_inputs.astype(BF16), [back.at[0] for back in backs])
    for back, delta in zip(backs, (delta0, delta1, delta2, delta3), strict=True):
        back[1] = delta[...]


def kernel_grads_b(normed, mixed_t, upstream, d_packed, send, keep, normed_t):
    normed_t[...] = normed[...].T
    core = lax.axis_index("lat") % 2
    grads_half(1 - core, normed_t, mixed_t, upstream[...], d_packed, send)
    grads_half(core, normed_t, mixed_t, upstream[...], d_packed, keep)


def kernel_backward_a(
    back0, back1, back2, back3, upstream, out, packed, probs, mixed_t, normed_t, sort_t,
    grad_middle_out, d_packed, send,
    d_probs, d_scores,
):
    d_inputs = join_pieces(sort_t[...], [back[0] for back in (back0, back1, back2, back3)])
    grad_middle = (upstream[...].astype(F32) + d_inputs).astype(BF16)
    grad_middle_out[...] = grad_middle
    backward_core(grad_middle, out, packed, probs, mixed_t, d_packed, d_probs, d_scores)
    core = lax.axis_index("lat") % 2
    grads_half(1 - core, normed_t, mixed_t, grad_middle, d_packed, send)


def kernel_keep_a(
    back0, back1, back2, back3, middle, normed_t, mixed_t, grad_middle, d_packed, place_t, sort_t,
    keep, advanced,
):
    core = lax.axis_index("lat") % 2
    grads_half(core, normed_t, mixed_t, grad_middle[...], d_packed, keep)
    delta = join_pieces(sort_t[...], [back[1] for back in (back0, back1, back2, back3)])
    store_grid(advanced, place_t[...], (middle[...].astype(F32) + delta).astype(BF16))


def kernel_finish_a(
    inputs, grad_middle, gain, qkv_hbm, d_packed, place_t, grad_fields, qkv, sems
):
    (qkv_in,) = fetch(((qkv_hbm, qkv),), sems)
    qkv_in.wait()
    d_inputs = norm_backward(
        inputs[...].astype(F32), gain[...].reshape(1, WIDTH), d_packed[...], qkv
    )
    total = (grad_middle[...].astype(F32) + d_inputs).astype(BF16)
    store_grid(grad_fields, place_t[...], total)


def rows_of(block, count):
    return pl.ds(pl.multiple_of(block * count, count), count)


def place_x():
    return lax.axis_index("lon") // 8 * 2 + lax.axis_index("lat") // 2 % 2


def place_y():
    return lax.axis_index("lat") // 4


def kernel_first_sum_a(keep, got, send_one, send_two, keep_one, keep_two):
    y = place_y()
    for side, first, send, kept in ((0, 1, send_one, keep_one), (1, 3, send_two, keep_two)):
        columns = slice(side * SIDE, (side + 1) * SIDE)
        for target, place, block in (
            (send, 0, y ^ first), (send, 1, y ^ 2), (kept, 0, y), (kept, 1, y ^ 2 ^ first)
        ):
            rows = rows_of(block, 64)
            target[place] = keep[rows, columns] + got[rows, columns]


def kernel_first_sum_b(keep, got, send_one, send_two, keep_one, keep_two):
    x = place_x()
    for part, first, send, kept in ((0, 1, send_one, keep_one), (1, 3, send_two, keep_two)):
        for target, place, block in (
            (send, 0, x ^ first), (send, 1, x ^ 2), (kept, 0, x), (kept, 1, x ^ 2 ^ first)
        ):
            columns = rows_of(block // 2, SIDE)
            for inner in range(2):
                rows = rows_of((part * 2 + inner) * 2 + block % 2, 32)
                target[place, inner * 32 : (inner + 1) * 32] = keep[rows, columns] + got[rows, columns]


def kernel_second_sum(keep_one, got_one, keep_two, got_two, send_one, send_two, held_one, held_two):
    send_one[...] = keep_one[1] + got_one[1]
    send_two[...] = keep_two[1] + got_two[1]
    held_one[...] = keep_one[0] + got_one[0]
    held_two[...] = keep_two[0] + got_two[0]


def third_sum(at, halves, send, keep):
    for target, place, block in ((send, 0, at ^ 1), (send, 1, at ^ 2), (keep, 0, at), (keep, 1, at ^ 3)):
        rows = rows_of(block % 2, 32)
        for half, (held, got) in enumerate(halves):

            @pl.when(block // 2 == half)
            def _(target=target, place=place, rows=rows, held=held, got=got):
                target[place] = held[rows, :] + got[rows, :]


def kernel_third_sum_a(held_one, got_one, held_two, got_two, send, keep):
    third_sum(place_x(), ((held_one, got_one), (held_two, got_two)), send, keep)


def kernel_third_sum_b(held_one, got_one, held_two, got_two, send, keep):
    third_sum(place_y(), ((held_one, got_one), (held_two, got_two)), send, keep)


def kernel_halve(keep, got, send, held):
    half = keep.shape[0] // 2
    held[...] = keep[:half] + got[:half]
    send[...] = keep[half:] + got[half:]


def kernel_columns(keep_a, got_a, keep_b, got_b, blocks):
    for rows, held, got in ((slice(0, 32), keep_a, got_a), (slice(32, 64), keep_b, got_b)):
        total = held[0].astype(F32) + got[0].astype(F32)
        for block in range(8):
            qkv = total[:, block * 96 : (block + 1) * 96]
            out = total[:, 768 + block * 32 : 768 + (block + 1) * 32]
            blocks[block, rows] = jnp.concatenate([qkv, out], axis=1).astype(BF16)


def kernel_total(parts, qkv_a, out_a, qkv_b, out_b):
    total = parts[0].astype(F32)
    for at in range(1, 8):
        total = total + parts[at].astype(F32)
    for rows, qkv, out in ((slice(0, 32), qkv_a, out_a), (slice(32, 64), qkv_b, out_b)):
        qkv[...] = total[rows, :96]
        out[...] = total[rows, 96:]


def call(kernel, outs, scratch, args, smem=(), hbm=(), copies=0, flops=0, final=()):
    def space(at):
        return pltpu.SMEM if at in smem else pltpu.HBM if at in hbm else pltpu.VMEM

    cost = pl.CostEstimate(flops=flops, bytes_accessed=1 << 20, transcendentals=0) if flops else None
    args = [
        pltpu.with_memory_space_constraint(arg, pltpu.HBM) if at in hbm or at in smem else arg
        for at, arg in enumerate(args)
    ]
    shapes = [pltpu.VMEM(shape, kind) for shape, kind in scratch]
    if copies:
        shapes.append(pltpu.SemaphoreType.DMA((copies,)))
    return pl.pallas_call(
        kernel,
        out_shape=tuple(
            jax.ShapeDtypeStruct(shape, kind) if at in final else pltpu.VMEM(shape, kind)
            for at, (shape, kind) in enumerate(outs)
        ),
        in_specs=[pl.BlockSpec(memory_space=space(at)) for at in range(len(args))],
        out_specs=tuple(pl.BlockSpec(memory_space=pltpu.VMEM) for _ in outs),
        scratch_shapes=shapes,
        cost_estimate=cost,
        compiler_params=pltpu.CompilerParams(vmem_limit_bytes=VMEM_LIMIT),
    )(*args)


def permute(array, axis, target):
    length = lax.axis_size(axis)
    return lax.ppermute(array, axis, [(i, target(i) % length) for i in range(length)])


def permute_both(array, by):
    lons, lats = lax.axis_size("lon"), lax.axis_size("lat")
    pairs = [
        (lon * lats + lat, (lon + by) % lons * lats + (lat + by) % lats)
        for lon in range(lons)
        for lat in range(lats)
    ]
    return lax.ppermute(array, ("lon", "lat"), pairs)


def to_core(array):
    return permute(array, "lat", lambda i: i ^ 1)


def to_y(array, by):
    return permute(array, "lat", lambda i: i ^ (4 * by))


def to_x(array, by):
    if by == 1:
        return permute(array, "lat", lambda i: i ^ 2)
    lons, lats = lax.axis_size("lon"), lax.axis_size("lat")
    pairs = [
        (lon * lats + lat, (lon ^ 8) * lats + (lat ^ 2)) for lon in range(lons) for lat in range(lats)
    ]
    return lax.ppermute(array, ("lon", "lat"), pairs)


def quarters(kernel, keep, got):
    return call(kernel, [((2, 64, SIDE), BF16)] * 4, [], (keep, got))


def second_sum(parts):
    return call(kernel_second_sum, [((64, SIDE), BF16)] * 4, [], parts)


def halve(keep, got):
    shape = (keep.shape[0] // 2,) + keep.shape[1:]
    return call(kernel_halve, [(shape, BF16)] * 2, [], (keep, got))


def exchange_z(messages):
    groups = [[x_hi * 8 + z for z in range(8)] for x_hi in range(2)]
    return lax.all_to_all(messages, "lon", 0, 0, axis_index_groups=groups, tiled=True)


def body(
    fields, cotangent, land_ids, gain_a, table_a, qkv_weight_a, out_weight_a,
    gain_b, table_b, qkv_weight_b, out_weight_b,
):
    place = jnp.asarray(PLACE, BF16)
    place_t = jnp.asarray(PLACE.T, BF16)
    sort = jnp.asarray(SORT, BF16)
    sort_t = jnp.asarray(SORT.T, BF16)
    where = jnp.asarray(WHERE)
    fields = fields.transpose(1, 2, 0, 3)
    cotangent = cotangent.transpose(1, 2, 0, 3)
    table_a = table_a.transpose(1, 2, 0)
    table_b = table_b.transpose(1, 2, 0)
    grid = (fields.shape, BF16)
    piece = ((PIECE, WIDTH), BF16)
    token = ((TOKENS, WIDTH), BF16)
    token_wide = ((TOKENS, WIDTH), F32)
    packed = ((TOKENS, 3 * WIDTH), BF16)
    probs = ((WINDOWS * HEADS, LENGTH, LENGTH), BF16)
    scores = ((WINDOWS * HEADS, LENGTH, LENGTH), F32)
    mixed_t = ((WINDOWS, WIDTH, LENGTH), BF16)
    half_grads = ((WIDTH // 2, 4 * WIDTH), BF16)
    normed_t = ((WIDTH, TOKENS), BF16)
    square = ((TOKENS, TOKENS), BF16)
    spare = ((16, HEADS * GROUP), BF16)
    query = ((LENGTH, GROUP), BF16)
    keys = ((LENGTH, HEADS * GROUP), BF16)
    ids = (land_ids.shape, jnp.int32)
    place_of = (where.shape, jnp.int32)
    vector = ((WIDTH,), F32)
    qkv_shape = ((WIDTH, 3 * WIDTH), BF16)
    out_shape = ((WIDTH, WIDTH), BF16)

    p0, p1, p2, p3, inputs_a, middle_a, normed_a, packed_a, probs_a, mixed_a = call(
        kernel_forward_a,
        [piece] * 4 + [token] * 3 + [packed, probs, mixed_t],
        [grid, ids, vector, qkv_shape, out_shape, square, square, place_of, token_wide, spare, keys, scores],
        (fields, land_ids, gain_a, table_a, qkv_weight_a, out_weight_a, place, sort, where),
        smem=(3,), hbm=(0, 1, 2, 4, 5, 6, 7, 8), copies=8, flops=7 * 10**9,
    )
    diagonal = permute_both(p0, -1)
    below = permute(p1, "lat", lambda i: i - 1)
    eastern = permute(p2, "lon", lambda i: i - 1)
    c0, c1, c2, c3, upstream_a, normed_a_t, query_b, keys_b = call(
        kernel_cotangent,
        [piece] * 4 + [token, normed_t, query, keys],
        [grid, token_wide, spare],
        (cotangent, place, sort, normed_a, land_ids, table_b, where),
        smem=(5,), hbm=(0,), copies=1, flops=2 * 10**9,
    )
    c_diagonal = permute_both(c0, -1)
    c_below = permute(c1, "lat", lambda i: i - 1)
    c_eastern = permute(c2, "lon", lambda i: i - 1)
    b0, b1, b2, b3, inputs_b, normed_b, packed_b, probs_b, mixed_b = call(
        kernel_forward_b,
        [piece] * 4 + [token] * 2 + [packed, probs, mixed_t],
        [scores],
        (p3, eastern, below, diagonal, query_b, keys_b, gain_b, qkv_weight_b, out_weight_b, sort, sort_t),
        flops=5 * 10**9,
    )
    twin = ((2, PIECE, WIDTH), BF16)
    d0, d1, d2, d3, upstream_b, d_packed_b = call(
        kernel_backward_b,
        [twin] * 4 + [token, packed],
        [scores, probs],
        (
            c3, c_eastern, c_below, c_diagonal, b0, b1, b2, b3, inputs_b, gain_b, qkv_weight_b,
            out_weight_b, packed_b, probs_b, mixed_b, sort, sort_t,
        ),
        flops=5 * 10**9,
    )
    d3 = permute_both(d3, 1)
    d2 = permute(d2, "lat", lambda i: i + 1)
    d1 = permute(d1, "lon", lambda i: i + 1)
    send_b, keep_b = call(
        kernel_grads_b, [half_grads] * 2, [normed_t], (normed_b, mixed_b, upstream_b, d_packed_b),
        flops=2 * 10**9,
    )
    send_one_b, send_two_b, keep_one_b, keep_two_b = quarters(
        kernel_first_sum_b, keep_b, to_core(send_b)
    )
    parts_b = (keep_one_b, to_x(send_one_b, 1), keep_two_b, to_x(send_two_b, 3))
    send_one_b, send_two_b, held_one_b, held_two_b = second_sum(parts_b)
    parts_b = (held_one_b, to_x(send_one_b, 3), held_two_b, to_x(send_two_b, 1))
    grad_middle, d_packed_a, send_a = call(
        kernel_backward_a,
        [token, packed, half_grads],
        [scores, probs],
        (
            d3, d2, d1, d0, upstream_a, out_weight_a, packed_a, probs_a, mixed_a, normed_a_t,
            sort_t,
        ),
        flops=5 * 10**9,
    )
    got_a = to_core(send_a)
    keep_a, advanced = call(
        kernel_keep_a,
        [half_grads, grid],
        [],
        (
            d3, d2, d1, d0, middle_a, normed_a_t, mixed_a, grad_middle, d_packed_a, place_t,
            sort_t,
        ),
        flops=2 * 10**9, final=(1,),
    )
    send_one_a, send_two_a, keep_one_a, keep_two_a = quarters(kernel_first_sum_a, keep_a, got_a)
    send_one_a, send_two_a, d_packed_a = lax.optimization_barrier((send_one_a, send_two_a, d_packed_a))
    parts_a = (keep_one_a, to_y(send_one_a, 1), keep_two_a, to_y(send_two_a, 3))
    grad_fields = call(
        kernel_finish_a,
        [grid],
        [qkv_shape],
        (inputs_a, grad_middle, gain_a, qkv_weight_a, d_packed_a, place_t),
        hbm=(3,), copies=1, flops=4 * 10**9, final=(0,),
    )[0]
    pair = ((2, 32, SIDE), BF16)
    send_b, keep_b = call(kernel_third_sum_b, [pair] * 2, [], parts_b)
    got_b = to_y(send_b, 1)
    send_one_a, send_two_a, held_one_a, held_two_a = second_sum(parts_a)
    send_one_a, send_two_a, grad_fields = lax.optimization_barrier(
        (send_one_a, send_two_a, grad_fields)
    )
    parts_a = (held_one_a, to_y(send_one_a, 3), held_two_a, to_y(send_two_a, 1))
    send_a, keep_a = call(kernel_third_sum_a, [pair] * 2, [], parts_a)
    got_a = to_x(send_a, 1)
    send_b, keep_b = halve(keep_b, got_b)
    got_b = to_y(send_b, 3)
    send_a, keep_a = halve(keep_a, got_a)
    got_a = to_x(send_a, 3)
    blocks = call(
        kernel_columns, [((8, 64, GROUP), BF16)], [], (keep_a, got_a, keep_b, got_b)
    )[0]
    parts = exchange_z(blocks)
    grads = call(
        kernel_total,
        [((32, 96), F32), ((32, 32), F32)] * 2,
        [],
        (parts,),
        final=(0, 1, 2, 3),
    )
    return (advanced.transpose(2, 0, 1, 3), grad_fields.transpose(2, 0, 1, 3), *grads)


def solution(mesh):
    grid = P(None, "lat", "lon", None)
    return jax.shard_map(
        body,
        mesh=mesh,
        in_specs=(grid, grid) + (P(),) * 9,
        out_specs=(grid, grid) + (P("lat", "lon"),) * 4,
        check_vma=False,
    )
```

```python
import jax
import jax.numpy as jnp
import numpy as np
from jax import lax
from jax.experimental import pallas as pl
from jax.experimental.pallas import tpu as pltpu
from jax.sharding import PartitionSpec as P

WINDOWS = 2
LENGTH = 144
QUARTER = 36
TOKENS = WINDOWS * LENGTH
PIECE = WINDOWS * QUARTER
WIDTH = 512
HEADS = 16
HEAD = 32
GROUP = 128
GROUPS = WIDTH // GROUP
PER_GROUP = GROUP // HEAD
ROOT = HEAD**0.5
SIDE = 2 * WIDTH
EPS = 1e-05
NEG = -1000000000.0
VMEM_LIMIT = 24 * 1024 * 1024
F32 = jnp.float32
BF16 = jnp.bfloat16


def _tables():
    place = np.zeros((TOKENS, TOKENS), np.float32)
    sort = np.zeros((TOKENS, TOKENS), np.float32)
    where = np.zeros((LENGTH, 8), np.int32)
    for window in range(WINDOWS):
        for quadrant in range(4):
            for level in range(2):
                for row in range(6):
                    for column in range(3):
                        inner = level * 18 + row * 3 + column
                        at = quadrant * QUARTER + inner
                        token = window * LENGTH + at
                        lat = quadrant // 2 * 6 + row
                        lon = quadrant % 2 * 3 + column
                        source = (lat * 6 + lon) * 4 + 2 * window + level
                        place[token, source] = 1
                        sort[quadrant * PIECE + window * QUARTER + inner, token] = 1
                        where[at, 0] = lat
                        where[at, 1] = lon
    return place, sort, where


PLACE, SORT, WHERE = _tables()


def mm(left, right):
    return jnp.dot(left, right, preferred_element_type=F32)


def mm_t(left, right):
    return lax.dot_general(left, right, (((1,), (1,)), ((), ())), preferred_element_type=F32)


def normalise(inputs):
    centre = inputs - jnp.mean(inputs, axis=-1, keepdims=True)
    spread = jnp.mean(centre * centre, axis=-1, keepdims=True)
    scale = lax.rsqrt(spread + EPS)
    return centre * scale, scale


def lanes(shape):
    return lax.broadcasted_iota(jnp.int32, shape, 1)


def head_masks():
    lane = lanes((1, GROUP))
    return [
        ((lane >= h * HEAD) & (lane < (h + 1) * HEAD)).astype(F32).astype(BF16)
        for h in range(PER_GROUP)
    ]


def bias_features(ids_ref, where_ref, table_ref, spare_ref, shift, last):
    lat_at = lax.axis_index("lat")
    lon_at = lax.axis_index("lon")
    rows, columns = ids_ref.shape
    row = where_ref[:, 0:1]
    column = where_ref[:, 1:2] + (lon_at * 6 + shift // 2)
    at = row + (lat_at * 12 + shift)
    at = jnp.where(at >= rows, at - rows, at)
    column = jnp.where(column >= columns, column - columns, column)
    pick = (lanes((LENGTH, rows)) == at).astype(F32).astype(BF16)
    found = mm(pick, ids_ref[...].astype(F32).astype(BF16))
    found = jnp.where(lanes((LENGTH, columns)) == column, found, 0.0)
    kind = jnp.sum(found, axis=1, keepdims=True).astype(jnp.int32)
    lane = lanes((LENGTH, GROUP))
    third = (lane >= 3).astype(jnp.int32) + (lane >= 6).astype(jnp.int32)
    query = ((lane < 9) & (third == kind)).astype(F32)
    key = ((lane < 3) & (lane == kind)).astype(F32)
    if last:
        flag = ((row >= 6) & (lat_at == lax.axis_size("lat") - 1)).astype(F32)
        query = jnp.where(lane == 9, flag, jnp.where(lane == 10, 1.0 - flag, query))
        key = jnp.where(lane == 3, 1.0 - flag, jnp.where(lane == 4, flag, key))
    small = (16, GROUP)
    lane = lanes(small)
    sub = lax.broadcasted_iota(jnp.int32, small, 0)
    third = (lane >= 3).astype(jnp.int32) + (lane >= 6).astype(jnp.int32)
    part = lane - 3 * third
    spots = {
        (first, second): (lane < 9) & (third == first) & (sub == second)
        for first in range(3)
        for second in range(3)
    }
    fixed = jnp.where(((sub == 3) & (lane == 9)) | ((sub == 4) & (lane == 10)), NEG * ROOT, 0.0)
    for head in range(HEADS):
        entry = fixed
        for (first, second), spot in spots.items():
            entry = jnp.where(spot, table_ref[first, second, head] * ROOT, entry)
        high = entry.astype(BF16).astype(F32)
        middle = (entry - high).astype(BF16).astype(F32)
        low = entry - high - middle
        entry = jnp.where(part == 0, high, jnp.where(part == 1, middle, low))
        entry = jnp.where(lane >= 9, high, entry)
        spare_ref[:, head * GROUP : (head + 1) * GROUP] = entry.astype(BF16)
    features = mm(key.astype(BF16)[:, :16], spare_ref[...])
    return query.astype(BF16), features.astype(BF16)


def forward_core(
    inputs, gain, qkv_ref, out_ref, query_features, key_ref, packed_ref, probs_ref, mixed_t_ref, scores_ref
):
    hat, _ = normalise(inputs)
    normed = (hat * gain).astype(BF16)
    packed_ref[...] = mm(normed, qkv_ref[...]).astype(BF16)
    masks = head_masks()
    factor = F32(1.0 / ROOT * np.log2(np.e))
    for window, group, rows, at in sections():
        query = packed_ref[rows, at : at + GROUP]
        keys = packed_ref[rows, WIDTH + at : WIDTH + at + GROUP]
        for h in range(PER_GROUP):
            head = group * PER_GROUP + h
            left = jnp.concatenate([keys, key_ref[:, head * GROUP : (head + 1) * GROUP]], axis=1)
            right = jnp.concatenate([query * masks[h], query_features], axis=1)
            scores_ref[window * HEADS + head] = mm_t(left, right)
    for item in range(WINDOWS * HEADS):
        scores = scores_ref[item]
        top = jnp.max(scores, axis=0, keepdims=True)
        raised = jnp.exp2((scores - top) * factor)
        total = jnp.sum(raised, axis=0, keepdims=True)
        probs_ref[item] = (raised * (1.0 / total)).astype(BF16)
    for window, group, rows, at in sections():
        values_t = packed_ref[rows, 2 * WIDTH + at : 2 * WIDTH + at + GROUP].T
        for h in range(PER_GROUP):
            head = group * PER_GROUP + h
            mixed = mm(values_t[h * HEAD : (h + 1) * HEAD], probs_ref[window * HEADS + head])
            mixed_t_ref[window, head * HEAD : (head + 1) * HEAD, :] = mixed.astype(BF16)
    parts = [mm(mixed_t_ref[window].T, out_ref[...]) for window in range(WINDOWS)]
    return normed, jnp.concatenate(parts, axis=0)


def sections():
    for window in range(WINDOWS):
        for group in range(GROUPS):
            rows = slice(window * LENGTH, (window + 1) * LENGTH)
            yield window, group, rows, group * GROUP


def backward_core(
    upstream, out_ref, packed_ref, probs_ref, mixed_t_ref, d_packed_ref, d_probs_ref, d_scores_ref
):
    masks = head_masks()
    d_mixed = mm_t(upstream, out_ref[...]).astype(BF16)
    for window, group, rows, at in sections():
        values = packed_ref[rows, 2 * WIDTH + at : 2 * WIDTH + at + GROUP]
        up = d_mixed[rows, at : at + GROUP]
        for h in range(PER_GROUP):
            d_probs_ref[window * HEADS + group * PER_GROUP + h] = mm_t(values, up * masks[h])
    for window in range(WINDOWS):
        here = upstream[window * LENGTH : (window + 1) * LENGTH]
        d_mixed_t = mm_t(out_ref[...], here).astype(BF16)
        dots = d_mixed_t.astype(F32) * mixed_t_ref[window].astype(F32)
        for head in range(HEADS):
            item = window * HEADS + head
            inner = jnp.sum(dots[head * HEAD : (head + 1) * HEAD], axis=0, keepdims=True)
            d_scores = (d_probs_ref[item] - inner) * F32(1.0 / ROOT)
            d_scores_ref[item] = (probs_ref[item].astype(F32) * d_scores).astype(BF16)
    for window, group, rows, at in sections():
        query = packed_ref[rows, at : at + GROUP]
        keys_t = packed_ref[rows, WIDTH + at : WIDTH + at + GROUP].T
        up = d_mixed[rows, at : at + GROUP]
        d_values = None
        d_keys = None
        d_query = []
        for h in range(PER_GROUP):
            item = window * HEADS + group * PER_GROUP + h
            d_value = mm(probs_ref[item], up * masks[h])
            d_key = mm(d_scores_ref[item], query * masks[h])
            d_values = d_value if d_values is None else d_values + d_value
            d_keys = d_key if d_keys is None else d_keys + d_key
            d_query.append(mm(keys_t[h * HEAD : (h + 1) * HEAD], d_scores_ref[item]))
        d_query = jnp.concatenate(d_query, axis=0).T
        d_packed_ref[rows, at : at + GROUP] = d_query.astype(BF16)
        d_packed_ref[rows, WIDTH + at : WIDTH + at + GROUP] = d_keys.astype(BF16)
        d_packed_ref[rows, 2 * WIDTH + at : 2 * WIDTH + at + GROUP] = d_values.astype(BF16)


def norm_backward(inputs, gain, d_packed, qkv_ref):
    d_normed = mm_t(d_packed, qkv_ref[...]).astype(BF16).astype(F32)
    hat, scale = normalise(inputs)
    d_hat = d_normed * gain
    mean = jnp.mean(d_hat, axis=-1, keepdims=True)
    along = jnp.mean(d_hat * hat, axis=-1, keepdims=True)
    return scale * (d_hat - mean - hat * along)


def grads_half(half, normed_t_ref, mixed_t_ref, upstream, d_packed_ref, result_ref):
    def blocks(ref, *first):
        return [
            ref[(*first, pl.ds(pl.multiple_of((2 * block + half) * 32, 32), 32), slice(None))]
            for block in range(8)
        ]

    left = jnp.concatenate(blocks(normed_t_ref), axis=0)
    qkv = mm(left, d_packed_ref[...]).astype(BF16)
    total = None
    for window in range(WINDOWS):
        left = jnp.concatenate(blocks(mixed_t_ref, window), axis=0)
        part = mm(left, upstream[window * LENGTH : (window + 1) * LENGTH])
        total = part if total is None else total + part
    total = total.astype(BF16)
    result_ref[:, :768] = qkv[:, :768]
    result_ref[:, 768:SIDE] = total[:, :256]
    result_ref[:, SIDE : SIDE + 768] = qkv[:, 768:]
    result_ref[:, SIDE + 768 :] = total[:, 256:]


def load_grid(ref, place, spare_ref):
    for row in range(12):
        for column in range(6):
            at = (row * 6 + column) * 4
            spare_ref[at : at + 4, :] = ref[row, column].astype(F32)
    return mm(place, spare_ref[...].astype(BF16))


def store_grid(ref, place_t, tokens):
    spread = mm(place_t, tokens)
    for row in range(12):
        for column in range(6):
            at = (row * 6 + column) * 4
            ref[row, column] = spread[at : at + 4].astype(BF16)


def split_pieces(sort, tokens, refs):
    tokens = mm(sort, tokens)
    for at, ref in enumerate(refs):
        ref[...] = tokens[at * PIECE : (at + 1) * PIECE].astype(BF16)


def join_pieces(sort_t, pieces):
    tokens = jnp.concatenate([piece.astype(F32) for piece in pieces], axis=0)
    return mm(sort_t, tokens.astype(BF16))


def fetch(pairs, sems):
    copies = [
        pltpu.make_async_copy(source, target, sems.at[at])
        for at, (source, target) in enumerate(pairs)
    ]
    for copy in copies:
        copy.start()
    return copies


def kernel_forward_a(
    fields_hbm, ids_hbm, gain_hbm, table_hbm, qkv_hbm, out_hbm, place_hbm, sort_hbm, where_hbm,
    piece0, piece1, piece2, piece3, inputs_out, middle_out, normed_out, packed, probs, mixed_t,
    fields, ids, gain, table, qkv, out, place, sort, where, grid, spare, key_features, scores, sems,
):
    *early, qkv_in, out_in, sort_in = fetch(
        (
            (ids_hbm, ids), (where_hbm, where), (table_hbm, table), (fields_hbm, fields),
            (place_hbm, place), (gain_hbm, gain), (qkv_hbm, qkv), (out_hbm, out), (sort_hbm, sort),
        ),
        sems,
    )
    for copy in early:
        copy.wait()
    query_features, features = bias_features(ids, where, table, spare, 0, False)
    key_features[...] = features
    inputs = load_grid(fields, place[...], grid)
    inputs_out[...] = inputs.astype(BF16)
    qkv_in.wait()
    out_in.wait()
    normed, delta = forward_core(
        inputs, gain[...].reshape(1, WIDTH), qkv, out, query_features, key_features,
        packed, probs, mixed_t, scores,
    )
    normed_out[...] = normed
    middle = (inputs + delta).astype(BF16)
    middle_out[...] = middle
    sort_in.wait()
    split_pieces(sort[...], middle, (piece0, piece1, piece2, piece3))


def kernel_cotangent(
    cotangent_hbm, place, sort, normed, ids, table, where,
    piece0, piece1, piece2, piece3, upstream_out, normed_t, query_out, key_out,
    cotangent, grid, spare, sems,
):
    (cotangent_in,) = fetch(((cotangent_hbm, cotangent),), sems)
    normed_t[...] = normed[...].T
    query, keys = bias_features(ids, where, table, spare, 6, True)
    query_out[...] = query
    key_out[...] = keys
    cotangent_in.wait()
    upstream = load_grid(cotangent, place[...], grid).astype(BF16)
    upstream_out[...] = upstream
    split_pieces(sort[...], upstream, (piece0, piece1, piece2, piece3))


def kernel_forward_b(
    piece0, piece1, piece2, piece3, query_features, key_features, gain, qkv, out, sort, sort_t,
    back0, back1, back2, back3, inputs_out, normed_out, packed, probs, mixed_t,
    scores,
):
    inputs = join_pieces(sort_t[...], [ref[...] for ref in (piece0, piece1, piece2, piece3)])
    inputs_out[...] = inputs.astype(BF16)
    normed, delta = forward_core(
        inputs, gain[...].reshape(1, WIDTH), qkv, out, query_features[...], key_features,
        packed, probs, mixed_t, scores,
    )
    normed_out[...] = normed
    split_pieces(sort[...], delta.astype(BF16), (back0, back1, back2, back3))


def kernel_backward_b(
    piece0, piece1, piece2, piece3, inputs, gain, qkv, out, packed, probs, mixed_t, sort, sort_t,
    back0, back1, back2, back3, upstream_out, d_packed,
    d_probs, d_scores,
):
    pieces = [ref[...] for ref in (piece0, piece1, piece2, piece3)]
    upstream = join_pieces(sort_t[...], pieces).astype(BF16)
    upstream_out[...] = upstream
    backward_core(upstream, out, packed, probs, mixed_t, d_packed, d_probs, d_scores)
    d_inputs = norm_backward(
        inputs[...].astype(F32), gain[...].reshape(1, WIDTH), d_packed[...], qkv
    )
    split_pieces(sort[...], d_inputs.astype(BF16), (back0, back1, back2, back3))


def kernel_grads_b(normed, mixed_t, upstream, d_packed, send, keep, normed_t):
    normed_t[...] = normed[...].T
    core = lax.axis_index("lat") % 2
    grads_half(1 - core, normed_t, mixed_t, upstream[...], d_packed, send)
    grads_half(core, normed_t, mixed_t, upstream[...], d_packed, keep)


def kernel_backward_a(
    back0, back1, back2, back3, upstream, out, packed, probs, mixed_t, normed_t, sort_t,
    grad_middle_out, d_packed, send,
    d_probs, d_scores,
):
    d_inputs = join_pieces(sort_t[...], [ref[...] for ref in (back0, back1, back2, back3)])
    grad_middle = (upstream[...].astype(F32) + d_inputs).astype(BF16)
    grad_middle_out[...] = grad_middle
    backward_core(grad_middle, out, packed, probs, mixed_t, d_packed, d_probs, d_scores)
    core = lax.axis_index("lat") % 2
    grads_half(1 - core, normed_t, mixed_t, grad_middle, d_packed, send)


def kernel_keep_a(normed_t, mixed_t, grad_middle, d_packed, keep):
    core = lax.axis_index("lat") % 2
    grads_half(core, normed_t, mixed_t, grad_middle[...], d_packed, keep)


def kernel_advanced(back0, back1, back2, back3, middle, place_t, sort_t, advanced):
    delta = join_pieces(sort_t[...], [ref[...] for ref in (back0, back1, back2, back3)])
    store_grid(advanced, place_t[...], (middle[...].astype(F32) + delta).astype(BF16))


def kernel_finish_a(
    inputs, grad_middle, gain, qkv_hbm, d_packed, place_t, grad_fields, qkv, sems
):
    (qkv_in,) = fetch(((qkv_hbm, qkv),), sems)
    qkv_in.wait()
    d_inputs = norm_backward(
        inputs[...].astype(F32), gain[...].reshape(1, WIDTH), d_packed[...], qkv
    )
    total = (grad_middle[...].astype(F32) + d_inputs).astype(BF16)
    store_grid(grad_fields, place_t[...], total)


def rows_of(block, count):
    return pl.ds(pl.multiple_of(block * count, count), count)


def place_x():
    return lax.axis_index("lon") // 8 * 2 + lax.axis_index("lat") // 2 % 2


def place_y():
    return lax.axis_index("lat") // 4


def kernel_first_sum_a(keep, got, send_one, send_two, keep_one, keep_two):
    y = place_y()
    for side, first, send, kept in ((0, 1, send_one, keep_one), (1, 3, send_two, keep_two)):
        columns = slice(side * SIDE, (side + 1) * SIDE)
        for target, place, block in (
            (send, 0, y ^ first), (send, 1, y ^ 2), (kept, 0, y), (kept, 1, y ^ 2 ^ first)
        ):
            rows = rows_of(block, 64)
            target[place] = keep[rows, columns] + got[rows, columns]


def kernel_first_sum_b(keep, got, send, kept):
    x = place_x()
    for target, place, block in ((send, 0, x ^ 1), (send, 1, x ^ 2), (kept, 0, x), (kept, 1, x ^ 3)):
        columns = rows_of(block // 2, SIDE)
        for y in range(4):
            rows = rows_of(y * 2 + block % 2, 32)
            target[place, y * 32 : (y + 1) * 32] = keep[rows, columns] + got[rows, columns]


def kernel_second_sum(keep_one, got_one, keep_two, got_two, send_one, send_two, held_one, held_two):
    send_one[...] = keep_one[1] + got_one[1]
    send_two[...] = keep_two[1] + got_two[1]
    held_one[...] = keep_one[0] + got_one[0]
    held_two[...] = keep_two[0] + got_two[0]


def third_sum(at, halves, send, keep):
    for target, place, block in ((send, 0, at ^ 1), (send, 1, at ^ 2), (keep, 0, at), (keep, 1, at ^ 3)):
        rows = rows_of(block % 2, 32)
        for half, (held, got) in enumerate(halves):

            @pl.when(block // 2 == half)
            def _(target=target, place=place, rows=rows, held=held, got=got):
                target[place] = held[rows, :] + got[rows, :]


def kernel_third_sum_a(held_one, got_one, held_two, got_two, send, keep):
    third_sum(place_x(), ((held_one, got_one), (held_two, got_two)), send, keep)


def kernel_third_sum_b(held, got, send, keep):
    y = place_y()
    for target, place, block in ((send, 0, y ^ 1), (send, 1, y ^ 2), (keep, 0, y), (keep, 1, y ^ 3)):
        rows = rows_of(block, 32)
        target[place] = held[0, rows] + got[0, rows]


def kernel_halve(keep, got, send, held):
    half = keep.shape[0] // 2
    held[...] = keep[:half] + got[:half]
    send[...] = keep[half:] + got[half:]


def kernel_columns(keep_a, got_a, keep_b, got_b, blocks):
    for rows, held, got in ((slice(0, 32), keep_a, got_a), (slice(32, 64), keep_b, got_b)):
        total = held[0].astype(F32) + got[0].astype(F32)
        for block in range(8):
            qkv = total[:, block * 96 : (block + 1) * 96]
            out = total[:, 768 + block * 32 : 768 + (block + 1) * 32]
            blocks[block, rows] = jnp.concatenate([qkv, out], axis=1).astype(BF16)


def kernel_total(parts, qkv_a, out_a, qkv_b, out_b):
    total = parts[0].astype(F32)
    for at in range(1, 8):
        total = total + parts[at].astype(F32)
    for rows, qkv, out in ((slice(0, 32), qkv_a, out_a), (slice(32, 64), qkv_b, out_b)):
        qkv[...] = total[rows, :96]
        out[...] = total[rows, 96:]


def call(kernel, outs, scratch, args, smem=(), hbm=(), copies=0, flops=0, final=()):
    def space(at):
        return pltpu.SMEM if at in smem else pltpu.HBM if at in hbm else pltpu.VMEM

    cost = pl.CostEstimate(flops=flops, bytes_accessed=1 << 20, transcendentals=0) if flops else None
    args = [
        pltpu.with_memory_space_constraint(arg, pltpu.HBM) if at in hbm or at in smem else arg
        for at, arg in enumerate(args)
    ]
    shapes = [pltpu.VMEM(*item) if isinstance(item, tuple) else item for item in scratch]
    if copies:
        shapes.append(pltpu.SemaphoreType.DMA((copies,)))
    return pl.pallas_call(
        kernel,
        out_shape=tuple(
            jax.ShapeDtypeStruct(shape, kind) if at in final else pltpu.VMEM(shape, kind)
            for at, (shape, kind) in enumerate(outs)
        ),
        in_specs=[pl.BlockSpec(memory_space=space(at)) for at in range(len(args))],
        out_specs=tuple(pl.BlockSpec(memory_space=pltpu.VMEM) for _ in outs),
        scratch_shapes=shapes,
        cost_estimate=cost,
        compiler_params=pltpu.CompilerParams(vmem_limit_bytes=VMEM_LIMIT),
    )(*args)


def permute(array, axis, target):
    length = lax.axis_size(axis)
    return lax.ppermute(array, axis, [(i, target(i) % length) for i in range(length)])


def permute_both(array, by):
    lons, lats = lax.axis_size("lon"), lax.axis_size("lat")
    pairs = [
        (lon * lats + lat, (lon + by) % lons * lats + (lat + by) % lats)
        for lon in range(lons)
        for lat in range(lats)
    ]
    return lax.ppermute(array, ("lon", "lat"), pairs)


def to_core(array):
    return permute(array, "lat", lambda i: i ^ 1)


def to_y(array, by):
    return permute(array, "lat", lambda i: i ^ (4 * by))


def to_x(array, by):
    if by == 1:
        return permute(array, "lat", lambda i: i ^ 2)
    lons, lats = lax.axis_size("lon"), lax.axis_size("lat")
    pairs = [
        (lon * lats + lat, (lon ^ 8) * lats + (lat ^ 2)) for lon in range(lons) for lat in range(lats)
    ]
    return lax.ppermute(array, ("lon", "lat"), pairs)


def quarters(kernel, keep, got):
    return call(kernel, [((2, 64, SIDE), BF16)] * 4, [], (keep, got))


def second_sum(parts):
    return call(kernel_second_sum, [((64, SIDE), BF16)] * 4, [], parts)


def halve(keep, got):
    shape = (keep.shape[0] // 2,) + keep.shape[1:]
    return call(kernel_halve, [(shape, BF16)] * 2, [], (keep, got))


def exchange_z(messages):
    groups = [[x_hi * 8 + z for z in range(8)] for x_hi in range(2)]
    return lax.all_to_all(messages, "lon", 0, 0, axis_index_groups=groups, tiled=True)


def body(
    fields, cotangent, land_ids, gain_a, table_a, qkv_weight_a, out_weight_a,
    gain_b, table_b, qkv_weight_b, out_weight_b,
):
    place = jnp.asarray(PLACE, BF16)
    place_t = jnp.asarray(PLACE.T, BF16)
    sort = jnp.asarray(SORT, BF16)
    sort_t = jnp.asarray(SORT.T, BF16)
    where = jnp.asarray(WHERE)
    fields = fields.transpose(1, 2, 0, 3)
    cotangent = cotangent.transpose(1, 2, 0, 3)
    table_a = table_a.transpose(1, 2, 0)
    table_b = table_b.transpose(1, 2, 0)
    grid = (fields.shape, BF16)
    piece = ((PIECE, WIDTH), BF16)
    token = ((TOKENS, WIDTH), BF16)
    token_wide = ((TOKENS, WIDTH), F32)
    packed = ((TOKENS, 3 * WIDTH), BF16)
    probs = ((WINDOWS * HEADS, LENGTH, LENGTH), BF16)
    scores = ((WINDOWS * HEADS, LENGTH, LENGTH), F32)
    mixed_t = ((WINDOWS, WIDTH, LENGTH), BF16)
    half_grads = ((WIDTH // 2, 4 * WIDTH), BF16)
    normed_t = ((WIDTH, TOKENS), BF16)
    square = ((TOKENS, TOKENS), BF16)
    spare = ((16, HEADS * GROUP), BF16)
    query = ((LENGTH, GROUP), BF16)
    keys = ((LENGTH, HEADS * GROUP), BF16)
    ids = (land_ids.shape, jnp.int32)
    place_of = (where.shape, jnp.int32)
    vector = ((WIDTH,), F32)
    qkv_shape = ((WIDTH, 3 * WIDTH), BF16)
    out_shape = ((WIDTH, WIDTH), BF16)

    p0, p1, p2, p3, inputs_a, middle_a, normed_a, packed_a, probs_a, mixed_a = call(
        kernel_forward_a,
        [piece] * 4 + [token] * 3 + [packed, probs, mixed_t],
        [
            grid, ids, vector, pltpu.SMEM(table_a.shape, F32), qkv_shape, out_shape, square, square,
            place_of, token_wide, spare, keys, scores,
        ],
        (fields, land_ids, gain_a, table_a, qkv_weight_a, out_weight_a, place, sort, where),
        hbm=(0, 1, 2, 3, 4, 5, 6, 7, 8), copies=9, flops=7 * 10**9,
    )
    diagonal = permute_both(p0, -1)
    below = permute(p1, "lat", lambda i: i - 1)
    eastern = permute(p2, "lon", lambda i: i - 1)
    c0, c1, c2, c3, upstream_a, normed_a_t, query_b, keys_b = call(
        kernel_cotangent,
        [piece] * 4 + [token, normed_t, query, keys],
        [grid, token_wide, spare],
        (cotangent, place, sort, normed_a, land_ids, table_b, where),
        smem=(5,), hbm=(0,), copies=1, flops=2 * 10**9,
    )
    c_diagonal = permute_both(c0, -1)
    c_below = permute(c1, "lat", lambda i: i - 1)
    c_eastern = permute(c2, "lon", lambda i: i - 1)
    b0, b1, b2, b3, inputs_b, normed_b, packed_b, probs_b, mixed_b = call(
        kernel_forward_b,
        [piece] * 4 + [token] * 2 + [packed, probs, mixed_t],
        [scores],
        (p3, eastern, below, diagonal, query_b, keys_b, gain_b, qkv_weight_b, out_weight_b, sort, sort_t),
        flops=5 * 10**9,
    )
    d0, d1, d2, d3, upstream_b, d_packed_b = call(
        kernel_backward_b,
        [piece] * 4 + [token, packed],
        [scores, probs],
        (
            c3, c_eastern, c_below, c_diagonal, inputs_b, gain_b, qkv_weight_b, out_weight_b,
            packed_b, probs_b, mixed_b, sort, sort_t,
        ),
        flops=5 * 10**9,
    )
    d3 = permute_both(d3, 1)
    d2 = permute(d2, "lat", lambda i: i + 1)
    d1 = permute(d1, "lon", lambda i: i + 1)
    send_b, keep_b = call(
        kernel_grads_b, [half_grads] * 2, [normed_t], (normed_b, mixed_b, upstream_b, d_packed_b),
        flops=2 * 10**9,
    )
    send_b, keep_b = call(
        kernel_first_sum_b, [((2, 128, SIDE), BF16)] * 2, [], (keep_b, to_core(send_b))
    )
    got_b = to_x(send_b, 1)
    grad_middle, d_packed_a, send_a = call(
        kernel_backward_a,
        [token, packed, half_grads],
        [scores, probs],
        (
            d3, d2, d1, d0, upstream_a, out_weight_a, packed_a, probs_a, mixed_a, normed_a_t,
            sort_t,
        ),
        flops=5 * 10**9,
    )
    got_a = to_core(send_a)
    keep_a = call(
        kernel_keep_a, [half_grads], [], (normed_a_t, mixed_a, grad_middle, d_packed_a),
        flops=10**9,
    )[0]
    send_one_a, send_two_a, keep_one_a, keep_two_a = quarters(kernel_first_sum_a, keep_a, got_a)
    send_one_a, send_two_a, d_packed_a = lax.optimization_barrier((send_one_a, send_two_a, d_packed_a))
    parts_a = (keep_one_a, to_y(send_one_a, 1), keep_two_a, to_y(send_two_a, 3))
    grad_fields = call(
        kernel_finish_a,
        [grid],
        [qkv_shape],
        (inputs_a, grad_middle, gain_a, qkv_weight_a, d_packed_a, place_t),
        hbm=(3,), copies=1, flops=4 * 10**9, final=(0,),
    )[0]
    got_b, grad_fields = lax.optimization_barrier((got_b, grad_fields))
    send_b, keep_b = halve(keep_b, got_b)
    got_b = to_x(send_b, 3)
    pair = ((2, 32, SIDE), BF16)
    send_b, keep_b = call(kernel_third_sum_b, [pair] * 2, [], (keep_b, got_b))
    got_b = to_y(send_b, 1)
    send_one_a, send_two_a, held_one_a, held_two_a = second_sum(parts_a)
    send_one_a, send_two_a, grad_fields = lax.optimization_barrier(
        (send_one_a, send_two_a, grad_fields)
    )
    parts_a = (held_one_a, to_y(send_one_a, 3), held_two_a, to_y(send_two_a, 1))
    send_a, keep_a = call(kernel_third_sum_a, [pair] * 2, [], parts_a)
    got_a = to_x(send_a, 1)
    send_b, keep_b = halve(keep_b, got_b)
    got_b = to_y(send_b, 3)
    send_a, keep_a = halve(keep_a, got_a)
    got_a = to_x(send_a, 3)
    blocks = call(
        kernel_columns, [((8, 64, GROUP), BF16)], [], (keep_a, got_a, keep_b, got_b)
    )[0]
    blocks, b1, b2, b3 = lax.optimization_barrier((blocks, b1, b2, b3))
    parts = exchange_z(blocks)
    advanced = call(
        kernel_advanced,
        [grid],
        [],
        (
            permute_both(b3, 1), permute(b2, "lat", lambda i: i + 1),
            permute(b1, "lon", lambda i: i + 1), b0, middle_a, place_t, sort_t,
        ),
        flops=10**9, final=(0,),
    )[0]
    grads = call(
        kernel_total,
        [((32, 96), F32), ((32, 32), F32)] * 2,
        [],
        (parts,),
        final=(0, 1, 2, 3),
    )
    return (advanced.transpose(2, 0, 1, 3), grad_fields.transpose(2, 0, 1, 3), *grads)


def solution(mesh):
    grid = P(None, "lat", "lon", None)
    return jax.shard_map(
        body,
        mesh=mesh,
        in_specs=(grid, grid) + (P(),) * 9,
        out_specs=(grid, grid) + (P("lat", "lon"),) * 4,
        check_vma=False,
    )
```

```python
import jax
import jax.numpy as jnp
import numpy as np
from jax import lax
from jax.experimental import pallas as pl
from jax.experimental.pallas import tpu as pltpu
from jax.sharding import PartitionSpec as P

WINDOWS = 2
LENGTH = 144
QUARTER = 36
TOKENS = WINDOWS * LENGTH
PIECE = WINDOWS * QUARTER
WIDTH = 512
HEADS = 16
HEAD = 32
GROUP = 128
GROUPS = WIDTH // GROUP
PER_GROUP = GROUP // HEAD
ROOT = HEAD**0.5
Z_GROUPS = ((0, 3, 4, 7), (1, 2, 5, 6))
SIDE = 2 * WIDTH
EPS = 1e-05
NEG = -1000000000.0
VMEM_LIMIT = 24 * 1024 * 1024
F32 = jnp.float32
BF16 = jnp.bfloat16


def _tables():
    place = np.zeros((TOKENS, TOKENS), np.float32)
    sort = np.zeros((TOKENS, TOKENS), np.float32)
    where = np.zeros((LENGTH, 8), np.int32)
    for window in range(WINDOWS):
        for quadrant in range(4):
            for level in range(2):
                for row in range(6):
                    for column in range(3):
                        inner = level * 18 + row * 3 + column
                        at = quadrant * QUARTER + inner
                        token = window * LENGTH + at
                        lat = quadrant // 2 * 6 + row
                        lon = quadrant % 2 * 3 + column
                        source = (lat * 6 + lon) * 4 + 2 * window + level
                        place[token, source] = 1
                        sort[quadrant * PIECE + window * QUARTER + inner, token] = 1
                        where[at, 0] = lat
                        where[at, 1] = lon
    return place, sort, where


PLACE, SORT, WHERE = _tables()


def mm(left, right):
    return jnp.dot(left, right, preferred_element_type=F32)


def mm_t(left, right):
    return lax.dot_general(left, right, (((1,), (1,)), ((), ())), preferred_element_type=F32)


def normalise(inputs):
    centre = inputs - jnp.mean(inputs, axis=-1, keepdims=True)
    spread = jnp.mean(centre * centre, axis=-1, keepdims=True)
    scale = lax.rsqrt(spread + EPS)
    return centre * scale, scale


def lanes(shape):
    return lax.broadcasted_iota(jnp.int32, shape, 1)


def head_masks():
    lane = lanes((1, GROUP))
    return [
        ((lane >= h * HEAD) & (lane < (h + 1) * HEAD)).astype(F32).astype(BF16)
        for h in range(PER_GROUP)
    ]


def bias_features(ids_ref, where_ref, table_ref, spare_ref, shift, last):
    lat_at = lax.axis_index("lat")
    lon_at = lax.axis_index("lon")
    rows, columns = ids_ref.shape
    row = where_ref[:, 0:1]
    column = where_ref[:, 1:2] + (lon_at * 6 + shift // 2)
    at = row + (lat_at * 12 + shift)
    at = jnp.where(at >= rows, at - rows, at)
    column = jnp.where(column >= columns, column - columns, column)
    pick = (lanes((LENGTH, rows)) == at).astype(F32).astype(BF16)
    found = mm(pick, ids_ref[...].astype(F32).astype(BF16))
    found = jnp.where(lanes((LENGTH, columns)) == column, found, 0.0)
    kind = jnp.sum(found, axis=1, keepdims=True).astype(jnp.int32)
    lane = lanes((LENGTH, GROUP))
    third = (lane >= 3).astype(jnp.int32) + (lane >= 6).astype(jnp.int32)
    query = ((lane < 9) & (third == kind)).astype(F32)
    key = ((lane < 3) & (lane == kind)).astype(F32)
    if last:
        flag = ((row >= 6) & (lat_at == lax.axis_size("lat") - 1)).astype(F32)
        query = jnp.where(lane == 9, flag, jnp.where(lane == 10, 1.0 - flag, query))
        key = jnp.where(lane == 3, 1.0 - flag, jnp.where(lane == 4, flag, key))
    small = (16, GROUP)
    lane = lanes(small)
    sub = lax.broadcasted_iota(jnp.int32, small, 0)
    third = (lane >= 3).astype(jnp.int32) + (lane >= 6).astype(jnp.int32)
    part = lane - 3 * third
    spots = {
        (first, second): (lane < 9) & (third == first) & (sub == second)
        for first in range(3)
        for second in range(3)
    }
    fixed = jnp.where(((sub == 3) & (lane == 9)) | ((sub == 4) & (lane == 10)), NEG * ROOT, 0.0)
    for head in range(HEADS):
        entry = fixed
        for (first, second), spot in spots.items():
            entry = jnp.where(spot, table_ref[first, second, head] * ROOT, entry)
        high = entry.astype(BF16).astype(F32)
        middle = (entry - high).astype(BF16).astype(F32)
        low = entry - high - middle
        entry = jnp.where(part == 0, high, jnp.where(part == 1, middle, low))
        entry = jnp.where(lane >= 9, high, entry)
        spare_ref[:, head * GROUP : (head + 1) * GROUP] = entry.astype(BF16)
    features = mm(key.astype(BF16)[:, :16], spare_ref[...])
    return query.astype(BF16), features.astype(BF16)


def forward_core(
    inputs, gain, qkv_ref, out_ref, query_features, key_ref, packed_ref, probs_ref, mixed_t_ref, scores_ref
):
    hat, _ = normalise(inputs)
    normed = (hat * gain).astype(BF16)
    packed_ref[...] = mm(normed, qkv_ref[...]).astype(BF16)
    masks = head_masks()
    factor = F32(1.0 / ROOT * np.log2(np.e))
    for window, group, rows, at in sections():
        query = packed_ref[rows, at : at + GROUP]
        keys = packed_ref[rows, WIDTH + at : WIDTH + at + GROUP]
        for h in range(PER_GROUP):
            head = group * PER_GROUP + h
            left = jnp.concatenate([keys, key_ref[:, head * GROUP : (head + 1) * GROUP]], axis=1)
            right = jnp.concatenate([query * masks[h], query_features], axis=1)
            scores_ref[window * HEADS + head] = mm_t(left, right)
    for item in range(WINDOWS * HEADS):
        scores = scores_ref[item]
        top = jnp.max(scores, axis=0, keepdims=True)
        raised = jnp.exp2((scores - top) * factor)
        total = jnp.sum(raised, axis=0, keepdims=True)
        probs_ref[item] = (raised * (1.0 / total)).astype(BF16)
    for window, group, rows, at in sections():
        values_t = packed_ref[rows, 2 * WIDTH + at : 2 * WIDTH + at + GROUP].T
        for h in range(PER_GROUP):
            head = group * PER_GROUP + h
            mixed = mm(values_t[h * HEAD : (h + 1) * HEAD], probs_ref[window * HEADS + head])
            mixed_t_ref[window, head * HEAD : (head + 1) * HEAD, :] = mixed.astype(BF16)
    parts = [mm(mixed_t_ref[window].T, out_ref[...]) for window in range(WINDOWS)]
    return normed, jnp.concatenate(parts, axis=0)


def sections():
    for window in range(WINDOWS):
        for group in range(GROUPS):
            rows = slice(window * LENGTH, (window + 1) * LENGTH)
            yield window, group, rows, group * GROUP


def backward_core(
    upstream, out_ref, packed_ref, probs_ref, mixed_t_ref, d_packed_ref, d_probs_ref, d_scores_ref
):
    masks = head_masks()
    d_mixed = mm_t(upstream, out_ref[...]).astype(BF16)
    for window, group, rows, at in sections():
        values = packed_ref[rows, 2 * WIDTH + at : 2 * WIDTH + at + GROUP]
        up = d_mixed[rows, at : at + GROUP]
        for h in range(PER_GROUP):
            d_probs_ref[window * HEADS + group * PER_GROUP + h] = mm_t(values, up * masks[h])
    for window in range(WINDOWS):
        here = upstream[window * LENGTH : (window + 1) * LENGTH]
        d_mixed_t = mm_t(out_ref[...], here).astype(BF16)
        dots = d_mixed_t.astype(F32) * mixed_t_ref[window].astype(F32)
        for head in range(HEADS):
            item = window * HEADS + head
            inner = jnp.sum(dots[head * HEAD : (head + 1) * HEAD], axis=0, keepdims=True)
            d_scores = (d_probs_ref[item] - inner) * F32(1.0 / ROOT)
            d_scores_ref[item] = (probs_ref[item].astype(F32) * d_scores).astype(BF16)
    for window, group, rows, at in sections():
        query = packed_ref[rows, at : at + GROUP]
        keys_t = packed_ref[rows, WIDTH + at : WIDTH + at + GROUP].T
        up = d_mixed[rows, at : at + GROUP]
        d_values = None
        d_keys = None
        d_query = []
        for h in range(PER_GROUP):
            item = window * HEADS + group * PER_GROUP + h
            d_value = mm(probs_ref[item], up * masks[h])
            d_key = mm(d_scores_ref[item], query * masks[h])
            d_values = d_value if d_values is None else d_values + d_value
            d_keys = d_key if d_keys is None else d_keys + d_key
            d_query.append(mm(keys_t[h * HEAD : (h + 1) * HEAD], d_scores_ref[item]))
        d_query = jnp.concatenate(d_query, axis=0).T
        d_packed_ref[rows, at : at + GROUP] = d_query.astype(BF16)
        d_packed_ref[rows, WIDTH + at : WIDTH + at + GROUP] = d_keys.astype(BF16)
        d_packed_ref[rows, 2 * WIDTH + at : 2 * WIDTH + at + GROUP] = d_values.astype(BF16)


def norm_backward(inputs, gain, d_packed, qkv_ref):
    d_normed = mm_t(d_packed, qkv_ref[...]).astype(BF16).astype(F32)
    hat, scale = normalise(inputs)
    d_hat = d_normed * gain
    mean = jnp.mean(d_hat, axis=-1, keepdims=True)
    along = jnp.mean(d_hat * hat, axis=-1, keepdims=True)
    return scale * (d_hat - mean - hat * along)


def grads_half(half, normed_t_ref, mixed_t_ref, upstream, d_packed_ref, result_ref):
    def blocks(ref, *first):
        return [
            ref[(*first, pl.ds(pl.multiple_of((2 * block + half) * 32, 32), 32), slice(None))]
            for block in range(8)
        ]

    left = jnp.concatenate(blocks(normed_t_ref), axis=0)
    qkv = mm(left, d_packed_ref[...]).astype(BF16)
    total = None
    for window in range(WINDOWS):
        left = jnp.concatenate(blocks(mixed_t_ref, window), axis=0)
        part = mm(left, upstream[window * LENGTH : (window + 1) * LENGTH])
        total = part if total is None else total + part
    total = total.astype(BF16)
    result_ref[:, :768] = qkv[:, :768]
    result_ref[:, 768:SIDE] = total[:, :256]
    result_ref[:, SIDE : SIDE + 768] = qkv[:, 768:]
    result_ref[:, SIDE + 768 :] = total[:, 256:]


def load_grid(ref, place, spare_ref):
    for row in range(12):
        for column in range(6):
            at = (row * 6 + column) * 4
            spare_ref[at : at + 4, :] = ref[row, column].astype(F32)
    return mm(place, spare_ref[...].astype(BF16))


def store_grid(ref, place_t, tokens):
    spread = mm(place_t, tokens)
    for row in range(12):
        for column in range(6):
            at = (row * 6 + column) * 4
            ref[row, column] = spread[at : at + 4].astype(BF16)


def split_pieces(sort, tokens, refs):
    tokens = mm(sort, tokens)
    for at, ref in enumerate(refs):
        ref[...] = tokens[at * PIECE : (at + 1) * PIECE].astype(BF16)


def join_pieces(sort_t, pieces):
    tokens = jnp.concatenate([piece.astype(F32) for piece in pieces], axis=0)
    return mm(sort_t, tokens.astype(BF16))


def fetch(pairs, sems):
    copies = [
        pltpu.make_async_copy(source, target, sems.at[at])
        for at, (source, target) in enumerate(pairs)
    ]
    for copy in copies:
        copy.start()
    return copies


def kernel_forward_a(
    fields_hbm, ids_hbm, gain_hbm, table_hbm, qkv_hbm, out_hbm, place_hbm, sort_hbm, where_hbm,
    piece0, piece1, piece2, piece3, inputs_out, middle_out, normed_out, packed, probs, mixed_t,
    fields, ids, gain, table, qkv, out, place, sort, where, grid, spare, key_features, scores, sems,
):
    *early, qkv_in, out_in, sort_in = fetch(
        (
            (ids_hbm, ids), (where_hbm, where), (table_hbm, table), (fields_hbm, fields),
            (place_hbm, place), (gain_hbm, gain), (qkv_hbm, qkv), (out_hbm, out), (sort_hbm, sort),
        ),
        sems,
    )
    for copy in early:
        copy.wait()
    query_features, features = bias_features(ids, where, table, spare, 0, False)
    key_features[...] = features
    inputs = load_grid(fields, place[...], grid)
    inputs_out[...] = inputs.astype(BF16)
    qkv_in.wait()
    out_in.wait()
    normed, delta = forward_core(
        inputs, gain[...].reshape(1, WIDTH), qkv, out, query_features, key_features,
        packed, probs, mixed_t, scores,
    )
    normed_out[...] = normed
    middle = (inputs + delta).astype(BF16)
    middle_out[...] = middle
    sort_in.wait()
    split_pieces(sort[...], middle, (piece0, piece1, piece2, piece3))


def kernel_cotangent(
    cotangent_hbm, place, sort, normed, ids, table, where,
    piece0, piece1, piece2, piece3, upstream_out, normed_t, query_out, key_out,
    cotangent, grid, spare, sems,
):
    (cotangent_in,) = fetch(((cotangent_hbm, cotangent),), sems)
    normed_t[...] = normed[...].T
    query, keys = bias_features(ids, where, table, spare, 6, True)
    query_out[...] = query
    key_out[...] = keys
    cotangent_in.wait()
    upstream = load_grid(cotangent, place[...], grid).astype(BF16)
    upstream_out[...] = upstream
    split_pieces(sort[...], upstream, (piece0, piece1, piece2, piece3))


def kernel_forward_b(
    piece0, piece1, piece2, piece3, query_features, key_features, gain, qkv, out, sort, sort_t,
    back0, back1, back2, back3, inputs_out, normed_out, packed, probs, mixed_t,
    scores,
):
    inputs = join_pieces(sort_t[...], [ref[...] for ref in (piece0, piece1, piece2, piece3)])
    inputs_out[...] = inputs.astype(BF16)
    normed, delta = forward_core(
        inputs, gain[...].reshape(1, WIDTH), qkv, out, query_features[...], key_features,
        packed, probs, mixed_t, scores,
    )
    normed_out[...] = normed
    split_pieces(sort[...], delta.astype(BF16), (back0, back1, back2, back3))


def kernel_backward_b(
    piece0, piece1, piece2, piece3, delta0, delta1, delta2, delta3,
    inputs, gain, qkv, out, packed, probs, mixed_t, sort, sort_t,
    back0, back1, back2, back3, upstream_out, d_packed,
    d_probs, d_scores,
):
    pieces = [ref[...] for ref in (piece0, piece1, piece2, piece3)]
    upstream = join_pieces(sort_t[...], pieces).astype(BF16)
    upstream_out[...] = upstream
    backward_core(upstream, out, packed, probs, mixed_t, d_packed, d_probs, d_scores)
    d_inputs = norm_backward(
        inputs[...].astype(F32), gain[...].reshape(1, WIDTH), d_packed[...], qkv
    )
    backs = (back0, back1, back2, back3)
    split_pieces(sort[...], d_inputs.astype(BF16), [back.at[0] for back in backs])
    for back, delta in zip(backs, (delta0, delta1, delta2, delta3), strict=True):
        back[1] = delta[...]


def kernel_grads_b(normed, mixed_t, upstream, d_packed, send, keep, normed_t):
    normed_t[...] = normed[...].T
    core = lax.axis_index("lat") % 2
    grads_half(1 - core, normed_t, mixed_t, upstream[...], d_packed, send)
    grads_half(core, normed_t, mixed_t, upstream[...], d_packed, keep)


def kernel_backward_a(
    back0, back1, back2, back3, upstream, out, packed, probs, mixed_t, normed_t, sort_t,
    grad_middle_out, d_packed, send,
    d_probs, d_scores,
):
    d_inputs = join_pieces(sort_t[...], [back[0] for back in (back0, back1, back2, back3)])
    grad_middle = (upstream[...].astype(F32) + d_inputs).astype(BF16)
    grad_middle_out[...] = grad_middle
    backward_core(grad_middle, out, packed, probs, mixed_t, d_packed, d_probs, d_scores)
    core = lax.axis_index("lat") % 2
    grads_half(1 - core, normed_t, mixed_t, grad_middle, d_packed, send)


def kernel_keep_a(normed_t, mixed_t, grad_middle, d_packed, keep):
    core = lax.axis_index("lat") % 2
    grads_half(core, normed_t, mixed_t, grad_middle[...], d_packed, keep)


def kernel_advanced(back0, back1, back2, back3, middle, place_t, sort_t, advanced):
    delta = join_pieces(sort_t[...], [back[1] for back in (back0, back1, back2, back3)])
    store_grid(advanced, place_t[...], (middle[...].astype(F32) + delta).astype(BF16))


def kernel_finish_a(
    inputs, grad_middle, gain, qkv_hbm, d_packed, place_t, grad_fields, qkv, sems
):
    (qkv_in,) = fetch(((qkv_hbm, qkv),), sems)
    qkv_in.wait()
    d_inputs = norm_backward(
        inputs[...].astype(F32), gain[...].reshape(1, WIDTH), d_packed[...], qkv
    )
    total = (grad_middle[...].astype(F32) + d_inputs).astype(BF16)
    store_grid(grad_fields, place_t[...], total)


def rows_of(block, count):
    return pl.ds(pl.multiple_of(block * count, count), count)


def place_x():
    return lax.axis_index("lon") // 8 * 2 + lax.axis_index("lat") // 2 % 2


def place_y():
    return lax.axis_index("lat") // 4


def kernel_first_sum_a(keep, got, send_one, send_two, keep_one, keep_two):
    y = place_y()
    for side, first, send, kept in ((0, 1, send_one, keep_one), (1, 3, send_two, keep_two)):
        columns = slice(side * SIDE, (side + 1) * SIDE)
        for target, place, block in (
            (send, 0, y ^ first), (send, 1, y ^ 2), (kept, 0, y), (kept, 1, y ^ 2 ^ first)
        ):
            rows = rows_of(block, 64)
            target[place] = keep[rows, columns] + got[rows, columns]


def kernel_first_sum_b(keep, got, send_one, send_two, keep_one, keep_two):
    x = place_x()
    for part, first, send, kept in ((0, 1, send_one, keep_one), (1, 3, send_two, keep_two)):
        for target, place, block in (
            (send, 0, x ^ first), (send, 1, x ^ 2), (kept, 0, x), (kept, 1, x ^ 2 ^ first)
        ):
            columns = rows_of(block // 2, SIDE)
            for inner in range(2):
                rows = rows_of((part * 2 + inner) * 2 + block % 2, 32)
                target[place, inner * 32 : (inner + 1) * 32] = keep[rows, columns] + got[rows, columns]


def kernel_second_sum(keep_one, got_one, keep_two, got_two, send_one, send_two, held_one, held_two):
    send_one[...] = keep_one[1] + got_one[1]
    send_two[...] = keep_two[1] + got_two[1]
    held_one[...] = keep_one[0] + got_one[0]
    held_two[...] = keep_two[0] + got_two[0]


def third_sum(at, halves, send, keep):
    for target, place, block in ((send, 0, at ^ 1), (send, 1, at ^ 2), (keep, 0, at), (keep, 1, at ^ 3)):
        rows = rows_of(block % 2, 32)
        for half, (held, got) in enumerate(halves):

            @pl.when(block // 2 == half)
            def _(target=target, place=place, rows=rows, held=held, got=got):
                target[place] = held[rows, :] + got[rows, :]


def kernel_third_sum_a(held_one, got_one, held_two, got_two, send, keep):
    third_sum(place_x(), ((held_one, got_one), (held_two, got_two)), send, keep)


def kernel_third_sum_b(held_one, got_one, held_two, got_two, send, keep):
    third_sum(place_y(), ((held_one, got_one), (held_two, got_two)), send, keep)


def kernel_halve(keep, got, send, held):
    half = keep.shape[0] // 2
    held[...] = keep[:half] + got[:half]
    send[...] = keep[half:] + got[half:]


def kernel_columns(keep_a, got_a, keep_b, got_b, send, keep, blocks):
    for rows, held, got in ((slice(0, 32), keep_a, got_a), (slice(32, 64), keep_b, got_b)):
        total = held[0].astype(F32) + got[0].astype(F32)
        for block in range(8):
            qkv = total[:, block * 96 : (block + 1) * 96]
            out = total[:, 768 + block * 32 : 768 + (block + 1) * 32]
            blocks[block, rows] = jnp.concatenate([qkv, out], axis=1).astype(BF16)
    group = (lax.axis_index("lon") % 8 + 1) // 2 % 2
    for at, (outer, inner) in enumerate(zip(*Z_GROUPS, strict=True)):
        keep[at] = blocks[outer + group * (inner - outer)]
        send[at] = blocks[inner + group * (outer - inner)]


def kernel_sum(keep, got, total):
    total[...] = keep[...] + got[...]


def kernel_total(parts, qkv_a, out_a, qkv_b, out_b):
    total = parts[0].astype(F32)
    for at in range(1, 4):
        total = total + parts[at].astype(F32)
    for rows, qkv, out in ((slice(0, 32), qkv_a, out_a), (slice(32, 64), qkv_b, out_b)):
        qkv[...] = total[rows, :96]
        out[...] = total[rows, 96:]


def call(kernel, outs, scratch, args, smem=(), hbm=(), copies=0, flops=0, final=()):
    def space(at):
        return pltpu.SMEM if at in smem else pltpu.HBM if at in hbm else pltpu.VMEM

    cost = pl.CostEstimate(flops=flops, bytes_accessed=1 << 20, transcendentals=0) if flops else None
    args = [
        pltpu.with_memory_space_constraint(arg, pltpu.HBM) if at in hbm or at in smem else arg
        for at, arg in enumerate(args)
    ]
    shapes = [pltpu.VMEM(*item) if isinstance(item, tuple) else item for item in scratch]
    if copies:
        shapes.append(pltpu.SemaphoreType.DMA((copies,)))
    return pl.pallas_call(
        kernel,
        out_shape=tuple(
            jax.ShapeDtypeStruct(shape, kind) if at in final else pltpu.VMEM(shape, kind)
            for at, (shape, kind) in enumerate(outs)
        ),
        in_specs=[pl.BlockSpec(memory_space=space(at)) for at in range(len(args))],
        out_specs=tuple(pl.BlockSpec(memory_space=pltpu.VMEM) for _ in outs),
        scratch_shapes=shapes,
        cost_estimate=cost,
        compiler_params=pltpu.CompilerParams(vmem_limit_bytes=VMEM_LIMIT),
    )(*args)


def permute(array, axis, target):
    length = lax.axis_size(axis)
    return lax.ppermute(array, axis, [(i, target(i) % length) for i in range(length)])


def permute_both(array, by):
    lons, lats = lax.axis_size("lon"), lax.axis_size("lat")
    pairs = [
        (lon * lats + lat, (lon + by) % lons * lats + (lat + by) % lats)
        for lon in range(lons)
        for lat in range(lats)
    ]
    return lax.ppermute(array, ("lon", "lat"), pairs)


def to_core(array):
    return permute(array, "lat", lambda i: i ^ 1)


def to_y(array, by):
    return permute(array, "lat", lambda i: i ^ (4 * by))


def to_x(array, by):
    if by == 1:
        return permute(array, "lat", lambda i: i ^ 2)
    lons, lats = lax.axis_size("lon"), lax.axis_size("lat")
    pairs = [
        (lon * lats + lat, (lon ^ 8) * lats + (lat ^ 2)) for lon in range(lons) for lat in range(lats)
    ]
    return lax.ppermute(array, ("lon", "lat"), pairs)


def quarters(kernel, keep, got):
    return call(kernel, [((2, 64, SIDE), BF16)] * 4, [], (keep, got))


def second_sum(parts):
    return call(kernel_second_sum, [((64, SIDE), BF16)] * 4, [], parts)


def halve(keep, got):
    shape = (keep.shape[0] // 2,) + keep.shape[1:]
    return call(kernel_halve, [(shape, BF16)] * 2, [], (keep, got))


def to_z(array):
    return permute(array, "lon", lambda i: i ^ 1)


def exchange_z(messages):
    groups = [[x_hi * 8 + z for z in group] for x_hi in range(2) for group in Z_GROUPS]
    return lax.all_to_all(messages, "lon", 0, 0, axis_index_groups=groups, tiled=True)


def body(
    fields, cotangent, land_ids, gain_a, table_a, qkv_weight_a, out_weight_a,
    gain_b, table_b, qkv_weight_b, out_weight_b,
):
    place = jnp.asarray(PLACE, BF16)
    place_t = jnp.asarray(PLACE.T, BF16)
    sort = jnp.asarray(SORT, BF16)
    sort_t = jnp.asarray(SORT.T, BF16)
    where = jnp.asarray(WHERE)
    fields = fields.transpose(1, 2, 0, 3)
    cotangent = cotangent.transpose(1, 2, 0, 3)
    table_a = table_a.transpose(1, 2, 0)
    table_b = table_b.transpose(1, 2, 0)
    grid = (fields.shape, BF16)
    piece = ((PIECE, WIDTH), BF16)
    token = ((TOKENS, WIDTH), BF16)
    token_wide = ((TOKENS, WIDTH), F32)
    packed = ((TOKENS, 3 * WIDTH), BF16)
    probs = ((WINDOWS * HEADS, LENGTH, LENGTH), BF16)
    scores = ((WINDOWS * HEADS, LENGTH, LENGTH), F32)
    mixed_t = ((WINDOWS, WIDTH, LENGTH), BF16)
    half_grads = ((WIDTH // 2, 4 * WIDTH), BF16)
    normed_t = ((WIDTH, TOKENS), BF16)
    square = ((TOKENS, TOKENS), BF16)
    spare = ((16, HEADS * GROUP), BF16)
    query = ((LENGTH, GROUP), BF16)
    keys = ((LENGTH, HEADS * GROUP), BF16)
    ids = (land_ids.shape, jnp.int32)
    place_of = (where.shape, jnp.int32)
    vector = ((WIDTH,), F32)
    qkv_shape = ((WIDTH, 3 * WIDTH), BF16)
    out_shape = ((WIDTH, WIDTH), BF16)

    p0, p1, p2, p3, inputs_a, middle_a, normed_a, packed_a, probs_a, mixed_a = call(
        kernel_forward_a,
        [piece] * 4 + [token] * 3 + [packed, probs, mixed_t],
        [
            grid, ids, vector, pltpu.SMEM(table_a.shape, F32), qkv_shape, out_shape, square, square,
            place_of, token_wide, spare, keys, scores,
        ],
        (fields, land_ids, gain_a, table_a, qkv_weight_a, out_weight_a, place, sort, where),
        hbm=(0, 1, 2, 3, 4, 5, 6, 7, 8), copies=9, flops=7 * 10**9,
    )
    diagonal = permute_both(p0, -1)
    below = permute(p1, "lat", lambda i: i - 1)
    eastern = permute(p2, "lon", lambda i: i - 1)
    c0, c1, c2, c3, upstream_a, normed_a_t, query_b, keys_b = call(
        kernel_cotangent,
        [piece] * 4 + [token, normed_t, query, keys],
        [grid, token_wide, spare],
        (cotangent, place, sort, normed_a, land_ids, table_b, where),
        smem=(5,), hbm=(0,), copies=1, flops=2 * 10**9,
    )
    c_diagonal = permute_both(c0, -1)
    c_below = permute(c1, "lat", lambda i: i - 1)
    c_eastern = permute(c2, "lon", lambda i: i - 1)
    b0, b1, b2, b3, inputs_b, normed_b, packed_b, probs_b, mixed_b = call(
        kernel_forward_b,
        [piece] * 4 + [token] * 2 + [packed, probs, mixed_t],
        [scores],
        (p3, eastern, below, diagonal, query_b, keys_b, gain_b, qkv_weight_b, out_weight_b, sort, sort_t),
        flops=5 * 10**9,
    )
    twin = ((2, PIECE, WIDTH), BF16)
    d0, d1, d2, d3, upstream_b, d_packed_b = call(
        kernel_backward_b,
        [twin] * 4 + [token, packed],
        [scores, probs],
        (
            c3, c_eastern, c_below, c_diagonal, b0, b1, b2, b3, inputs_b, gain_b, qkv_weight_b,
            out_weight_b, packed_b, probs_b, mixed_b, sort, sort_t,
        ),
        flops=5 * 10**9,
    )
    d3 = permute_both(d3, 1)
    d2 = permute(d2, "lat", lambda i: i + 1)
    d1 = permute(d1, "lon", lambda i: i + 1)
    send_b, keep_b = call(
        kernel_grads_b, [half_grads] * 2, [normed_t], (normed_b, mixed_b, upstream_b, d_packed_b),
        flops=2 * 10**9,
    )
    send_one_b, send_two_b, keep_one_b, keep_two_b = quarters(
        kernel_first_sum_b, keep_b, to_core(send_b)
    )
    parts_b = (keep_one_b, to_x(send_one_b, 1), keep_two_b, to_x(send_two_b, 3))
    send_one_b, send_two_b, held_one_b, held_two_b = second_sum(parts_b)
    parts_b = (held_one_b, to_x(send_one_b, 3), held_two_b, to_x(send_two_b, 1))
    grad_middle, d_packed_a, send_a = call(
        kernel_backward_a,
        [token, packed, half_grads],
        [scores, probs],
        (
            d3, d2, d1, d0, upstream_a, out_weight_a, packed_a, probs_a, mixed_a, normed_a_t,
            sort_t,
        ),
        flops=5 * 10**9,
    )
    got_a = to_core(send_a)
    keep_a = call(
        kernel_keep_a, [half_grads], [], (normed_a_t, mixed_a, grad_middle, d_packed_a),
        flops=10**9,
    )[0]
    send_one_a, send_two_a, keep_one_a, keep_two_a = quarters(kernel_first_sum_a, keep_a, got_a)
    send_one_a, send_two_a, d_packed_a = lax.optimization_barrier((send_one_a, send_two_a, d_packed_a))
    parts_a = (keep_one_a, to_y(send_one_a, 1), keep_two_a, to_y(send_two_a, 3))
    grad_fields = call(
        kernel_finish_a,
        [grid],
        [qkv_shape],
        (inputs_a, grad_middle, gain_a, qkv_weight_a, d_packed_a, place_t),
        hbm=(3,), copies=1, flops=4 * 10**9, final=(0,),
    )[0]
    pair = ((2, 32, SIDE), BF16)
    send_b, keep_b = call(kernel_third_sum_b, [pair] * 2, [], parts_b)
    got_b = to_y(send_b, 1)
    send_one_a, send_two_a, held_one_a, held_two_a = second_sum(parts_a)
    send_one_a, send_two_a, grad_fields = lax.optimization_barrier(
        (send_one_a, send_two_a, grad_fields)
    )
    parts_a = (held_one_a, to_y(send_one_a, 3), held_two_a, to_y(send_two_a, 1))
    send_a, keep_a = call(kernel_third_sum_a, [pair] * 2, [], parts_a)
    got_a = to_x(send_a, 1)
    send_b, keep_b = halve(keep_b, got_b)
    got_b = to_y(send_b, 3)
    send_a, keep_a = halve(keep_a, got_a)
    send_a, middle_a = lax.optimization_barrier((send_a, middle_a))
    got_a = to_x(send_a, 3)
    advanced = call(
        kernel_advanced, [grid], [], (d3, d2, d1, d0, middle_a, place_t, sort_t),
        flops=2 * 10**9, final=(0,),
    )[0]
    got_a, got_b, advanced = lax.optimization_barrier((got_a, got_b, advanced))
    four = ((4, 64, GROUP), BF16)
    send, keep = call(
        kernel_columns, [four] * 2, [((8, 64, GROUP), BF16)], (keep_a, got_a, keep_b, got_b)
    )
    parts = exchange_z(call(kernel_sum, [four], [], (keep, to_z(send)))[0])
    grads = call(
        kernel_total,
        [((32, 96), F32), ((32, 32), F32)] * 2,
        [],
        (parts,),
        final=(0, 1, 2, 3),
    )
    return (advanced.transpose(2, 0, 1, 3), grad_fields.transpose(2, 0, 1, 3), *grads)


def solution(mesh):
    grid = P(None, "lat", "lon", None)
    return jax.shard_map(
        body,
        mesh=mesh,
        in_specs=(grid, grid) + (P(),) * 9,
        out_specs=(grid, grid) + (P("lat", "lon"),) * 4,
        check_vma=False,
    )
```

```python
import jax
import jax.numpy as jnp
import numpy as np
from jax import lax
from jax.experimental import pallas as pl
from jax.experimental.pallas import tpu as pltpu
from jax.sharding import PartitionSpec as P

WINDOWS = 2
LENGTH = 144
QUARTER = 36
TOKENS = WINDOWS * LENGTH
PIECE = WINDOWS * QUARTER
WIDTH = 512
HEADS = 16
HEAD = 32
GROUP = 128
GROUPS = WIDTH // GROUP
PER_GROUP = GROUP // HEAD
ROOT = HEAD**0.5
SIDE = 2 * WIDTH
EPS = 1e-05
NEG = -1000000000.0
VMEM_LIMIT = 24 * 1024 * 1024
F32 = jnp.float32
BF16 = jnp.bfloat16


def _tables():
    place = np.zeros((TOKENS, TOKENS), np.float32)
    sort = np.zeros((TOKENS, TOKENS), np.float32)
    where = np.zeros((LENGTH, 8), np.int32)
    for window in range(WINDOWS):
        for quadrant in range(4):
            for level in range(2):
                for row in range(6):
                    for column in range(3):
                        inner = level * 18 + row * 3 + column
                        at = quadrant * QUARTER + inner
                        token = window * LENGTH + at
                        lat = quadrant // 2 * 6 + row
                        lon = quadrant % 2 * 3 + column
                        source = (lat * 6 + lon) * 4 + 2 * window + level
                        place[token, source] = 1
                        sort[quadrant * PIECE + window * QUARTER + inner, token] = 1
                        where[at, 0] = lat
                        where[at, 1] = lon
    return place, sort, where


PLACE, SORT, WHERE = _tables()


def mm(left, right):
    return jnp.dot(left, right, preferred_element_type=F32)


def mm_t(left, right):
    return lax.dot_general(left, right, (((1,), (1,)), ((), ())), preferred_element_type=F32)


def normalise(inputs):
    centre = inputs - jnp.mean(inputs, axis=-1, keepdims=True)
    spread = jnp.mean(centre * centre, axis=-1, keepdims=True)
    scale = lax.rsqrt(spread + EPS)
    return centre * scale, scale


def lanes(shape):
    return lax.broadcasted_iota(jnp.int32, shape, 1)


def head_masks():
    lane = lanes((1, GROUP))
    return [
        ((lane >= h * HEAD) & (lane < (h + 1) * HEAD)).astype(F32).astype(BF16)
        for h in range(PER_GROUP)
    ]


def bias_features(ids_ref, where_ref, table_ref, spare_ref, shift, last):
    lat_at = lax.axis_index("lat")
    lon_at = lax.axis_index("lon")
    rows, columns = ids_ref.shape
    row = where_ref[:, 0:1]
    column = where_ref[:, 1:2] + (lon_at * 6 + shift // 2)
    at = row + (lat_at * 12 + shift)
    at = jnp.where(at >= rows, at - rows, at)
    column = jnp.where(column >= columns, column - columns, column)
    pick = (lanes((LENGTH, rows)) == at).astype(F32).astype(BF16)
    found = mm(pick, ids_ref[...].astype(F32).astype(BF16))
    found = jnp.where(lanes((LENGTH, columns)) == column, found, 0.0)
    kind = jnp.sum(found, axis=1, keepdims=True).astype(jnp.int32)
    lane = lanes((LENGTH, GROUP))
    third = (lane >= 3).astype(jnp.int32) + (lane >= 6).astype(jnp.int32)
    query = ((lane < 9) & (third == kind)).astype(F32)
    key = ((lane < 3) & (lane == kind)).astype(F32)
    if last:
        flag = ((row >= 6) & (lat_at == lax.axis_size("lat") - 1)).astype(F32)
        query = jnp.where(lane == 9, flag, jnp.where(lane == 10, 1.0 - flag, query))
        key = jnp.where(lane == 3, 1.0 - flag, jnp.where(lane == 4, flag, key))
    small = (16, GROUP)
    lane = lanes(small)
    sub = lax.broadcasted_iota(jnp.int32, small, 0)
    third = (lane >= 3).astype(jnp.int32) + (lane >= 6).astype(jnp.int32)
    part = lane - 3 * third
    spots = {
        (first, second): (lane < 9) & (third == first) & (sub == second)
        for first in range(3)
        for second in range(3)
    }
    fixed = jnp.where(((sub == 3) & (lane == 9)) | ((sub == 4) & (lane == 10)), NEG * ROOT, 0.0)
    for head in range(HEADS):
        entry = fixed
        for (first, second), spot in spots.items():
            entry = jnp.where(spot, table_ref[first, second, head] * ROOT, entry)
        high = entry.astype(BF16).astype(F32)
        middle = (entry - high).astype(BF16).astype(F32)
        low = entry - high - middle
        entry = jnp.where(part == 0, high, jnp.where(part == 1, middle, low))
        entry = jnp.where(lane >= 9, high, entry)
        spare_ref[:, head * GROUP : (head + 1) * GROUP] = entry.astype(BF16)
    features = mm(key.astype(BF16)[:, :16], spare_ref[...])
    return query.astype(BF16), features.astype(BF16)


def forward_core(
    inputs, gain, qkv_ref, out_ref, query_features, key_ref, packed_ref, probs_ref, mixed_t_ref, scores_ref
):
    hat, _ = normalise(inputs)
    normed = (hat * gain).astype(BF16)
    packed_ref[...] = mm(normed, qkv_ref[...]).astype(BF16)
    masks = head_masks()
    factor = F32(1.0 / ROOT * np.log2(np.e))
    for window, group, rows, at in sections():
        query = packed_ref[rows, at : at + GROUP]
        keys = packed_ref[rows, WIDTH + at : WIDTH + at + GROUP]
        for h in range(PER_GROUP):
            head = group * PER_GROUP + h
            left = jnp.concatenate([keys, key_ref[:, head * GROUP : (head + 1) * GROUP]], axis=1)
            right = jnp.concatenate([query * masks[h], query_features], axis=1)
            scores_ref[window * HEADS + head] = mm_t(left, right)
    for item in range(WINDOWS * HEADS):
        scores = scores_ref[item]
        top = jnp.max(scores, axis=0, keepdims=True)
        raised = jnp.exp2((scores - top) * factor)
        total = jnp.sum(raised, axis=0, keepdims=True)
        probs_ref[item] = (raised * (1.0 / total)).astype(BF16)
    for window, group, rows, at in sections():
        values_t = packed_ref[rows, 2 * WIDTH + at : 2 * WIDTH + at + GROUP].T
        for h in range(PER_GROUP):
            head = group * PER_GROUP + h
            mixed = mm(values_t[h * HEAD : (h + 1) * HEAD], probs_ref[window * HEADS + head])
            mixed_t_ref[window, head * HEAD : (head + 1) * HEAD, :] = mixed.astype(BF16)
    parts = [mm(mixed_t_ref[window].T, out_ref[...]) for window in range(WINDOWS)]
    return normed, jnp.concatenate(parts, axis=0)


def sections():
    for window in range(WINDOWS):
        for group in range(GROUPS):
            rows = slice(window * LENGTH, (window + 1) * LENGTH)
            yield window, group, rows, group * GROUP


def backward_core(
    upstream, out_ref, packed_ref, probs_ref, mixed_t_ref, d_packed_ref, d_probs_ref, d_scores_ref
):
    masks = head_masks()
    d_mixed = mm_t(upstream, out_ref[...]).astype(BF16)
    for window, group, rows, at in sections():
        values = packed_ref[rows, 2 * WIDTH + at : 2 * WIDTH + at + GROUP]
        up = d_mixed[rows, at : at + GROUP]
        for h in range(PER_GROUP):
            d_probs_ref[window * HEADS + group * PER_GROUP + h] = mm_t(values, up * masks[h])
    for window in range(WINDOWS):
        here = upstream[window * LENGTH : (window + 1) * LENGTH]
        d_mixed_t = mm_t(out_ref[...], here).astype(BF16)
        dots = d_mixed_t.astype(F32) * mixed_t_ref[window].astype(F32)
        for head in range(HEADS):
            item = window * HEADS + head
            inner = jnp.sum(dots[head * HEAD : (head + 1) * HEAD], axis=0, keepdims=True)
            d_scores = (d_probs_ref[item] - inner) * F32(1.0 / ROOT)
            d_scores_ref[item] = (probs_ref[item].astype(F32) * d_scores).astype(BF16)
    for window, group, rows, at in sections():
        query = packed_ref[rows, at : at + GROUP]
        keys_t = packed_ref[rows, WIDTH + at : WIDTH + at + GROUP].T
        up = d_mixed[rows, at : at + GROUP]
        d_values = None
        d_keys = None
        d_query = []
        for h in range(PER_GROUP):
            item = window * HEADS + group * PER_GROUP + h
            d_value = mm(probs_ref[item], up * masks[h])
            d_key = mm(d_scores_ref[item], query * masks[h])
            d_values = d_value if d_values is None else d_values + d_value
            d_keys = d_key if d_keys is None else d_keys + d_key
            d_query.append(mm(keys_t[h * HEAD : (h + 1) * HEAD], d_scores_ref[item]))
        d_query = jnp.concatenate(d_query, axis=0).T
        d_packed_ref[rows, at : at + GROUP] = d_query.astype(BF16)
        d_packed_ref[rows, WIDTH + at : WIDTH + at + GROUP] = d_keys.astype(BF16)
        d_packed_ref[rows, 2 * WIDTH + at : 2 * WIDTH + at + GROUP] = d_values.astype(BF16)


def norm_backward(inputs, gain, d_packed, qkv_ref):
    d_normed = mm_t(d_packed, qkv_ref[...]).astype(BF16).astype(F32)
    hat, scale = normalise(inputs)
    d_hat = d_normed * gain
    mean = jnp.mean(d_hat, axis=-1, keepdims=True)
    along = jnp.mean(d_hat * hat, axis=-1, keepdims=True)
    return scale * (d_hat - mean - hat * along)


def grads_half(half, normed_t_ref, mixed_t_ref, upstream, d_packed_ref, result_ref):
    def blocks(ref, *first):
        return [
            ref[(*first, pl.ds(pl.multiple_of((2 * block + half) * 32, 32), 32), slice(None))]
            for block in range(8)
        ]

    left = jnp.concatenate(blocks(normed_t_ref), axis=0)
    qkv = mm(left, d_packed_ref[...]).astype(BF16)
    total = None
    for window in range(WINDOWS):
        left = jnp.concatenate(blocks(mixed_t_ref, window), axis=0)
        part = mm(left, upstream[window * LENGTH : (window + 1) * LENGTH])
        total = part if total is None else total + part
    total = total.astype(BF16)
    result_ref[:, :768] = qkv[:, :768]
    result_ref[:, 768:SIDE] = total[:, :256]
    result_ref[:, SIDE : SIDE + 768] = qkv[:, 768:]
    result_ref[:, SIDE + 768 :] = total[:, 256:]


def load_grid(ref, place, spare_ref):
    for row in range(12):
        for column in range(6):
            at = (row * 6 + column) * 4
            spare_ref[at : at + 4, :] = ref[row, column].astype(F32)
    return mm(place, spare_ref[...].astype(BF16))


def store_grid(ref, place_t, tokens):
    spread = mm(place_t, tokens)
    for row in range(12):
        for column in range(6):
            at = (row * 6 + column) * 4
            ref[row, column] = spread[at : at + 4].astype(BF16)


def split_pieces(sort, tokens, refs):
    tokens = mm(sort, tokens)
    for at, ref in enumerate(refs):
        ref[...] = tokens[at * PIECE : (at + 1) * PIECE].astype(BF16)


def join_pieces(sort_t, pieces):
    tokens = jnp.concatenate([piece.astype(F32) for piece in pieces], axis=0)
    return mm(sort_t, tokens.astype(BF16))


def fetch(pairs, sems):
    copies = [
        pltpu.make_async_copy(source, target, sems.at[at])
        for at, (source, target) in enumerate(pairs)
    ]
    for copy in copies:
        copy.start()
    return copies


def kernel_forward_a(
    fields_hbm, ids_hbm, gain_hbm, table_hbm, qkv_hbm, out_hbm, place_hbm, sort_hbm, where_hbm,
    piece0, piece1, piece2, piece3, inputs_out, middle_out, normed_out, packed, probs, mixed_t,
    fields, ids, gain, table, qkv, out, place, sort, where, grid, spare, key_features, scores, sems,
):
    *early, qkv_in, out_in, sort_in = fetch(
        (
            (ids_hbm, ids), (where_hbm, where), (table_hbm, table), (fields_hbm, fields),
            (place_hbm, place), (gain_hbm, gain), (qkv_hbm, qkv), (out_hbm, out), (sort_hbm, sort),
        ),
        sems,
    )
    for copy in early:
        copy.wait()
    query_features, features = bias_features(ids, where, table, spare, 0, False)
    key_features[...] = features
    inputs = load_grid(fields, place[...], grid)
    inputs_out[...] = inputs.astype(BF16)
    qkv_in.wait()
    out_in.wait()
    normed, delta = forward_core(
        inputs, gain[...].reshape(1, WIDTH), qkv, out, query_features, key_features,
        packed, probs, mixed_t, scores,
    )
    normed_out[...] = normed
    middle = (inputs + delta).astype(BF16)
    middle_out[...] = middle
    sort_in.wait()
    split_pieces(sort[...], middle, (piece0, piece1, piece2, piece3))


def kernel_cotangent(
    cotangent_hbm, place, sort, normed, ids, table, where,
    piece0, piece1, piece2, piece3, upstream_out, normed_t, query_out, key_out,
    cotangent, grid, spare, sems,
):
    (cotangent_in,) = fetch(((cotangent_hbm, cotangent),), sems)
    normed_t[...] = normed[...].T
    query, keys = bias_features(ids, where, table, spare, 6, True)
    query_out[...] = query
    key_out[...] = keys
    cotangent_in.wait()
    upstream = load_grid(cotangent, place[...], grid).astype(BF16)
    upstream_out[...] = upstream
    split_pieces(sort[...], upstream, (piece0, piece1, piece2, piece3))


def kernel_forward_b(
    piece0, piece1, piece2, piece3, query_features, key_features, gain, qkv, out, sort, sort_t,
    back0, back1, back2, back3, inputs_out, normed_out, packed, probs, mixed_t,
    scores,
):
    inputs = join_pieces(sort_t[...], [ref[...] for ref in (piece0, piece1, piece2, piece3)])
    inputs_out[...] = inputs.astype(BF16)
    normed, delta = forward_core(
        inputs, gain[...].reshape(1, WIDTH), qkv, out, query_features[...], key_features,
        packed, probs, mixed_t, scores,
    )
    normed_out[...] = normed
    split_pieces(sort[...], delta.astype(BF16), (back0, back1, back2, back3))


def kernel_backward_b(
    piece0, piece1, piece2, piece3, delta0, delta1, delta2, delta3,
    inputs, gain, qkv, out, packed, probs, mixed_t, sort, sort_t,
    back0, back1, back2, back3, upstream_out, d_packed,
    d_probs, d_scores,
):
    pieces = [ref[...] for ref in (piece0, piece1, piece2, piece3)]
    upstream = join_pieces(sort_t[...], pieces).astype(BF16)
    upstream_out[...] = upstream
    backward_core(upstream, out, packed, probs, mixed_t, d_packed, d_probs, d_scores)
    d_inputs = norm_backward(
        inputs[...].astype(F32), gain[...].reshape(1, WIDTH), d_packed[...], qkv
    )
    backs = (back0, back1, back2, back3)
    split_pieces(sort[...], d_inputs.astype(BF16), [back.at[0] for back in backs])
    for back, delta in zip(backs, (delta0, delta1, delta2, delta3), strict=True):
        back[1] = delta[...]


def kernel_grads_b(normed, mixed_t, upstream, d_packed, send, keep, normed_t):
    normed_t[...] = normed[...].T
    core = lax.axis_index("lat") % 2
    grads_half(1 - core, normed_t, mixed_t, upstream[...], d_packed, send)
    grads_half(core, normed_t, mixed_t, upstream[...], d_packed, keep)


def kernel_backward_a(
    back0, back1, back2, back3, upstream, out, packed, probs, mixed_t, normed_t, sort_t,
    grad_middle_out, d_packed, send,
    d_probs, d_scores,
):
    d_inputs = join_pieces(sort_t[...], [back[0] for back in (back0, back1, back2, back3)])
    grad_middle = (upstream[...].astype(F32) + d_inputs).astype(BF16)
    grad_middle_out[...] = grad_middle
    backward_core(grad_middle, out, packed, probs, mixed_t, d_packed, d_probs, d_scores)
    core = lax.axis_index("lat") % 2
    grads_half(1 - core, normed_t, mixed_t, grad_middle, d_packed, send)


def kernel_keep_a(normed_t, mixed_t, grad_middle, d_packed, keep):
    core = lax.axis_index("lat") % 2
    grads_half(core, normed_t, mixed_t, grad_middle[...], d_packed, keep)


def kernel_advanced(back0, back1, back2, back3, middle, place_t, sort_t, advanced):
    delta = join_pieces(sort_t[...], [back[1] for back in (back0, back1, back2, back3)])
    store_grid(advanced, place_t[...], (middle[...].astype(F32) + delta).astype(BF16))


def kernel_finish_a(
    inputs, grad_middle, gain, qkv_hbm, d_packed, place_t, grad_fields, qkv, sems
):
    (qkv_in,) = fetch(((qkv_hbm, qkv),), sems)
    qkv_in.wait()
    d_inputs = norm_backward(
        inputs[...].astype(F32), gain[...].reshape(1, WIDTH), d_packed[...], qkv
    )
    total = (grad_middle[...].astype(F32) + d_inputs).astype(BF16)
    store_grid(grad_fields, place_t[...], total)


def rows_of(block, count):
    return pl.ds(pl.multiple_of(block * count, count), count)


def place_x():
    return lax.axis_index("lon") // 8 * 2 + lax.axis_index("lat") // 2 % 2


def place_y():
    return lax.axis_index("lat") // 4


def kernel_first_sum_a(keep, got, send_one, send_two, keep_one, keep_two):
    y = place_y()
    for side, first, send, kept in ((0, 1, send_one, keep_one), (1, 3, send_two, keep_two)):
        columns = slice(side * SIDE, (side + 1) * SIDE)
        for target, place, block in (
            (send, 0, y ^ first), (send, 1, y ^ 2), (kept, 0, y), (kept, 1, y ^ 2 ^ first)
        ):
            rows = rows_of(block, 64)
            target[place] = keep[rows, columns] + got[rows, columns]


def kernel_first_sum_b(keep, got, send_one, send_two, keep_one, keep_two):
    x = place_x()
    for part, first, send, kept in ((0, 1, send_one, keep_one), (1, 3, send_two, keep_two)):
        for target, place, block in (
            (send, 0, x ^ first), (send, 1, x ^ 2), (kept, 0, x), (kept, 1, x ^ 2 ^ first)
        ):
            columns = rows_of(block // 2, SIDE)
            for inner in range(2):
                rows = rows_of((part * 2 + inner) * 2 + block % 2, 32)
                target[place, inner * 32 : (inner + 1) * 32] = keep[rows, columns] + got[rows, columns]


def kernel_second_sum(keep_one, got_one, keep_two, got_two, send_one, send_two, held_one, held_two):
    send_one[...] = keep_one[1] + got_one[1]
    send_two[...] = keep_two[1] + got_two[1]
    held_one[...] = keep_one[0] + got_one[0]
    held_two[...] = keep_two[0] + got_two[0]


def third_sum(at, halves, send, keep):
    for target, place, block in ((send, 0, at ^ 1), (send, 1, at ^ 2), (keep, 0, at), (keep, 1, at ^ 3)):
        rows = rows_of(block % 2, 32)
        for half, (held, got) in enumerate(halves):

            @pl.when(block // 2 == half)
            def _(target=target, place=place, rows=rows, held=held, got=got):
                target[place] = held[rows, :] + got[rows, :]


def kernel_third_sum_a(held_one, got_one, held_two, got_two, send, keep):
    third_sum(place_x(), ((held_one, got_one), (held_two, got_two)), send, keep)


def kernel_third_sum_b(held_one, got_one, held_two, got_two, send, keep):
    third_sum(place_y(), ((held_one, got_one), (held_two, got_two)), send, keep)


def kernel_halve(keep, got, send, held):
    half = keep.shape[0] // 2
    held[...] = keep[:half] + got[:half]
    send[...] = keep[half:] + got[half:]


def kernel_columns(keep_a, got_a, keep_b, got_b, blocks):
    for rows, held, got in ((slice(0, 32), keep_a, got_a), (slice(32, 64), keep_b, got_b)):
        total = held[0].astype(F32) + got[0].astype(F32)
        for block in range(8):
            qkv = total[:, block * 96 : (block + 1) * 96]
            out = total[:, 768 + block * 32 : 768 + (block + 1) * 32]
            blocks[block, rows] = jnp.concatenate([qkv, out], axis=1).astype(BF16)


def kernel_total(parts, qkv_a, out_a, qkv_b, out_b):
    total = parts[0].astype(F32)
    for at in range(1, 8):
        total = total + parts[at].astype(F32)
    for rows, qkv, out in ((slice(0, 32), qkv_a, out_a), (slice(32, 64), qkv_b, out_b)):
        qkv[...] = total[rows, :96]
        out[...] = total[rows, 96:]


def call(kernel, outs, scratch, args, smem=(), hbm=(), copies=0, flops=0, final=()):
    def space(at):
        return pltpu.SMEM if at in smem else pltpu.HBM if at in hbm else pltpu.VMEM

    cost = pl.CostEstimate(flops=flops, bytes_accessed=1 << 20, transcendentals=0) if flops else None
    args = [
        pltpu.with_memory_space_constraint(arg, pltpu.HBM) if at in hbm or at in smem else arg
        for at, arg in enumerate(args)
    ]
    shapes = [pltpu.VMEM(*item) if isinstance(item, tuple) else item for item in scratch]
    if copies:
        shapes.append(pltpu.SemaphoreType.DMA((copies,)))
    return pl.pallas_call(
        kernel,
        out_shape=tuple(
            jax.ShapeDtypeStruct(shape, kind) if at in final else pltpu.VMEM(shape, kind)
            for at, (shape, kind) in enumerate(outs)
        ),
        in_specs=[pl.BlockSpec(memory_space=space(at)) for at in range(len(args))],
        out_specs=tuple(pl.BlockSpec(memory_space=pltpu.VMEM) for _ in outs),
        scratch_shapes=shapes,
        cost_estimate=cost,
        compiler_params=pltpu.CompilerParams(vmem_limit_bytes=VMEM_LIMIT),
    )(*args)


def permute(array, axis, target):
    length = lax.axis_size(axis)
    return lax.ppermute(array, axis, [(i, target(i) % length) for i in range(length)])


def permute_both(array, by):
    lons, lats = lax.axis_size("lon"), lax.axis_size("lat")
    pairs = [
        (lon * lats + lat, (lon + by) % lons * lats + (lat + by) % lats)
        for lon in range(lons)
        for lat in range(lats)
    ]
    return lax.ppermute(array, ("lon", "lat"), pairs)


def to_core(array):
    return permute(array, "lat", lambda i: i ^ 1)


def to_y(array, by):
    return permute(array, "lat", lambda i: i ^ (4 * by))


def to_x(array, by):
    if by == 1:
        return permute(array, "lat", lambda i: i ^ 2)
    lons, lats = lax.axis_size("lon"), lax.axis_size("lat")
    pairs = [
        (lon * lats + lat, (lon ^ 8) * lats + (lat ^ 2)) for lon in range(lons) for lat in range(lats)
    ]
    return lax.ppermute(array, ("lon", "lat"), pairs)


def quarters(kernel, keep, got):
    return call(kernel, [((2, 64, SIDE), BF16)] * 4, [], (keep, got))


def second_sum(parts):
    return call(kernel_second_sum, [((64, SIDE), BF16)] * 4, [], parts)


def halve(keep, got):
    shape = (keep.shape[0] // 2,) + keep.shape[1:]
    return call(kernel_halve, [(shape, BF16)] * 2, [], (keep, got))


def exchange_z(messages):
    groups = [[x_hi * 8 + z for z in range(8)] for x_hi in range(2)]
    return lax.all_to_all(messages, "lon", 0, 0, axis_index_groups=groups, tiled=True)


def body(
    fields, cotangent, land_ids, gain_a, table_a, qkv_weight_a, out_weight_a,
    gain_b, table_b, qkv_weight_b, out_weight_b,
):
    place = jnp.asarray(PLACE, BF16)
    place_t = jnp.asarray(PLACE.T, BF16)
    sort = jnp.asarray(SORT, BF16)
    sort_t = jnp.asarray(SORT.T, BF16)
    where = jnp.asarray(WHERE)
    fields = fields.transpose(1, 2, 0, 3)
    cotangent = cotangent.transpose(1, 2, 0, 3)
    table_a = table_a.transpose(1, 2, 0)
    table_b = table_b.transpose(1, 2, 0)
    grid = (fields.shape, BF16)
    piece = ((PIECE, WIDTH), BF16)
    token = ((TOKENS, WIDTH), BF16)
    token_wide = ((TOKENS, WIDTH), F32)
    packed = ((TOKENS, 3 * WIDTH), BF16)
    probs = ((WINDOWS * HEADS, LENGTH, LENGTH), BF16)
    scores = ((WINDOWS * HEADS, LENGTH, LENGTH), F32)
    mixed_t = ((WINDOWS, WIDTH, LENGTH), BF16)
    half_grads = ((WIDTH // 2, 4 * WIDTH), BF16)
    normed_t = ((WIDTH, TOKENS), BF16)
    square = ((TOKENS, TOKENS), BF16)
    spare = ((16, HEADS * GROUP), BF16)
    query = ((LENGTH, GROUP), BF16)
    keys = ((LENGTH, HEADS * GROUP), BF16)
    ids = (land_ids.shape, jnp.int32)
    place_of = (where.shape, jnp.int32)
    vector = ((WIDTH,), F32)
    qkv_shape = ((WIDTH, 3 * WIDTH), BF16)
    out_shape = ((WIDTH, WIDTH), BF16)

    p0, p1, p2, p3, inputs_a, middle_a, normed_a, packed_a, probs_a, mixed_a = call(
        kernel_forward_a,
        [piece] * 4 + [token] * 3 + [packed, probs, mixed_t],
        [
            grid, ids, vector, pltpu.SMEM(table_a.shape, F32), qkv_shape, out_shape, square, square,
            place_of, token_wide, spare, keys, scores,
        ],
        (fields, land_ids, gain_a, table_a, qkv_weight_a, out_weight_a, place, sort, where),
        hbm=(0, 1, 2, 3, 4, 5, 6, 7, 8), copies=9, flops=7 * 10**9,
    )
    diagonal = permute_both(p0, -1)
    below = permute(p1, "lat", lambda i: i - 1)
    eastern = permute(p2, "lon", lambda i: i - 1)
    c0, c1, c2, c3, upstream_a, normed_a_t, query_b, keys_b = call(
        kernel_cotangent,
        [piece] * 4 + [token, normed_t, query, keys],
        [grid, token_wide, spare],
        (cotangent, place, sort, normed_a, land_ids, table_b, where),
        smem=(5,), hbm=(0,), copies=1, flops=2 * 10**9,
    )
    c_diagonal = permute_both(c0, -1)
    c_below = permute(c1, "lat", lambda i: i - 1)
    c_eastern = permute(c2, "lon", lambda i: i - 1)
    b0, b1, b2, b3, inputs_b, normed_b, packed_b, probs_b, mixed_b = call(
        kernel_forward_b,
        [piece] * 4 + [token] * 2 + [packed, probs, mixed_t],
        [scores],
        (p3, eastern, below, diagonal, query_b, keys_b, gain_b, qkv_weight_b, out_weight_b, sort, sort_t),
        flops=5 * 10**9,
    )
    twin = ((2, PIECE, WIDTH), BF16)
    d0, d1, d2, d3, upstream_b, d_packed_b = call(
        kernel_backward_b,
        [twin] * 4 + [token, packed],
        [scores, probs],
        (
            c3, c_eastern, c_below, c_diagonal, b0, b1, b2, b3, inputs_b, gain_b, qkv_weight_b,
            out_weight_b, packed_b, probs_b, mixed_b, sort, sort_t,
        ),
        flops=5 * 10**9,
    )
    d3 = permute_both(d3, 1)
    d2 = permute(d2, "lat", lambda i: i + 1)
    d1 = permute(d1, "lon", lambda i: i + 1)
    send_b, keep_b = call(
        kernel_grads_b, [half_grads] * 2, [normed_t], (normed_b, mixed_b, upstream_b, d_packed_b),
        flops=2 * 10**9,
    )
    send_one_b, send_two_b, keep_one_b, keep_two_b = quarters(
        kernel_first_sum_b, keep_b, to_core(send_b)
    )
    parts_b = (keep_one_b, to_x(send_one_b, 1), keep_two_b, to_x(send_two_b, 3))
    send_one_b, send_two_b, held_one_b, held_two_b = second_sum(parts_b)
    parts_b = (held_one_b, to_x(send_one_b, 3), held_two_b, to_x(send_two_b, 1))
    grad_middle, d_packed_a, send_a = call(
        kernel_backward_a,
        [token, packed, half_grads],
        [scores, probs],
        (
            d3, d2, d1, d0, upstream_a, out_weight_a, packed_a, probs_a, mixed_a, normed_a_t,
            sort_t,
        ),
        flops=5 * 10**9,
    )
    got_a = to_core(send_a)
    keep_a = call(
        kernel_keep_a, [half_grads], [], (normed_a_t, mixed_a, grad_middle, d_packed_a),
        flops=10**9,
    )[0]
    send_one_a, send_two_a, keep_one_a, keep_two_a = quarters(kernel_first_sum_a, keep_a, got_a)
    parts_a = (keep_one_a, to_y(send_one_a, 1), keep_two_a, to_y(send_two_a, 3))
    pair = ((2, 32, SIDE), BF16)
    send_b, keep_b = call(kernel_third_sum_b, [pair] * 2, [], parts_b)
    got_b = to_y(send_b, 1)
    send_one_a, send_two_a, held_one_a, held_two_a = second_sum(parts_a)
    parts_a = (held_one_a, to_y(send_one_a, 3), held_two_a, to_y(send_two_a, 1))
    send_a, keep_a = call(kernel_third_sum_a, [pair] * 2, [], parts_a)
    got_a = to_x(send_a, 1)
    send_b, keep_b = halve(keep_b, got_b)
    got_b = to_y(send_b, 3)
    send_a, keep_a = halve(keep_a, got_a)
    got_a = to_x(send_a, 3)
    blocks = call(
        kernel_columns, [((8, 64, GROUP), BF16)], [], (keep_a, got_a, keep_b, got_b)
    )[0]
    blocks, d_packed_a, middle_a = lax.optimization_barrier((blocks, d_packed_a, middle_a))
    parts = exchange_z(blocks)
    advanced = call(
        kernel_advanced, [grid], [], (d3, d2, d1, d0, middle_a, place_t, sort_t),
        flops=2 * 10**9, final=(0,),
    )[0]
    grad_fields = call(
        kernel_finish_a,
        [grid],
        [qkv_shape],
        (inputs_a, grad_middle, gain_a, qkv_weight_a, d_packed_a, place_t),
        hbm=(3,), copies=1, flops=4 * 10**9, final=(0,),
    )[0]
    grads = call(
        kernel_total,
        [((32, 96), F32), ((32, 32), F32)] * 2,
        [],
        (parts,),
        final=(0, 1, 2, 3),
    )
    return (advanced.transpose(2, 0, 1, 3), grad_fields.transpose(2, 0, 1, 3), *grads)


def solution(mesh):
    grid = P(None, "lat", "lon", None)
    return jax.shard_map(
        body,
        mesh=mesh,
        in_specs=(grid, grid) + (P(),) * 9,
        out_specs=(grid, grid) + (P("lat", "lon"),) * 4,
        check_vma=False,
    )
```

```python
import jax
import jax.numpy as jnp
import numpy as np
from jax import lax
from jax.experimental import pallas as pl
from jax.experimental.pallas import tpu as pltpu
from jax.sharding import PartitionSpec as P

WINDOWS = 2
LENGTH = 144
QUARTER = 36
TOKENS = WINDOWS * LENGTH
PIECE = WINDOWS * QUARTER
WIDTH = 512
HEADS = 16
HEAD = 32
GROUP = 128
GROUPS = WIDTH // GROUP
PER_GROUP = GROUP // HEAD
ROOT = HEAD**0.5
SIDE = 2 * WIDTH
EPS = 1e-05
NEG = -1000000000.0
VMEM_LIMIT = 24 * 1024 * 1024
F32 = jnp.float32
BF16 = jnp.bfloat16


def _tables():
    place = np.zeros((TOKENS, TOKENS), np.float32)
    sort = np.zeros((TOKENS, TOKENS), np.float32)
    where = np.zeros((LENGTH, 8), np.int32)
    for window in range(WINDOWS):
        for quadrant in range(4):
            for level in range(2):
                for row in range(6):
                    for column in range(3):
                        inner = level * 18 + row * 3 + column
                        at = quadrant * QUARTER + inner
                        token = window * LENGTH + at
                        lat = quadrant // 2 * 6 + row
                        lon = quadrant % 2 * 3 + column
                        source = (lat * 6 + lon) * 4 + 2 * window + level
                        place[token, source] = 1
                        sort[quadrant * PIECE + window * QUARTER + inner, token] = 1
                        where[at, 0] = lat
                        where[at, 1] = lon
    return place, sort, where


PLACE, SORT, WHERE = _tables()


def mm(left, right):
    return jnp.dot(left, right, preferred_element_type=F32)


def mm_t(left, right):
    return lax.dot_general(left, right, (((1,), (1,)), ((), ())), preferred_element_type=F32)


def normalise(inputs):
    centre = inputs - jnp.mean(inputs, axis=-1, keepdims=True)
    spread = jnp.mean(centre * centre, axis=-1, keepdims=True)
    scale = lax.rsqrt(spread + EPS)
    return centre * scale, scale


def lanes(shape):
    return lax.broadcasted_iota(jnp.int32, shape, 1)


def head_masks():
    lane = lanes((1, GROUP))
    return [
        ((lane >= h * HEAD) & (lane < (h + 1) * HEAD)).astype(F32).astype(BF16)
        for h in range(PER_GROUP)
    ]


def bias_features(ids_ref, where_ref, table_ref, spare_ref, shift, last):
    lat_at = lax.axis_index("lat")
    lon_at = lax.axis_index("lon")
    rows, columns = ids_ref.shape
    row = where_ref[:, 0:1]
    column = where_ref[:, 1:2] + (lon_at * 6 + shift // 2)
    at = row + (lat_at * 12 + shift)
    at = jnp.where(at >= rows, at - rows, at)
    column = jnp.where(column >= columns, column - columns, column)
    pick = (lanes((LENGTH, rows)) == at).astype(F32).astype(BF16)
    found = mm(pick, ids_ref[...].astype(F32).astype(BF16))
    found = jnp.where(lanes((LENGTH, columns)) == column, found, 0.0)
    kind = jnp.sum(found, axis=1, keepdims=True).astype(jnp.int32)
    lane = lanes((LENGTH, GROUP))
    third = (lane >= 3).astype(jnp.int32) + (lane >= 6).astype(jnp.int32)
    query = ((lane < 9) & (third == kind)).astype(F32)
    key = ((lane < 3) & (lane == kind)).astype(F32)
    if last:
        flag = ((row >= 6) & (lat_at == lax.axis_size("lat") - 1)).astype(F32)
        query = jnp.where(lane == 9, flag, jnp.where(lane == 10, 1.0 - flag, query))
        key = jnp.where(lane == 3, 1.0 - flag, jnp.where(lane == 4, flag, key))
    small = (16, GROUP)
    lane = lanes(small)
    sub = lax.broadcasted_iota(jnp.int32, small, 0)
    third = (lane >= 3).astype(jnp.int32) + (lane >= 6).astype(jnp.int32)
    part = lane - 3 * third
    spots = {
        (first, second): (lane < 9) & (third == first) & (sub == second)
        for first in range(3)
        for second in range(3)
    }
    fixed = jnp.where(((sub == 3) & (lane == 9)) | ((sub == 4) & (lane == 10)), NEG * ROOT, 0.0)
    for head in range(HEADS):
        entry = fixed
        for (first, second), spot in spots.items():
            entry = jnp.where(spot, table_ref[first, second, head] * ROOT, entry)
        high = entry.astype(BF16).astype(F32)
        middle = (entry - high).astype(BF16).astype(F32)
        low = entry - high - middle
        entry = jnp.where(part == 0, high, jnp.where(part == 1, middle, low))
        entry = jnp.where(lane >= 9, high, entry)
        spare_ref[:, head * GROUP : (head + 1) * GROUP] = entry.astype(BF16)
    features = mm(key.astype(BF16)[:, :16], spare_ref[...])
    return query.astype(BF16), features.astype(BF16)


def forward_core(
    inputs, gain, qkv_ref, out_ref, query_features, key_ref, packed_ref, probs_ref, mixed_t_ref, scores_ref
):
    hat, _ = normalise(inputs)
    normed = (hat * gain).astype(BF16)
    packed_ref[...] = mm(normed, qkv_ref[...]).astype(BF16)
    masks = head_masks()
    factor = F32(1.0 / ROOT * np.log2(np.e))
    for window, group, rows, at in sections():
        query = packed_ref[rows, at : at + GROUP]
        keys = packed_ref[rows, WIDTH + at : WIDTH + at + GROUP]
        for h in range(PER_GROUP):
            head = group * PER_GROUP + h
            left = jnp.concatenate([keys, key_ref[:, head * GROUP : (head + 1) * GROUP]], axis=1)
            right = jnp.concatenate([query * masks[h], query_features], axis=1)
            scores_ref[window * HEADS + head] = mm_t(left, right)
    for item in range(WINDOWS * HEADS):
        scores = scores_ref[item]
        top = jnp.max(scores, axis=0, keepdims=True)
        raised = jnp.exp2((scores - top) * factor)
        total = jnp.sum(raised, axis=0, keepdims=True)
        probs_ref[item] = (raised * (1.0 / total)).astype(BF16)
    for window, group, rows, at in sections():
        values_t = packed_ref[rows, 2 * WIDTH + at : 2 * WIDTH + at + GROUP].T
        for h in range(PER_GROUP):
            head = group * PER_GROUP + h
            mixed = mm(values_t[h * HEAD : (h + 1) * HEAD], probs_ref[window * HEADS + head])
            mixed_t_ref[window, head * HEAD : (head + 1) * HEAD, :] = mixed.astype(BF16)
    parts = [mm(mixed_t_ref[window].T, out_ref[...]) for window in range(WINDOWS)]
    return normed, jnp.concatenate(parts, axis=0)


def sections():
    for window in range(WINDOWS):
        for group in range(GROUPS):
            rows = slice(window * LENGTH, (window + 1) * LENGTH)
            yield window, group, rows, group * GROUP


def backward_core(
    upstream, out_ref, packed_ref, probs_ref, mixed_t_ref, d_packed_ref, d_probs_ref, d_scores_ref
):
    masks = head_masks()
    d_mixed = mm_t(upstream, out_ref[...]).astype(BF16)
    for window, group, rows, at in sections():
        values = packed_ref[rows, 2 * WIDTH + at : 2 * WIDTH + at + GROUP]
        up = d_mixed[rows, at : at + GROUP]
        for h in range(PER_GROUP):
            d_probs_ref[window * HEADS + group * PER_GROUP + h] = mm_t(values, up * masks[h])
    for window in range(WINDOWS):
        here = upstream[window * LENGTH : (window + 1) * LENGTH]
        d_mixed_t = mm_t(out_ref[...], here).astype(BF16)
        dots = d_mixed_t.astype(F32) * mixed_t_ref[window].astype(F32)
        for head in range(HEADS):
            item = window * HEADS + head
            inner = jnp.sum(dots[head * HEAD : (head + 1) * HEAD], axis=0, keepdims=True)
            d_scores = (d_probs_ref[item] - inner) * F32(1.0 / ROOT)
            d_scores_ref[item] = (probs_ref[item].astype(F32) * d_scores).astype(BF16)
    for window, group, rows, at in sections():
        query = packed_ref[rows, at : at + GROUP]
        keys_t = packed_ref[rows, WIDTH + at : WIDTH + at + GROUP].T
        up = d_mixed[rows, at : at + GROUP]
        d_values = None
        d_keys = None
        d_query = []
        for h in range(PER_GROUP):
            item = window * HEADS + group * PER_GROUP + h
            d_value = mm(probs_ref[item], up * masks[h])
            d_key = mm(d_scores_ref[item], query * masks[h])
            d_values = d_value if d_values is None else d_values + d_value
            d_keys = d_key if d_keys is None else d_keys + d_key
            d_query.append(mm(keys_t[h * HEAD : (h + 1) * HEAD], d_scores_ref[item]))
        d_query = jnp.concatenate(d_query, axis=0).T
        d_packed_ref[rows, at : at + GROUP] = d_query.astype(BF16)
        d_packed_ref[rows, WIDTH + at : WIDTH + at + GROUP] = d_keys.astype(BF16)
        d_packed_ref[rows, 2 * WIDTH + at : 2 * WIDTH + at + GROUP] = d_values.astype(BF16)


def norm_backward(inputs, gain, d_packed, qkv_ref):
    d_normed = mm_t(d_packed, qkv_ref[...]).astype(BF16).astype(F32)
    hat, scale = normalise(inputs)
    d_hat = d_normed * gain
    mean = jnp.mean(d_hat, axis=-1, keepdims=True)
    along = jnp.mean(d_hat * hat, axis=-1, keepdims=True)
    return scale * (d_hat - mean - hat * along)


def grads_half(half, normed_t_ref, mixed_t_ref, upstream, d_packed_ref, result_ref):
    def blocks(ref, *first):
        return [
            ref[(*first, pl.ds(pl.multiple_of((2 * block + half) * 32, 32), 32), slice(None))]
            for block in range(8)
        ]

    left = jnp.concatenate(blocks(normed_t_ref), axis=0)
    qkv = mm(left, d_packed_ref[...]).astype(BF16)
    total = None
    for window in range(WINDOWS):
        left = jnp.concatenate(blocks(mixed_t_ref, window), axis=0)
        part = mm(left, upstream[window * LENGTH : (window + 1) * LENGTH])
        total = part if total is None else total + part
    total = total.astype(BF16)
    result_ref[:, :768] = qkv[:, :768]
    result_ref[:, 768:SIDE] = total[:, :256]
    result_ref[:, SIDE : SIDE + 768] = qkv[:, 768:]
    result_ref[:, SIDE + 768 :] = total[:, 256:]


def load_grid(ref, place, spare_ref):
    for row in range(12):
        for column in range(6):
            at = (row * 6 + column) * 4
            spare_ref[at : at + 4, :] = ref[row, column].astype(F32)
    return mm(place, spare_ref[...].astype(BF16))


def store_grid(ref, place_t, tokens):
    spread = mm(place_t, tokens)
    for row in range(12):
        for column in range(6):
            at = (row * 6 + column) * 4
            ref[row, column] = spread[at : at + 4].astype(BF16)


def split_pieces(sort, tokens, refs):
    tokens = mm(sort, tokens)
    for at, ref in enumerate(refs):
        ref[...] = tokens[at * PIECE : (at + 1) * PIECE].astype(BF16)


def join_pieces(sort_t, pieces):
    tokens = jnp.concatenate([piece.astype(F32) for piece in pieces], axis=0)
    return mm(sort_t, tokens.astype(BF16))


def fetch(pairs, sems):
    copies = [
        pltpu.make_async_copy(source, target, sems.at[at])
        for at, (source, target) in enumerate(pairs)
    ]
    for copy in copies:
        copy.start()
    return copies


def kernel_forward_a(
    fields_hbm, ids_hbm, gain_hbm, table_hbm, qkv_hbm, out_hbm, place_hbm, sort_hbm, where_hbm,
    piece0, piece1, piece2, piece3, inputs_out, middle_out, normed_out, packed, probs, mixed_t,
    fields, ids, gain, table, qkv, out, place, sort, where, grid, spare, key_features, scores, sems,
):
    *early, qkv_in, out_in, sort_in = fetch(
        (
            (ids_hbm, ids), (where_hbm, where), (table_hbm, table), (fields_hbm, fields),
            (place_hbm, place), (gain_hbm, gain), (qkv_hbm, qkv), (out_hbm, out), (sort_hbm, sort),
        ),
        sems,
    )
    for copy in early:
        copy.wait()
    query_features, features = bias_features(ids, where, table, spare, 0, False)
    key_features[...] = features
    inputs = load_grid(fields, place[...], grid)
    inputs_out[...] = inputs.astype(BF16)
    qkv_in.wait()
    out_in.wait()
    normed, delta = forward_core(
        inputs, gain[...].reshape(1, WIDTH), qkv, out, query_features, key_features,
        packed, probs, mixed_t, scores,
    )
    normed_out[...] = normed
    middle = (inputs + delta).astype(BF16)
    middle_out[...] = middle
    sort_in.wait()
    split_pieces(sort[...], middle, (piece0, piece1, piece2, piece3))


def kernel_cotangent(
    cotangent_hbm, place, sort, normed, ids, table, where,
    piece0, piece1, piece2, piece3, upstream_out, normed_t, query_out, key_out,
    cotangent, grid, spare, sems,
):
    (cotangent_in,) = fetch(((cotangent_hbm, cotangent),), sems)
    normed_t[...] = normed[...].T
    query, keys = bias_features(ids, where, table, spare, 6, True)
    query_out[...] = query
    key_out[...] = keys
    cotangent_in.wait()
    upstream = load_grid(cotangent, place[...], grid).astype(BF16)
    upstream_out[...] = upstream
    split_pieces(sort[...], upstream, (piece0, piece1, piece2, piece3))


def kernel_forward_b(
    piece0, piece1, piece2, piece3, query_features, key_features, gain, qkv, out, sort, sort_t,
    back0, back1, back2, back3, inputs_out, normed_out, packed, probs, mixed_t,
    scores,
):
    inputs = join_pieces(sort_t[...], [ref[...] for ref in (piece0, piece1, piece2, piece3)])
    inputs_out[...] = inputs.astype(BF16)
    normed, delta = forward_core(
        inputs, gain[...].reshape(1, WIDTH), qkv, out, query_features[...], key_features,
        packed, probs, mixed_t, scores,
    )
    normed_out[...] = normed
    split_pieces(sort[...], delta.astype(BF16), (back0, back1, back2, back3))


def kernel_backward_b(
    piece0, piece1, piece2, piece3, inputs, gain, qkv, out, packed, probs, mixed_t, sort, sort_t,
    back0, back1, back2, back3, upstream_out, d_packed,
    d_probs, d_scores,
):
    pieces = [ref[...] for ref in (piece0, piece1, piece2, piece3)]
    upstream = join_pieces(sort_t[...], pieces).astype(BF16)
    upstream_out[...] = upstream
    backward_core(upstream, out, packed, probs, mixed_t, d_packed, d_probs, d_scores)
    d_inputs = norm_backward(
        inputs[...].astype(F32), gain[...].reshape(1, WIDTH), d_packed[...], qkv
    )
    split_pieces(sort[...], d_inputs.astype(BF16), (back0, back1, back2, back3))


def kernel_grads_b(normed, mixed_t, upstream, d_packed, send, keep, normed_t):
    normed_t[...] = normed[...].T
    core = lax.axis_index("lat") % 2
    grads_half(1 - core, normed_t, mixed_t, upstream[...], d_packed, send)
    grads_half(core, normed_t, mixed_t, upstream[...], d_packed, keep)


def kernel_backward_a(
    back0, back1, back2, back3, upstream, out, packed, probs, mixed_t, normed_t, sort_t,
    grad_middle_out, d_packed, send,
    d_probs, d_scores,
):
    d_inputs = join_pieces(sort_t[...], [ref[...] for ref in (back0, back1, back2, back3)])
    grad_middle = (upstream[...].astype(F32) + d_inputs).astype(BF16)
    grad_middle_out[...] = grad_middle
    backward_core(grad_middle, out, packed, probs, mixed_t, d_packed, d_probs, d_scores)
    core = lax.axis_index("lat") % 2
    grads_half(1 - core, normed_t, mixed_t, grad_middle, d_packed, send)


def kernel_keep_a(normed_t, mixed_t, grad_middle, d_packed, keep):
    core = lax.axis_index("lat") % 2
    grads_half(core, normed_t, mixed_t, grad_middle[...], d_packed, keep)


def kernel_advanced(back0, back1, back2, back3, middle, place_t, sort_t, advanced):
    delta = join_pieces(sort_t[...], [ref[...] for ref in (back0, back1, back2, back3)])
    store_grid(advanced, place_t[...], (middle[...].astype(F32) + delta).astype(BF16))


def kernel_finish_a(
    inputs, grad_middle, gain, qkv_hbm, d_packed, place_t, grad_fields, qkv, sems
):
    (qkv_in,) = fetch(((qkv_hbm, qkv),), sems)
    qkv_in.wait()
    d_inputs = norm_backward(
        inputs[...].astype(F32), gain[...].reshape(1, WIDTH), d_packed[...], qkv
    )
    total = (grad_middle[...].astype(F32) + d_inputs).astype(BF16)
    store_grid(grad_fields, place_t[...], total)


def rows_of(block, count):
    return pl.ds(pl.multiple_of(block * count, count), count)


def place_x():
    return lax.axis_index("lon") // 8 * 2 + lax.axis_index("lat") // 2 % 2


def place_y():
    return lax.axis_index("lat") // 4


def kernel_first_sum_a(keep, got, send_one, send_two, keep_one, keep_two):
    y = place_y()
    for side, first, send, kept in ((0, 1, send_one, keep_one), (1, 3, send_two, keep_two)):
        columns = slice(side * SIDE, (side + 1) * SIDE)
        for target, place, block in (
            (send, 0, y ^ first), (send, 1, y ^ 2), (kept, 0, y), (kept, 1, y ^ 2 ^ first)
        ):
            rows = rows_of(block, 64)
            target[place] = keep[rows, columns] + got[rows, columns]


def kernel_first_sum_b(keep, got, send_one, send_two, keep_one, keep_two):
    x = place_x()
    for part, first, send, kept in ((0, 1, send_one, keep_one), (1, 3, send_two, keep_two)):
        for target, place, block in (
            (send, 0, x ^ first), (send, 1, x ^ 2), (kept, 0, x), (kept, 1, x ^ 2 ^ first)
        ):
            columns = rows_of(block // 2, SIDE)
            for inner in range(2):
                rows = rows_of((part * 2 + inner) * 2 + block % 2, 32)
                target[place, inner * 32 : (inner + 1) * 32] = keep[rows, columns] + got[rows, columns]


def kernel_second_sum(keep_one, got_one, keep_two, got_two, send_one, send_two, held_one, held_two):
    send_one[...] = keep_one[1] + got_one[1]
    send_two[...] = keep_two[1] + got_two[1]
    held_one[...] = keep_one[0] + got_one[0]
    held_two[...] = keep_two[0] + got_two[0]


def third_sum(at, halves, send, keep):
    for target, place, block in ((send, 0, at ^ 1), (send, 1, at ^ 2), (keep, 0, at), (keep, 1, at ^ 3)):
        rows = rows_of(block % 2, 32)
        for half, (held, got) in enumerate(halves):

            @pl.when(block // 2 == half)
            def _(target=target, place=place, rows=rows, held=held, got=got):
                target[place] = held[rows, :] + got[rows, :]


def kernel_third_sum_a(held_one, got_one, held_two, got_two, send, keep):
    third_sum(place_x(), ((held_one, got_one), (held_two, got_two)), send, keep)


def kernel_third_sum_b(held_one, got_one, held_two, got_two, send, keep):
    third_sum(place_y(), ((held_one, got_one), (held_two, got_two)), send, keep)


def kernel_halve(keep, got, send, held):
    half = keep.shape[0] // 2
    held[...] = keep[:half] + got[:half]
    send[...] = keep[half:] + got[half:]


def kernel_columns(keep_a, got_a, keep_b, got_b, blocks):
    for rows, held, got in ((slice(0, 32), keep_a, got_a), (slice(32, 64), keep_b, got_b)):
        total = held[0].astype(F32) + got[0].astype(F32)
        for block in range(8):
            qkv = total[:, block * 96 : (block + 1) * 96]
            out = total[:, 768 + block * 32 : 768 + (block + 1) * 32]
            blocks[block, rows] = jnp.concatenate([qkv, out], axis=1).astype(BF16)


def kernel_total(parts, qkv_a, out_a, qkv_b, out_b):
    total = parts[0].astype(F32)
    for at in range(1, 8):
        total = total + parts[at].astype(F32)
    for rows, qkv, out in ((slice(0, 32), qkv_a, out_a), (slice(32, 64), qkv_b, out_b)):
        qkv[...] = total[rows, :96]
        out[...] = total[rows, 96:]


def call(kernel, outs, scratch, args, smem=(), hbm=(), copies=0, flops=0, final=()):
    def space(at):
        return pltpu.SMEM if at in smem else pltpu.HBM if at in hbm else pltpu.VMEM

    cost = pl.CostEstimate(flops=flops, bytes_accessed=1 << 20, transcendentals=0) if flops else None
    args = [
        pltpu.with_memory_space_constraint(arg, pltpu.HBM) if at in hbm or at in smem else arg
        for at, arg in enumerate(args)
    ]
    shapes = [pltpu.VMEM(*item) if isinstance(item, tuple) else item for item in scratch]
    if copies:
        shapes.append(pltpu.SemaphoreType.DMA((copies,)))
    return pl.pallas_call(
        kernel,
        out_shape=tuple(
            jax.ShapeDtypeStruct(shape, kind) if at in final else pltpu.VMEM(shape, kind)
            for at, (shape, kind) in enumerate(outs)
        ),
        in_specs=[pl.BlockSpec(memory_space=space(at)) for at in range(len(args))],
        out_specs=tuple(pl.BlockSpec(memory_space=pltpu.VMEM) for _ in outs),
        scratch_shapes=shapes,
        cost_estimate=cost,
        compiler_params=pltpu.CompilerParams(vmem_limit_bytes=VMEM_LIMIT),
    )(*args)


def permute(array, axis, target):
    length = lax.axis_size(axis)
    return lax.ppermute(array, axis, [(i, target(i) % length) for i in range(length)])


def permute_both(array, by):
    lons, lats = lax.axis_size("lon"), lax.axis_size("lat")
    pairs = [
        (lon * lats + lat, (lon + by) % lons * lats + (lat + by) % lats)
        for lon in range(lons)
        for lat in range(lats)
    ]
    return lax.ppermute(array, ("lon", "lat"), pairs)


def to_core(array):
    return permute(array, "lat", lambda i: i ^ 1)


def to_y(array, by):
    return permute(array, "lat", lambda i: i ^ (4 * by))


def to_x(array, by):
    if by == 1:
        return permute(array, "lat", lambda i: i ^ 2)
    lons, lats = lax.axis_size("lon"), lax.axis_size("lat")
    pairs = [
        (lon * lats + lat, (lon ^ 8) * lats + (lat ^ 2)) for lon in range(lons) for lat in range(lats)
    ]
    return lax.ppermute(array, ("lon", "lat"), pairs)


def quarters(kernel, keep, got):
    return call(kernel, [((2, 64, SIDE), BF16)] * 4, [], (keep, got))


def second_sum(parts):
    return call(kernel_second_sum, [((64, SIDE), BF16)] * 4, [], parts)


def halve(keep, got):
    shape = (keep.shape[0] // 2,) + keep.shape[1:]
    return call(kernel_halve, [(shape, BF16)] * 2, [], (keep, got))


def exchange_z(messages):
    groups = [[x_hi * 8 + z for z in range(8)] for x_hi in range(2)]
    return lax.all_to_all(messages, "lon", 0, 0, axis_index_groups=groups, tiled=True)


def body(
    fields, cotangent, land_ids, gain_a, table_a, qkv_weight_a, out_weight_a,
    gain_b, table_b, qkv_weight_b, out_weight_b,
):
    place = jnp.asarray(PLACE, BF16)
    place_t = jnp.asarray(PLACE.T, BF16)
    sort = jnp.asarray(SORT, BF16)
    sort_t = jnp.asarray(SORT.T, BF16)
    where = jnp.asarray(WHERE)
    fields = fields.transpose(1, 2, 0, 3)
    cotangent = cotangent.transpose(1, 2, 0, 3)
    table_a = table_a.transpose(1, 2, 0)
    table_b = table_b.transpose(1, 2, 0)
    grid = (fields.shape, BF16)
    piece = ((PIECE, WIDTH), BF16)
    token = ((TOKENS, WIDTH), BF16)
    token_wide = ((TOKENS, WIDTH), F32)
    packed = ((TOKENS, 3 * WIDTH), BF16)
    probs = ((WINDOWS * HEADS, LENGTH, LENGTH), BF16)
    scores = ((WINDOWS * HEADS, LENGTH, LENGTH), F32)
    mixed_t = ((WINDOWS, WIDTH, LENGTH), BF16)
    half_grads = ((WIDTH // 2, 4 * WIDTH), BF16)
    normed_t = ((WIDTH, TOKENS), BF16)
    square = ((TOKENS, TOKENS), BF16)
    spare = ((16, HEADS * GROUP), BF16)
    query = ((LENGTH, GROUP), BF16)
    keys = ((LENGTH, HEADS * GROUP), BF16)
    ids = (land_ids.shape, jnp.int32)
    place_of = (where.shape, jnp.int32)
    vector = ((WIDTH,), F32)
    qkv_shape = ((WIDTH, 3 * WIDTH), BF16)
    out_shape = ((WIDTH, WIDTH), BF16)

    p0, p1, p2, p3, inputs_a, middle_a, normed_a, packed_a, probs_a, mixed_a = call(
        kernel_forward_a,
        [piece] * 4 + [token] * 3 + [packed, probs, mixed_t],
        [
            grid, ids, vector, pltpu.SMEM(table_a.shape, F32), qkv_shape, out_shape, square, square,
            place_of, token_wide, spare, keys, scores,
        ],
        (fields, land_ids, gain_a, table_a, qkv_weight_a, out_weight_a, place, sort, where),
        hbm=(0, 1, 2, 3, 4, 5, 6, 7, 8), copies=9, flops=7 * 10**9,
    )
    diagonal = permute_both(p0, -1)
    below = permute(p1, "lat", lambda i: i - 1)
    eastern = permute(p2, "lon", lambda i: i - 1)
    c0, c1, c2, c3, upstream_a, normed_a_t, query_b, keys_b = call(
        kernel_cotangent,
        [piece] * 4 + [token, normed_t, query, keys],
        [grid, token_wide, spare],
        (cotangent, place, sort, normed_a, land_ids, table_b, where),
        smem=(5,), hbm=(0,), copies=1, flops=2 * 10**9,
    )
    c_diagonal = permute_both(c0, -1)
    c_below = permute(c1, "lat", lambda i: i - 1)
    c_eastern = permute(c2, "lon", lambda i: i - 1)
    b0, b1, b2, b3, inputs_b, normed_b, packed_b, probs_b, mixed_b = call(
        kernel_forward_b,
        [piece] * 4 + [token] * 2 + [packed, probs, mixed_t],
        [scores],
        (p3, eastern, below, diagonal, query_b, keys_b, gain_b, qkv_weight_b, out_weight_b, sort, sort_t),
        flops=5 * 10**9,
    )
    d0, d1, d2, d3, upstream_b, d_packed_b = call(
        kernel_backward_b,
        [piece] * 4 + [token, packed],
        [scores, probs],
        (
            c3, c_eastern, c_below, c_diagonal, inputs_b, gain_b, qkv_weight_b, out_weight_b,
            packed_b, probs_b, mixed_b, sort, sort_t,
        ),
        flops=5 * 10**9,
    )
    d3 = permute_both(d3, 1)
    d2 = permute(d2, "lat", lambda i: i + 1)
    d1 = permute(d1, "lon", lambda i: i + 1)
    send_b, keep_b = call(
        kernel_grads_b, [half_grads] * 2, [normed_t], (normed_b, mixed_b, upstream_b, d_packed_b),
        flops=2 * 10**9,
    )
    send_one_b, send_two_b, keep_one_b, keep_two_b = quarters(
        kernel_first_sum_b, keep_b, to_core(send_b)
    )
    parts_b = (keep_one_b, to_x(send_one_b, 1), keep_two_b, to_x(send_two_b, 3))
    send_one_b, send_two_b, held_one_b, held_two_b = second_sum(parts_b)
    parts_b = (held_one_b, to_x(send_one_b, 3), held_two_b, to_x(send_two_b, 1))
    grad_middle, d_packed_a, send_a = call(
        kernel_backward_a,
        [token, packed, half_grads],
        [scores, probs],
        (
            d3, d2, d1, d0, upstream_a, out_weight_a, packed_a, probs_a, mixed_a, normed_a_t,
            sort_t,
        ),
        flops=5 * 10**9,
    )
    got_a = to_core(send_a)
    keep_a = call(
        kernel_keep_a, [half_grads], [], (normed_a_t, mixed_a, grad_middle, d_packed_a),
        flops=10**9,
    )[0]
    send_one_a, send_two_a, keep_one_a, keep_two_a = quarters(kernel_first_sum_a, keep_a, got_a)
    send_one_a, send_two_a, b1, b2, b3 = lax.optimization_barrier(
        (send_one_a, send_two_a, b1, b2, b3)
    )
    b3 = permute_both(b3, 1)
    b2 = permute(b2, "lat", lambda i: i + 1)
    b1 = permute(b1, "lon", lambda i: i + 1)
    parts_a = (keep_one_a, to_y(send_one_a, 1), keep_two_a, to_y(send_two_a, 3))
    pair = ((2, 32, SIDE), BF16)
    send_b, keep_b = call(kernel_third_sum_b, [pair] * 2, [], parts_b)
    got_b = to_y(send_b, 1)
    parts_a, b1, b2, b3 = lax.optimization_barrier((parts_a, b1, b2, b3))
    send_one_a, send_two_a, held_one_a, held_two_a = second_sum(parts_a)
    parts_a = (held_one_a, to_y(send_one_a, 3), held_two_a, to_y(send_two_a, 1))
    send_a, keep_a = call(kernel_third_sum_a, [pair] * 2, [], parts_a)
    got_a = to_x(send_a, 1)
    send_b, keep_b = halve(keep_b, got_b)
    got_b = to_y(send_b, 3)
    send_a, keep_a = halve(keep_a, got_a)
    got_a = to_x(send_a, 3)
    blocks = call(
        kernel_columns, [((8, 64, GROUP), BF16)], [], (keep_a, got_a, keep_b, got_b)
    )[0]
    blocks, d_packed_a, middle_a = lax.optimization_barrier((blocks, d_packed_a, middle_a))
    parts = exchange_z(blocks)
    advanced = call(
        kernel_advanced, [grid], [], (b3, b2, b1, b0, middle_a, place_t, sort_t),
        flops=2 * 10**9, final=(0,),
    )[0]
    grad_fields = call(
        kernel_finish_a,
        [grid],
        [qkv_shape],
        (inputs_a, grad_middle, gain_a, qkv_weight_a, d_packed_a, place_t),
        hbm=(3,), copies=1, flops=4 * 10**9, final=(0,),
    )[0]
    grads = call(
        kernel_total,
        [((32, 96), F32), ((32, 32), F32)] * 2,
        [],
        (parts,),
        final=(0, 1, 2, 3),
    )
    return (advanced.transpose(2, 0, 1, 3), grad_fields.transpose(2, 0, 1, 3), *grads)


def solution(mesh):
    grid = P(None, "lat", "lon", None)
    return jax.shard_map(
        body,
        mesh=mesh,
        in_specs=(grid, grid) + (P(),) * 9,
        out_specs=(grid, grid) + (P("lat", "lon"),) * 4,
        check_vma=False,
    )
```

```python
import jax
import jax.numpy as jnp
import numpy as np
from jax import lax
from jax.experimental import pallas as pl
from jax.experimental.pallas import tpu as pltpu
from jax.sharding import PartitionSpec as P

WINDOWS = 2
LENGTH = 144
QUARTER = 36
TOKENS = WINDOWS * LENGTH
PIECE = WINDOWS * QUARTER
WIDTH = 512
HEADS = 16
HEAD = 32
GROUP = 128
GROUPS = WIDTH // GROUP
PER_GROUP = GROUP // HEAD
ROOT = HEAD**0.5
SIDE = 2 * WIDTH
EPS = 1e-05
NEG = -1000000000.0
VMEM_LIMIT = 24 * 1024 * 1024
F32 = jnp.float32
BF16 = jnp.bfloat16


def _tables():
    place = np.zeros((TOKENS, TOKENS), np.float32)
    sort = np.zeros((TOKENS, TOKENS), np.float32)
    where = np.zeros((LENGTH, 8), np.int32)
    for window in range(WINDOWS):
        for quadrant in range(4):
            for level in range(2):
                for row in range(6):
                    for column in range(3):
                        inner = level * 18 + row * 3 + column
                        at = quadrant * QUARTER + inner
                        token = window * LENGTH + at
                        lat = quadrant // 2 * 6 + row
                        lon = quadrant % 2 * 3 + column
                        source = (lat * 6 + lon) * 4 + 2 * window + level
                        place[token, source] = 1
                        sort[quadrant * PIECE + window * QUARTER + inner, token] = 1
                        where[at, 0] = lat
                        where[at, 1] = lon
    return place, sort, where


PLACE, SORT, WHERE = _tables()


def mm(left, right):
    return jnp.dot(left, right, preferred_element_type=F32)


def mm_t(left, right):
    return lax.dot_general(left, right, (((1,), (1,)), ((), ())), preferred_element_type=F32)


def normalise(inputs):
    centre = inputs - jnp.mean(inputs, axis=-1, keepdims=True)
    spread = jnp.mean(centre * centre, axis=-1, keepdims=True)
    scale = lax.rsqrt(spread + EPS)
    return centre * scale, scale


def lanes(shape):
    return lax.broadcasted_iota(jnp.int32, shape, 1)


def head_masks():
    lane = lanes((1, GROUP))
    return [
        ((lane >= h * HEAD) & (lane < (h + 1) * HEAD)).astype(F32).astype(BF16)
        for h in range(PER_GROUP)
    ]


def bias_features(ids_ref, where_ref, table_ref, spare_ref, shift, last):
    lat_at = lax.axis_index("lat")
    lon_at = lax.axis_index("lon")
    rows, columns = ids_ref.shape
    row = where_ref[:, 0:1]
    column = where_ref[:, 1:2] + (lon_at * 6 + shift // 2)
    at = row + (lat_at * 12 + shift)
    at = jnp.where(at >= rows, at - rows, at)
    column = jnp.where(column >= columns, column - columns, column)
    pick = (lanes((LENGTH, rows)) == at).astype(F32).astype(BF16)
    found = mm(pick, ids_ref[...].astype(F32).astype(BF16))
    found = jnp.where(lanes((LENGTH, columns)) == column, found, 0.0)
    kind = jnp.sum(found, axis=1, keepdims=True).astype(jnp.int32)
    lane = lanes((LENGTH, GROUP))
    third = (lane >= 3).astype(jnp.int32) + (lane >= 6).astype(jnp.int32)
    query = ((lane < 9) & (third == kind)).astype(F32)
    key = ((lane < 3) & (lane == kind)).astype(F32)
    if last:
        flag = ((row >= 6) & (lat_at == lax.axis_size("lat") - 1)).astype(F32)
        query = jnp.where(lane == 9, flag, jnp.where(lane == 10, 1.0 - flag, query))
        key = jnp.where(lane == 3, 1.0 - flag, jnp.where(lane == 4, flag, key))
    small = (16, GROUP)
    lane = lanes(small)
    sub = lax.broadcasted_iota(jnp.int32, small, 0)
    third = (lane >= 3).astype(jnp.int32) + (lane >= 6).astype(jnp.int32)
    part = lane - 3 * third
    spots = {
        (first, second): (lane < 9) & (third == first) & (sub == second)
        for first in range(3)
        for second in range(3)
    }
    fixed = jnp.where(((sub == 3) & (lane == 9)) | ((sub == 4) & (lane == 10)), NEG * ROOT, 0.0)
    for head in range(HEADS):
        entry = fixed
        for (first, second), spot in spots.items():
            entry = jnp.where(spot, table_ref[first, second, head] * ROOT, entry)
        high = entry.astype(BF16).astype(F32)
        middle = (entry - high).astype(BF16).astype(F32)
        low = entry - high - middle
        entry = jnp.where(part == 0, high, jnp.where(part == 1, middle, low))
        entry = jnp.where(lane >= 9, high, entry)
        spare_ref[:, head * GROUP : (head + 1) * GROUP] = entry.astype(BF16)
    features = mm(key.astype(BF16)[:, :16], spare_ref[...])
    return query.astype(BF16), features.astype(BF16)


def forward_core(
    inputs, gain, qkv_ref, out_ref, query_features, key_ref, packed_ref, probs_ref, mixed_t_ref, scores_ref
):
    hat, _ = normalise(inputs)
    normed = (hat * gain).astype(BF16)
    packed_ref[...] = mm(normed, qkv_ref[...]).astype(BF16)
    masks = head_masks()
    factor = F32(1.0 / ROOT * np.log2(np.e))
    for window, group, rows, at in sections():
        query = packed_ref[rows, at : at + GROUP]
        keys = packed_ref[rows, WIDTH + at : WIDTH + at + GROUP]
        for h in range(PER_GROUP):
            head = group * PER_GROUP + h
            left = jnp.concatenate([keys, key_ref[:, head * GROUP : (head + 1) * GROUP]], axis=1)
            right = jnp.concatenate([query * masks[h], query_features], axis=1)
            scores_ref[window * HEADS + head] = mm_t(left, right)
    for item in range(WINDOWS * HEADS):
        scores = scores_ref[item]
        top = jnp.max(scores, axis=0, keepdims=True)
        raised = jnp.exp2((scores - top) * factor)
        total = jnp.sum(raised, axis=0, keepdims=True)
        probs_ref[item] = (raised * (1.0 / total)).astype(BF16)
    for window, group, rows, at in sections():
        values_t = packed_ref[rows, 2 * WIDTH + at : 2 * WIDTH + at + GROUP].T
        for h in range(PER_GROUP):
            head = group * PER_GROUP + h
            mixed = mm(values_t[h * HEAD : (h + 1) * HEAD], probs_ref[window * HEADS + head])
            mixed_t_ref[window, head * HEAD : (head + 1) * HEAD, :] = mixed.astype(BF16)
    parts = [mm(mixed_t_ref[window].T, out_ref[...]) for window in range(WINDOWS)]
    return normed, jnp.concatenate(parts, axis=0)


def sections():
    for window in range(WINDOWS):
        for group in range(GROUPS):
            rows = slice(window * LENGTH, (window + 1) * LENGTH)
            yield window, group, rows, group * GROUP


def backward_core(
    upstream, out_ref, packed_ref, probs_ref, mixed_t_ref, d_packed_ref, d_probs_ref, d_scores_ref
):
    masks = head_masks()
    d_mixed = mm_t(upstream, out_ref[...]).astype(BF16)
    for window, group, rows, at in sections():
        values = packed_ref[rows, 2 * WIDTH + at : 2 * WIDTH + at + GROUP]
        up = d_mixed[rows, at : at + GROUP]
        for h in range(PER_GROUP):
            d_probs_ref[window * HEADS + group * PER_GROUP + h] = mm_t(values, up * masks[h])
    for window in range(WINDOWS):
        here = upstream[window * LENGTH : (window + 1) * LENGTH]
        d_mixed_t = mm_t(out_ref[...], here).astype(BF16)
        dots = d_mixed_t.astype(F32) * mixed_t_ref[window].astype(F32)
        for head in range(HEADS):
            item = window * HEADS + head
            inner = jnp.sum(dots[head * HEAD : (head + 1) * HEAD], axis=0, keepdims=True)
            d_scores = (d_probs_ref[item] - inner) * F32(1.0 / ROOT)
            d_scores_ref[item] = (probs_ref[item].astype(F32) * d_scores).astype(BF16)
    for window, group, rows, at in sections():
        query = packed_ref[rows, at : at + GROUP]
        keys_t = packed_ref[rows, WIDTH + at : WIDTH + at + GROUP].T
        up = d_mixed[rows, at : at + GROUP]
        d_values = None
        d_keys = None
        d_query = []
        for h in range(PER_GROUP):
            item = window * HEADS + group * PER_GROUP + h
            d_value = mm(probs_ref[item], up * masks[h])
            d_key = mm(d_scores_ref[item], query * masks[h])
            d_values = d_value if d_values is None else d_values + d_value
            d_keys = d_key if d_keys is None else d_keys + d_key
            d_query.append(mm(keys_t[h * HEAD : (h + 1) * HEAD], d_scores_ref[item]))
        d_query = jnp.concatenate(d_query, axis=0).T
        d_packed_ref[rows, at : at + GROUP] = d_query.astype(BF16)
        d_packed_ref[rows, WIDTH + at : WIDTH + at + GROUP] = d_keys.astype(BF16)
        d_packed_ref[rows, 2 * WIDTH + at : 2 * WIDTH + at + GROUP] = d_values.astype(BF16)


def norm_backward(inputs, gain, d_packed, qkv_ref):
    d_normed = mm_t(d_packed, qkv_ref[...]).astype(BF16).astype(F32)
    hat, scale = normalise(inputs)
    d_hat = d_normed * gain
    mean = jnp.mean(d_hat, axis=-1, keepdims=True)
    along = jnp.mean(d_hat * hat, axis=-1, keepdims=True)
    return scale * (d_hat - mean - hat * along)


def grads_half(half, normed_t_ref, mixed_t_ref, upstream, d_packed_ref, result_ref):
    def blocks(ref, *first):
        return [
            ref[(*first, pl.ds(pl.multiple_of((2 * block + half) * 32, 32), 32), slice(None))]
            for block in range(8)
        ]

    left = jnp.concatenate(blocks(normed_t_ref), axis=0)
    qkv = mm(left, d_packed_ref[...]).astype(BF16)
    total = None
    for window in range(WINDOWS):
        left = jnp.concatenate(blocks(mixed_t_ref, window), axis=0)
        part = mm(left, upstream[window * LENGTH : (window + 1) * LENGTH])
        total = part if total is None else total + part
    total = total.astype(BF16)
    result_ref[:, :768] = qkv[:, :768]
    result_ref[:, 768:SIDE] = total[:, :256]
    result_ref[:, SIDE : SIDE + 768] = qkv[:, 768:]
    result_ref[:, SIDE + 768 :] = total[:, 256:]


def load_grid(ref, place, spare_ref):
    for row in range(12):
        for column in range(6):
            at = (row * 6 + column) * 4
            spare_ref[at : at + 4, :] = ref[row, column].astype(F32)
    return mm(place, spare_ref[...].astype(BF16))


def store_grid(ref, place_t, tokens):
    spread = mm(place_t, tokens)
    for row in range(12):
        for column in range(6):
            at = (row * 6 + column) * 4
            ref[row, column] = spread[at : at + 4].astype(BF16)


def split_pieces(sort, tokens, refs):
    tokens = mm(sort, tokens)
    for at, ref in enumerate(refs):
        ref[...] = tokens[at * PIECE : (at + 1) * PIECE].astype(BF16)


def join_pieces(sort_t, pieces):
    tokens = jnp.concatenate([piece.astype(F32) for piece in pieces], axis=0)
    return mm(sort_t, tokens.astype(BF16))


def fetch(pairs, sems):
    copies = [
        pltpu.make_async_copy(source, target, sems.at[at])
        for at, (source, target) in enumerate(pairs)
    ]
    for copy in copies:
        copy.start()
    return copies


def kernel_forward_a(
    fields_hbm, ids_hbm, gain_hbm, table_hbm, qkv_hbm, out_hbm, place_hbm, sort_hbm, where_hbm,
    piece0, piece1, piece2, piece3, inputs_out, middle_out, normed_out, packed, probs, mixed_t,
    fields, ids, gain, table, qkv, out, place, sort, where, grid, spare, key_features, scores, sems,
):
    *early, qkv_in, out_in, sort_in = fetch(
        (
            (ids_hbm, ids), (where_hbm, where), (table_hbm, table), (fields_hbm, fields),
            (place_hbm, place), (gain_hbm, gain), (qkv_hbm, qkv), (out_hbm, out), (sort_hbm, sort),
        ),
        sems,
    )
    for copy in early:
        copy.wait()
    query_features, features = bias_features(ids, where, table, spare, 0, False)
    key_features[...] = features
    inputs = load_grid(fields, place[...], grid)
    inputs_out[...] = inputs.astype(BF16)
    qkv_in.wait()
    out_in.wait()
    normed, delta = forward_core(
        inputs, gain[...].reshape(1, WIDTH), qkv, out, query_features, key_features,
        packed, probs, mixed_t, scores,
    )
    normed_out[...] = normed
    middle = (inputs + delta).astype(BF16)
    middle_out[...] = middle
    sort_in.wait()
    split_pieces(sort[...], middle, (piece0, piece1, piece2, piece3))


def kernel_cotangent(
    cotangent_hbm, place, sort, normed, ids, table, where,
    piece0, piece1, piece2, piece3, upstream_out, normed_t, query_out, key_out,
    cotangent, grid, spare, sems,
):
    (cotangent_in,) = fetch(((cotangent_hbm, cotangent),), sems)
    normed_t[...] = normed[...].T
    query, keys = bias_features(ids, where, table, spare, 6, True)
    query_out[...] = query
    key_out[...] = keys
    cotangent_in.wait()
    upstream = load_grid(cotangent, place[...], grid).astype(BF16)
    upstream_out[...] = upstream
    split_pieces(sort[...], upstream, (piece0, piece1, piece2, piece3))


def kernel_forward_b(
    piece0, piece1, piece2, piece3, query_features, key_features, gain, qkv, out, sort, sort_t,
    back0, back1, back2, back3, inputs_out, normed_out, packed, probs, mixed_t,
    scores,
):
    inputs = join_pieces(sort_t[...], [ref[...] for ref in (piece0, piece1, piece2, piece3)])
    inputs_out[...] = inputs.astype(BF16)
    normed, delta = forward_core(
        inputs, gain[...].reshape(1, WIDTH), qkv, out, query_features[...], key_features,
        packed, probs, mixed_t, scores,
    )
    normed_out[...] = normed
    split_pieces(sort[...], delta.astype(BF16), (back0, back1, back2, back3))


def kernel_backward_b(
    piece0, piece1, piece2, piece3, delta0, delta1, delta2, delta3,
    inputs, gain, qkv, out, packed, probs, mixed_t, sort, sort_t,
    back0, back1, back2, back3, upstream_out, d_packed,
    d_probs, d_scores,
):
    pieces = [ref[...] for ref in (piece0, piece1, piece2, piece3)]
    upstream = join_pieces(sort_t[...], pieces).astype(BF16)
    upstream_out[...] = upstream
    backward_core(upstream, out, packed, probs, mixed_t, d_packed, d_probs, d_scores)
    d_inputs = norm_backward(
        inputs[...].astype(F32), gain[...].reshape(1, WIDTH), d_packed[...], qkv
    )
    backs = (back0, back1, back2, back3)
    split_pieces(sort[...], d_inputs.astype(BF16), [back.at[0] for back in backs])
    for back, delta in zip(backs, (delta0, delta1, delta2, delta3), strict=True):
        back[1] = delta[...]


def kernel_grads_b(normed, mixed_t, upstream, d_packed, send, keep, normed_t):
    normed_t[...] = normed[...].T
    core = lax.axis_index("lat") % 2
    grads_half(1 - core, normed_t, mixed_t, upstream[...], d_packed, send)
    grads_half(core, normed_t, mixed_t, upstream[...], d_packed, keep)


def kernel_backward_a(
    back0, back1, back2, back3, upstream, out, packed, probs, mixed_t, normed_t, sort_t,
    grad_middle_out, d_packed, send,
    d_probs, d_scores,
):
    d_inputs = join_pieces(sort_t[...], [back[0] for back in (back0, back1, back2, back3)])
    grad_middle = (upstream[...].astype(F32) + d_inputs).astype(BF16)
    grad_middle_out[...] = grad_middle
    backward_core(grad_middle, out, packed, probs, mixed_t, d_packed, d_probs, d_scores)
    core = lax.axis_index("lat") % 2
    grads_half(1 - core, normed_t, mixed_t, grad_middle, d_packed, send)


def kernel_keep_a(normed_t, mixed_t, grad_middle, d_packed, keep):
    core = lax.axis_index("lat") % 2
    grads_half(core, normed_t, mixed_t, grad_middle[...], d_packed, keep)


def kernel_advanced(back0, back1, back2, back3, middle, place_t, sort_t, advanced):
    delta = join_pieces(sort_t[...], [back[1] for back in (back0, back1, back2, back3)])
    store_grid(advanced, place_t[...], (middle[...].astype(F32) + delta).astype(BF16))


def kernel_finish_a(
    inputs, grad_middle, gain, qkv_hbm, d_packed, place_t, grad_fields, qkv, sems
):
    (qkv_in,) = fetch(((qkv_hbm, qkv),), sems)
    qkv_in.wait()
    d_inputs = norm_backward(
        inputs[...].astype(F32), gain[...].reshape(1, WIDTH), d_packed[...], qkv
    )
    total = (grad_middle[...].astype(F32) + d_inputs).astype(BF16)
    store_grid(grad_fields, place_t[...], total)


def rows_of(block, count):
    return pl.ds(pl.multiple_of(block * count, count), count)


def place_x():
    return lax.axis_index("lon") // 8 * 2 + lax.axis_index("lat") // 2 % 2


def place_y():
    return lax.axis_index("lat") // 4


def kernel_first_sum_a(keep, got, send_one, send_two, keep_one, keep_two):
    y = place_y()
    for side, first, send, kept in ((0, 1, send_one, keep_one), (1, 3, send_two, keep_two)):
        columns = slice(side * SIDE, (side + 1) * SIDE)
        for target, place, block in (
            (send, 0, y ^ first), (send, 1, y ^ 2), (kept, 0, y), (kept, 1, y ^ 2 ^ first)
        ):
            rows = rows_of(block, 64)
            target[place] = keep[rows, columns] + got[rows, columns]


def kernel_first_sum_b(keep, got, send_one, send_two, keep_one, keep_two):
    x = place_x()
    for part, first, send, kept in ((0, 1, send_one, keep_one), (1, 3, send_two, keep_two)):
        for target, place, block in (
            (send, 0, x ^ first), (send, 1, x ^ 2), (kept, 0, x), (kept, 1, x ^ 2 ^ first)
        ):
            columns = rows_of(block // 2, SIDE)
            for inner in range(2):
                rows = rows_of((part * 2 + inner) * 2 + block % 2, 32)
                target[place, inner * 32 : (inner + 1) * 32] = keep[rows, columns] + got[rows, columns]


def kernel_second_sum(keep_one, got_one, keep_two, got_two, send_one, send_two, held_one, held_two):
    send_one[...] = keep_one[1] + got_one[1]
    send_two[...] = keep_two[1] + got_two[1]
    held_one[...] = keep_one[0] + got_one[0]
    held_two[...] = keep_two[0] + got_two[0]


def third_sum(at, halves, send, keep):
    for target, place, block in ((send, 0, at ^ 1), (send, 1, at ^ 2), (keep, 0, at), (keep, 1, at ^ 3)):
        rows = rows_of(block % 2, 32)
        for half, (held, got) in enumerate(halves):

            @pl.when(block // 2 == half)
            def _(target=target, place=place, rows=rows, held=held, got=got):
                target[place] = held[rows, :] + got[rows, :]


def kernel_third_sum_a(held_one, got_one, held_two, got_two, send, keep):
    third_sum(place_x(), ((held_one, got_one), (held_two, got_two)), send, keep)


def kernel_third_sum_b(held_one, got_one, held_two, got_two, send, keep):
    third_sum(place_y(), ((held_one, got_one), (held_two, got_two)), send, keep)


def kernel_halve(keep, got, send, held):
    half = keep.shape[0] // 2
    held[...] = keep[:half] + got[:half]
    send[...] = keep[half:] + got[half:]


def kernel_columns(keep_a, got_a, keep_b, got_b, blocks):
    for rows, held, got in ((slice(0, 32), keep_a, got_a), (slice(32, 64), keep_b, got_b)):
        total = held[0].astype(F32) + got[0].astype(F32)
        for block in range(8):
            qkv = total[:, block * 96 : (block + 1) * 96]
            out = total[:, 768 + block * 32 : 768 + (block + 1) * 32]
            blocks[block, rows] = jnp.concatenate([qkv, out], axis=1).astype(BF16)


def kernel_total(parts, qkv_a, out_a, qkv_b, out_b):
    total = parts[0].astype(F32)
    for at in range(1, 8):
        total = total + parts[at].astype(F32)
    for rows, qkv, out in ((slice(0, 32), qkv_a, out_a), (slice(32, 64), qkv_b, out_b)):
        qkv[...] = total[rows, :96]
        out[...] = total[rows, 96:]


def call(kernel, outs, scratch, args, smem=(), hbm=(), copies=0, flops=0, final=()):
    def space(at):
        return pltpu.SMEM if at in smem else pltpu.HBM if at in hbm else pltpu.VMEM

    cost = pl.CostEstimate(flops=flops, bytes_accessed=1 << 20, transcendentals=0) if flops else None
    args = [
        pltpu.with_memory_space_constraint(arg, pltpu.HBM) if at in hbm or at in smem else arg
        for at, arg in enumerate(args)
    ]
    shapes = [pltpu.VMEM(*item) if isinstance(item, tuple) else item for item in scratch]
    if copies:
        shapes.append(pltpu.SemaphoreType.DMA((copies,)))
    return pl.pallas_call(
        kernel,
        out_shape=tuple(
            jax.ShapeDtypeStruct(shape, kind) if at in final else pltpu.VMEM(shape, kind)
            for at, (shape, kind) in enumerate(outs)
        ),
        in_specs=[pl.BlockSpec(memory_space=space(at)) for at in range(len(args))],
        out_specs=tuple(pl.BlockSpec(memory_space=pltpu.VMEM) for _ in outs),
        scratch_shapes=shapes,
        cost_estimate=cost,
        compiler_params=pltpu.CompilerParams(vmem_limit_bytes=VMEM_LIMIT),
    )(*args)


def permute(array, axis, target):
    length = lax.axis_size(axis)
    return lax.ppermute(array, axis, [(i, target(i) % length) for i in range(length)])


def permute_both(array, by):
    lons, lats = lax.axis_size("lon"), lax.axis_size("lat")
    pairs = [
        (lon * lats + lat, (lon + by) % lons * lats + (lat + by) % lats)
        for lon in range(lons)
        for lat in range(lats)
    ]
    return lax.ppermute(array, ("lon", "lat"), pairs)


def to_core(array):
    return permute(array, "lat", lambda i: i ^ 1)


def to_y(array, by):
    return permute(array, "lat", lambda i: i ^ (4 * by))


def to_x(array, by):
    if by == 1:
        return permute(array, "lat", lambda i: i ^ 2)
    lons, lats = lax.axis_size("lon"), lax.axis_size("lat")
    pairs = [
        (lon * lats + lat, (lon ^ 8) * lats + (lat ^ 2)) for lon in range(lons) for lat in range(lats)
    ]
    return lax.ppermute(array, ("lon", "lat"), pairs)


def quarters(kernel, keep, got):
    return call(kernel, [((2, 64, SIDE), BF16)] * 4, [], (keep, got))


def second_sum(parts):
    return call(kernel_second_sum, [((64, SIDE), BF16)] * 4, [], parts)


def halve(keep, got):
    shape = (keep.shape[0] // 2,) + keep.shape[1:]
    return call(kernel_halve, [(shape, BF16)] * 2, [], (keep, got))


def exchange_z(messages):
    groups = [[x_hi * 8 + z for z in range(8)] for x_hi in range(2)]
    return lax.all_to_all(messages, "lon", 0, 0, axis_index_groups=groups, tiled=True)


def body(
    fields, cotangent, land_ids, gain_a, table_a, qkv_weight_a, out_weight_a,
    gain_b, table_b, qkv_weight_b, out_weight_b,
):
    place = jnp.asarray(PLACE, BF16)
    place_t = jnp.asarray(PLACE.T, BF16)
    sort = jnp.asarray(SORT, BF16)
    sort_t = jnp.asarray(SORT.T, BF16)
    where = jnp.asarray(WHERE)
    fields = fields.transpose(1, 2, 0, 3)
    cotangent = cotangent.transpose(1, 2, 0, 3)
    table_a = table_a.transpose(1, 2, 0)
    table_b = table_b.transpose(1, 2, 0)
    grid = (fields.shape, BF16)
    piece = ((PIECE, WIDTH), BF16)
    token = ((TOKENS, WIDTH), BF16)
    token_wide = ((TOKENS, WIDTH), F32)
    packed = ((TOKENS, 3 * WIDTH), BF16)
    probs = ((WINDOWS * HEADS, LENGTH, LENGTH), BF16)
    scores = ((WINDOWS * HEADS, LENGTH, LENGTH), F32)
    mixed_t = ((WINDOWS, WIDTH, LENGTH), BF16)
    half_grads = ((WIDTH // 2, 4 * WIDTH), BF16)
    normed_t = ((WIDTH, TOKENS), BF16)
    square = ((TOKENS, TOKENS), BF16)
    spare = ((16, HEADS * GROUP), BF16)
    query = ((LENGTH, GROUP), BF16)
    keys = ((LENGTH, HEADS * GROUP), BF16)
    ids = (land_ids.shape, jnp.int32)
    place_of = (where.shape, jnp.int32)
    vector = ((WIDTH,), F32)
    qkv_shape = ((WIDTH, 3 * WIDTH), BF16)
    out_shape = ((WIDTH, WIDTH), BF16)

    p0, p1, p2, p3, inputs_a, middle_a, normed_a, packed_a, probs_a, mixed_a = call(
        kernel_forward_a,
        [piece] * 4 + [token] * 3 + [packed, probs, mixed_t],
        [
            grid, ids, vector, pltpu.SMEM(table_a.shape, F32), qkv_shape, out_shape, square, square,
            place_of, token_wide, spare, keys, scores,
        ],
        (fields, land_ids, gain_a, table_a, qkv_weight_a, out_weight_a, place, sort, where),
        hbm=(0, 1, 2, 3, 4, 5, 6, 7, 8), copies=9, flops=7 * 10**9,
    )
    diagonal = permute_both(p0, -1)
    below = permute(p1, "lat", lambda i: i - 1)
    eastern = permute(p2, "lon", lambda i: i - 1)
    c0, c1, c2, c3, upstream_a, normed_a_t, query_b, keys_b = call(
        kernel_cotangent,
        [piece] * 4 + [token, normed_t, query, keys],
        [grid, token_wide, spare],
        (cotangent, place, sort, normed_a, land_ids, table_b, where),
        smem=(5,), hbm=(0,), copies=1, flops=2 * 10**9,
    )
    c_diagonal = permute_both(c0, -1)
    c_below = permute(c1, "lat", lambda i: i - 1)
    c_eastern = permute(c2, "lon", lambda i: i - 1)
    b0, b1, b2, b3, inputs_b, normed_b, packed_b, probs_b, mixed_b = call(
        kernel_forward_b,
        [piece] * 4 + [token] * 2 + [packed, probs, mixed_t],
        [scores],
        (p3, eastern, below, diagonal, query_b, keys_b, gain_b, qkv_weight_b, out_weight_b, sort, sort_t),
        flops=5 * 10**9,
    )
    twin = ((2, PIECE, WIDTH), BF16)
    d0, d1, d2, d3, upstream_b, d_packed_b = call(
        kernel_backward_b,
        [twin] * 4 + [token, packed],
        [scores, probs],
        (
            c3, c_eastern, c_below, c_diagonal, b0, b1, b2, b3, inputs_b, gain_b, qkv_weight_b,
            out_weight_b, packed_b, probs_b, mixed_b, sort, sort_t,
        ),
        flops=5 * 10**9,
    )
    d3 = permute_both(d3, 1)
    d2 = permute(d2, "lat", lambda i: i + 1)
    d1 = permute(d1, "lon", lambda i: i + 1)
    send_b, keep_b = call(
        kernel_grads_b, [half_grads] * 2, [normed_t], (normed_b, mixed_b, upstream_b, d_packed_b),
        flops=2 * 10**9,
    )
    send_one_b, send_two_b, keep_one_b, keep_two_b = quarters(
        kernel_first_sum_b, keep_b, to_core(send_b)
    )
    parts_b = (keep_one_b, to_x(send_one_b, 1), keep_two_b, to_x(send_two_b, 3))
    send_one_b, send_two_b, held_one_b, held_two_b = second_sum(parts_b)
    parts_b = (held_one_b, to_x(send_one_b, 3), held_two_b, to_x(send_two_b, 1))
    grad_middle, d_packed_a, send_a = call(
        kernel_backward_a,
        [token, packed, half_grads],
        [scores, probs],
        (
            d3, d2, d1, d0, upstream_a, out_weight_a, packed_a, probs_a, mixed_a, normed_a_t,
            sort_t,
        ),
        flops=5 * 10**9,
    )
    got_a = to_core(send_a)
    keep_a = call(
        kernel_keep_a, [half_grads], [], (normed_a_t, mixed_a, grad_middle, d_packed_a),
        flops=10**9,
    )[0]
    send_one_a, send_two_a, keep_one_a, keep_two_a = quarters(kernel_first_sum_a, keep_a, got_a)
    send_one_a, send_two_a, d_packed_a = lax.optimization_barrier((send_one_a, send_two_a, d_packed_a))
    parts_a = (keep_one_a, to_y(send_one_a, 1), keep_two_a, to_y(send_two_a, 3))
    grad_fields = call(
        kernel_finish_a,
        [grid],
        [qkv_shape],
        (inputs_a, grad_middle, gain_a, qkv_weight_a, d_packed_a, place_t),
        hbm=(3,), copies=1, flops=4 * 10**9, final=(0,),
    )[0]
    pair = ((2, 32, SIDE), BF16)
    send_b, keep_b = call(kernel_third_sum_b, [pair] * 2, [], parts_b)
    got_b = to_y(send_b, 1)
    send_one_a, send_two_a, held_one_a, held_two_a = second_sum(parts_a)
    send_one_a, send_two_a, grad_fields = lax.optimization_barrier(
        (send_one_a, send_two_a, grad_fields)
    )
    parts_a = (held_one_a, to_y(send_one_a, 3), held_two_a, to_y(send_two_a, 1))
    send_a, keep_a = call(kernel_third_sum_a, [pair] * 2, [], parts_a)
    got_a = to_x(send_a, 1)
    send_b, keep_b = halve(keep_b, got_b)
    got_b = to_y(send_b, 3)
    send_a, keep_a = halve(keep_a, got_a)
    send_a, middle_a = lax.optimization_barrier((send_a, middle_a))
    got_a = to_x(send_a, 3)
    advanced = call(
        kernel_advanced, [grid], [], (d3, d2, d1, d0, middle_a, place_t, sort_t),
        flops=2 * 10**9, final=(0,),
    )[0]
    got_a, got_b, advanced = lax.optimization_barrier((got_a, got_b, advanced))
    blocks = call(
        kernel_columns, [((8, 64, GROUP), BF16)], [], (keep_a, got_a, keep_b, got_b)
    )[0]
    parts = exchange_z(blocks)
    grads = call(
        kernel_total,
        [((32, 96), F32), ((32, 32), F32)] * 2,
        [],
        (parts,),
        final=(0, 1, 2, 3),
    )
    return (advanced.transpose(2, 0, 1, 3), grad_fields.transpose(2, 0, 1, 3), *grads)


def solution(mesh):
    grid = P(None, "lat", "lon", None)
    return jax.shard_map(
        body,
        mesh=mesh,
        in_specs=(grid, grid) + (P(),) * 9,
        out_specs=(grid, grid) + (P("lat", "lon"),) * 4,
        check_vma=False,
    )
```

```python
import jax
import jax.numpy as jnp
import numpy as np
from jax import lax
from jax.experimental import pallas as pl
from jax.experimental.pallas import tpu as pltpu
from jax.sharding import PartitionSpec as P

WINDOWS = 2
LENGTH = 144
QUARTER = 36
TOKENS = WINDOWS * LENGTH
PIECE = WINDOWS * QUARTER
WIDTH = 512
HEADS = 16
HEAD = 32
GROUP = 128
GROUPS = WIDTH // GROUP
PER_GROUP = GROUP // HEAD
ROOT = HEAD**0.5
SIDE = 2 * WIDTH
EPS = 1e-05
NEG = -1000000000.0
VMEM_LIMIT = 24 * 1024 * 1024
F32 = jnp.float32
BF16 = jnp.bfloat16


def _tables():
    place = np.zeros((TOKENS, TOKENS), np.float32)
    sort = np.zeros((TOKENS, TOKENS), np.float32)
    where = np.zeros((LENGTH, 8), np.int32)
    for window in range(WINDOWS):
        for quadrant in range(4):
            for level in range(2):
                for row in range(6):
                    for column in range(3):
                        inner = level * 18 + row * 3 + column
                        at = quadrant * QUARTER + inner
                        token = window * LENGTH + at
                        lat = quadrant // 2 * 6 + row
                        lon = quadrant % 2 * 3 + column
                        source = (lat * 6 + lon) * 4 + 2 * window + level
                        place[token, source] = 1
                        sort[quadrant * PIECE + window * QUARTER + inner, token] = 1
                        where[at, 0] = lat
                        where[at, 1] = lon
    return place, sort, where


PLACE, SORT, WHERE = _tables()


def mm(left, right):
    return jnp.dot(left, right, preferred_element_type=F32)


def mm_t(left, right):
    return lax.dot_general(left, right, (((1,), (1,)), ((), ())), preferred_element_type=F32)


def normalise(inputs):
    centre = inputs - jnp.mean(inputs, axis=-1, keepdims=True)
    spread = jnp.mean(centre * centre, axis=-1, keepdims=True)
    scale = lax.rsqrt(spread + EPS)
    return centre * scale, scale


def lanes(shape):
    return lax.broadcasted_iota(jnp.int32, shape, 1)


def head_masks():
    lane = lanes((1, GROUP))
    return [
        ((lane >= h * HEAD) & (lane < (h + 1) * HEAD)).astype(F32).astype(BF16)
        for h in range(PER_GROUP)
    ]


def bias_features(ids_ref, where_ref, table_ref, spare_ref, shift, last):
    lat_at = lax.axis_index("lat")
    lon_at = lax.axis_index("lon")
    rows, columns = ids_ref.shape
    row = where_ref[:, 0:1]
    column = where_ref[:, 1:2] + (lon_at * 6 + shift // 2)
    at = row + (lat_at * 12 + shift)
    at = jnp.where(at >= rows, at - rows, at)
    column = jnp.where(column >= columns, column - columns, column)
    pick = (lanes((LENGTH, rows)) == at).astype(F32).astype(BF16)
    found = mm(pick, ids_ref[...].astype(F32).astype(BF16))
    found = jnp.where(lanes((LENGTH, columns)) == column, found, 0.0)
    kind = jnp.sum(found, axis=1, keepdims=True).astype(jnp.int32)
    lane = lanes((LENGTH, GROUP))
    third = (lane >= 3).astype(jnp.int32) + (lane >= 6).astype(jnp.int32)
    query = ((lane < 9) & (third == kind)).astype(F32)
    key = ((lane < 3) & (lane == kind)).astype(F32)
    if last:
        flag = ((row >= 6) & (lat_at == lax.axis_size("lat") - 1)).astype(F32)
        query = jnp.where(lane == 9, flag, jnp.where(lane == 10, 1.0 - flag, query))
        key = jnp.where(lane == 3, 1.0 - flag, jnp.where(lane == 4, flag, key))
    small = (16, GROUP)
    lane = lanes(small)
    sub = lax.broadcasted_iota(jnp.int32, small, 0)
    third = (lane >= 3).astype(jnp.int32) + (lane >= 6).astype(jnp.int32)
    part = lane - 3 * third
    spots = {
        (first, second): (lane < 9) & (third == first) & (sub == second)
        for first in range(3)
        for second in range(3)
    }
    fixed = jnp.where(((sub == 3) & (lane == 9)) | ((sub == 4) & (lane == 10)), NEG * ROOT, 0.0)
    for head in range(HEADS):
        entry = fixed
        for (first, second), spot in spots.items():
            entry = jnp.where(spot, table_ref[first, second, head] * ROOT, entry)
        high = entry.astype(BF16).astype(F32)
        middle = (entry - high).astype(BF16).astype(F32)
        low = entry - high - middle
        entry = jnp.where(part == 0, high, jnp.where(part == 1, middle, low))
        entry = jnp.where(lane >= 9, high, entry)
        spare_ref[:, head * GROUP : (head + 1) * GROUP] = entry.astype(BF16)
    features = mm(key.astype(BF16)[:, :16], spare_ref[...])
    return query.astype(BF16), features.astype(BF16)


def forward_core(
    inputs, gain, qkv_ref, out_ref, query_features, key_ref, packed_ref, probs_ref, mixed_t_ref, scores_ref
):
    hat, _ = normalise(inputs)
    normed = (hat * gain).astype(BF16)
    packed_ref[...] = mm(normed, qkv_ref[...]).astype(BF16)
    masks = head_masks()
    factor = F32(1.0 / ROOT * np.log2(np.e))
    for window, group, rows, at in sections():
        query = packed_ref[rows, at : at + GROUP]
        keys = packed_ref[rows, WIDTH + at : WIDTH + at + GROUP]
        for h in range(PER_GROUP):
            head = group * PER_GROUP + h
            left = jnp.concatenate([keys, key_ref[:, head * GROUP : (head + 1) * GROUP]], axis=1)
            right = jnp.concatenate([query * masks[h], query_features], axis=1)
            scores_ref[window * HEADS + head] = mm_t(left, right)
    for item in range(WINDOWS * HEADS):
        scores = scores_ref[item]
        top = jnp.max(scores, axis=0, keepdims=True)
        raised = jnp.exp2((scores - top) * factor)
        total = jnp.sum(raised, axis=0, keepdims=True)
        probs_ref[item] = (raised * (1.0 / total)).astype(BF16)
    for window, group, rows, at in sections():
        values_t = packed_ref[rows, 2 * WIDTH + at : 2 * WIDTH + at + GROUP].T
        for h in range(PER_GROUP):
            head = group * PER_GROUP + h
            mixed = mm(values_t[h * HEAD : (h + 1) * HEAD], probs_ref[window * HEADS + head])
            mixed_t_ref[window, head * HEAD : (head + 1) * HEAD, :] = mixed.astype(BF16)
    parts = [mm(mixed_t_ref[window].T, out_ref[...]) for window in range(WINDOWS)]
    return normed, jnp.concatenate(parts, axis=0)


def sections():
    for window in range(WINDOWS):
        for group in range(GROUPS):
            rows = slice(window * LENGTH, (window + 1) * LENGTH)
            yield window, group, rows, group * GROUP


def backward_core(
    upstream, out_ref, packed_ref, probs_ref, mixed_t_ref, d_packed_ref, d_probs_ref, d_scores_ref
):
    masks = head_masks()
    d_mixed = mm_t(upstream, out_ref[...]).astype(BF16)
    for window, group, rows, at in sections():
        values = packed_ref[rows, 2 * WIDTH + at : 2 * WIDTH + at + GROUP]
        up = d_mixed[rows, at : at + GROUP]
        for h in range(PER_GROUP):
            d_probs_ref[window * HEADS + group * PER_GROUP + h] = mm_t(values, up * masks[h])
    for window in range(WINDOWS):
        here = upstream[window * LENGTH : (window + 1) * LENGTH]
        d_mixed_t = mm_t(out_ref[...], here).astype(BF16)
        dots = d_mixed_t.astype(F32) * mixed_t_ref[window].astype(F32)
        for head in range(HEADS):
            item = window * HEADS + head
            inner = jnp.sum(dots[head * HEAD : (head + 1) * HEAD], axis=0, keepdims=True)
            d_scores = (d_probs_ref[item] - inner) * F32(1.0 / ROOT)
            d_scores_ref[item] = (probs_ref[item].astype(F32) * d_scores).astype(BF16)
    for window, group, rows, at in sections():
        query = packed_ref[rows, at : at + GROUP]
        keys_t = packed_ref[rows, WIDTH + at : WIDTH + at + GROUP].T
        up = d_mixed[rows, at : at + GROUP]
        d_values = None
        d_keys = None
        d_query = []
        for h in range(PER_GROUP):
            item = window * HEADS + group * PER_GROUP + h
            d_value = mm(probs_ref[item], up * masks[h])
            d_key = mm(d_scores_ref[item], query * masks[h])
            d_values = d_value if d_values is None else d_values + d_value
            d_keys = d_key if d_keys is None else d_keys + d_key
            d_query.append(mm(keys_t[h * HEAD : (h + 1) * HEAD], d_scores_ref[item]))
        d_query = jnp.concatenate(d_query, axis=0).T
        d_packed_ref[rows, at : at + GROUP] = d_query.astype(BF16)
        d_packed_ref[rows, WIDTH + at : WIDTH + at + GROUP] = d_keys.astype(BF16)
        d_packed_ref[rows, 2 * WIDTH + at : 2 * WIDTH + at + GROUP] = d_values.astype(BF16)


def norm_backward(inputs, gain, d_packed, qkv_ref):
    d_normed = mm_t(d_packed, qkv_ref[...]).astype(BF16).astype(F32)
    hat, scale = normalise(inputs)
    d_hat = d_normed * gain
    mean = jnp.mean(d_hat, axis=-1, keepdims=True)
    along = jnp.mean(d_hat * hat, axis=-1, keepdims=True)
    return scale * (d_hat - mean - hat * along)


def grads_half(half, normed_t_ref, mixed_t_ref, upstream, d_packed_ref, result_ref):
    def blocks(ref, *first):
        return [
            ref[(*first, pl.ds(pl.multiple_of((2 * block + half) * 32, 32), 32), slice(None))]
            for block in range(8)
        ]

    left = jnp.concatenate(blocks(normed_t_ref), axis=0)
    qkv = mm(left, d_packed_ref[...]).astype(BF16)
    total = None
    for window in range(WINDOWS):
        left = jnp.concatenate(blocks(mixed_t_ref, window), axis=0)
        part = mm(left, upstream[window * LENGTH : (window + 1) * LENGTH])
        total = part if total is None else total + part
    total = total.astype(BF16)
    result_ref[:, :768] = qkv[:, :768]
    result_ref[:, 768:SIDE] = total[:, :256]
    result_ref[:, SIDE : SIDE + 768] = qkv[:, 768:]
    result_ref[:, SIDE + 768 :] = total[:, 256:]


def load_grid(ref, place, spare_ref):
    for row in range(12):
        for column in range(6):
            at = (row * 6 + column) * 4
            spare_ref[at : at + 4, :] = ref[row, column].astype(F32)
    return mm(place, spare_ref[...].astype(BF16))


def store_grid(ref, place_t, tokens):
    spread = mm(place_t, tokens)
    for row in range(12):
        for column in range(6):
            at = (row * 6 + column) * 4
            ref[row, column] = spread[at : at + 4].astype(BF16)


def split_pieces(sort, tokens, refs):
    tokens = mm(sort, tokens)
    for at, ref in enumerate(refs):
        ref[...] = tokens[at * PIECE : (at + 1) * PIECE].astype(BF16)


def join_pieces(sort_t, pieces):
    tokens = jnp.concatenate([piece.astype(F32) for piece in pieces], axis=0)
    return mm(sort_t, tokens.astype(BF16))


def fetch(pairs, sems):
    copies = [
        pltpu.make_async_copy(source, target, sems.at[at])
        for at, (source, target) in enumerate(pairs)
    ]
    for copy in copies:
        copy.start()
    return copies


def kernel_forward_a(
    fields_hbm, ids_hbm, gain_hbm, table_hbm, qkv_hbm, out_hbm, place_hbm, sort_hbm, where_hbm,
    piece0, piece1, piece2, piece3, inputs_out, middle_out, normed_out, packed, probs, mixed_t,
    fields, ids, gain, table, qkv, out, place, sort, where, grid, spare, key_features, scores, sems,
):
    *early, qkv_in, out_in, sort_in = fetch(
        (
            (ids_hbm, ids), (where_hbm, where), (table_hbm, table), (fields_hbm, fields),
            (place_hbm, place), (gain_hbm, gain), (qkv_hbm, qkv), (out_hbm, out), (sort_hbm, sort),
        ),
        sems,
    )
    for copy in early:
        copy.wait()
    query_features, features = bias_features(ids, where, table, spare, 0, False)
    key_features[...] = features
    inputs = load_grid(fields, place[...], grid)
    inputs_out[...] = inputs.astype(BF16)
    qkv_in.wait()
    out_in.wait()
    normed, delta = forward_core(
        inputs, gain[...].reshape(1, WIDTH), qkv, out, query_features, key_features,
        packed, probs, mixed_t, scores,
    )
    normed_out[...] = normed
    middle = (inputs + delta).astype(BF16)
    middle_out[...] = middle
    sort_in.wait()
    split_pieces(sort[...], middle, (piece0, piece1, piece2, piece3))


def kernel_cotangent(
    cotangent_hbm, place, sort, normed, ids, table, where,
    piece0, piece1, piece2, piece3, upstream_out, normed_t, query_out, key_out,
    cotangent, grid, spare, sems,
):
    (cotangent_in,) = fetch(((cotangent_hbm, cotangent),), sems)
    normed_t[...] = normed[...].T
    query, keys = bias_features(ids, where, table, spare, 6, True)
    query_out[...] = query
    key_out[...] = keys
    cotangent_in.wait()
    upstream = load_grid(cotangent, place[...], grid).astype(BF16)
    upstream_out[...] = upstream
    split_pieces(sort[...], upstream, (piece0, piece1, piece2, piece3))


def kernel_forward_b(
    piece0, piece1, piece3, piece2, query_features, key_features, gain, qkv, out, sort, sort_t,
    back0, back1, back2, back3, inputs_out, normed_out, packed, probs, mixed_t,
    scores,
):
    inputs = join_pieces(sort_t[...], [ref[...] for ref in (piece0, piece1, piece2, piece3)])
    inputs_out[...] = inputs.astype(BF16)
    normed, delta = forward_core(
        inputs, gain[...].reshape(1, WIDTH), qkv, out, query_features[...], key_features,
        packed, probs, mixed_t, scores,
    )
    normed_out[...] = normed
    split_pieces(sort[...], delta.astype(BF16), (back0, back1, back2, back3))


def kernel_backward_b(
    piece0, piece1, piece3, piece2, delta0, delta1, delta2, delta3,
    inputs, gain, qkv, out, packed, probs, mixed_t, sort, sort_t,
    back0, back1, back2, back3, upstream_out, d_packed,
    d_probs, d_scores,
):
    pieces = [ref[...] for ref in (piece0, piece1, piece2, piece3)]
    upstream = join_pieces(sort_t[...], pieces).astype(BF16)
    upstream_out[...] = upstream
    backward_core(upstream, out, packed, probs, mixed_t, d_packed, d_probs, d_scores)
    d_inputs = norm_backward(
        inputs[...].astype(F32), gain[...].reshape(1, WIDTH), d_packed[...], qkv
    )
    backs = (back0, back1, back2, back3)
    split_pieces(sort[...], d_inputs.astype(BF16), [back.at[0] for back in backs])
    for back, delta in zip(backs, (delta0, delta1, delta2, delta3), strict=True):
        back[1] = delta[...]


def kernel_grads_b(normed, mixed_t, upstream, d_packed, send, keep, normed_t):
    normed_t[...] = normed[...].T
    core = lax.axis_index("lat") % 2
    grads_half(1 - core, normed_t, mixed_t, upstream[...], d_packed, send)
    grads_half(core, normed_t, mixed_t, upstream[...], d_packed, keep)


def kernel_backward_a(
    back0, back2, back1, back3, upstream, out, packed, probs, mixed_t, normed_t, sort_t,
    grad_middle_out, d_packed, send,
    d_probs, d_scores,
):
    d_inputs = join_pieces(sort_t[...], [back[0] for back in (back0, back1, back2, back3)])
    grad_middle = (upstream[...].astype(F32) + d_inputs).astype(BF16)
    grad_middle_out[...] = grad_middle
    backward_core(grad_middle, out, packed, probs, mixed_t, d_packed, d_probs, d_scores)
    core = lax.axis_index("lat") % 2
    grads_half(1 - core, normed_t, mixed_t, grad_middle, d_packed, send)


def kernel_keep_a(normed_t, mixed_t, grad_middle, d_packed, keep):
    core = lax.axis_index("lat") % 2
    grads_half(core, normed_t, mixed_t, grad_middle[...], d_packed, keep)


def kernel_advanced(back0, back2, back1, back3, middle, place_t, sort_t, advanced):
    delta = join_pieces(sort_t[...], [back[1] for back in (back0, back1, back2, back3)])
    store_grid(advanced, place_t[...], (middle[...].astype(F32) + delta).astype(BF16))


def kernel_finish_a(
    inputs, grad_middle, gain, qkv_hbm, d_packed, place_t, grad_fields, qkv, sems
):
    (qkv_in,) = fetch(((qkv_hbm, qkv),), sems)
    qkv_in.wait()
    d_inputs = norm_backward(
        inputs[...].astype(F32), gain[...].reshape(1, WIDTH), d_packed[...], qkv
    )
    total = (grad_middle[...].astype(F32) + d_inputs).astype(BF16)
    store_grid(grad_fields, place_t[...], total)


def rows_of(block, count):
    return pl.ds(pl.multiple_of(block * count, count), count)


def place_x():
    return lax.axis_index("lon") // 8 * 2 + lax.axis_index("lat") // 2 % 2


def place_y():
    return lax.axis_index("lat") // 4


def kernel_first_sum_a(keep, got, send_one, send_two, keep_one, keep_two):
    y = place_y()
    for side, first, send, kept in ((0, 1, send_one, keep_one), (1, 3, send_two, keep_two)):
        columns = slice(side * SIDE, (side + 1) * SIDE)
        for target, place, block in (
            (send, 0, y ^ first), (send, 1, y ^ 2), (kept, 0, y), (kept, 1, y ^ 2 ^ first)
        ):
            rows = rows_of(block, 64)
            target[place] = keep[rows, columns] + got[rows, columns]


def kernel_first_sum_b(keep, got, send_one, send_two, keep_one, keep_two):
    x = place_x()
    for part, first, send, kept in ((0, 1, send_one, keep_one), (1, 3, send_two, keep_two)):
        for target, place, block in (
            (send, 0, x ^ first), (send, 1, x ^ 2), (kept, 0, x), (kept, 1, x ^ 2 ^ first)
        ):
            columns = rows_of(block // 2, SIDE)
            for inner in range(2):
                rows = rows_of((part * 2 + inner) * 2 + block % 2, 32)
                target[place, inner * 32 : (inner + 1) * 32] = keep[rows, columns] + got[rows, columns]


def kernel_second_sum(keep_one, got_one, keep_two, got_two, send_one, send_two, held_one, held_two):
    send_one[...] = keep_one[1] + got_one[1]
    send_two[...] = keep_two[1] + got_two[1]
    held_one[...] = keep_one[0] + got_one[0]
    held_two[...] = keep_two[0] + got_two[0]


def third_sum(at, halves, send, keep):
    for target, place, block in ((send, 0, at ^ 1), (send, 1, at ^ 2), (keep, 0, at), (keep, 1, at ^ 3)):
        rows = rows_of(block % 2, 32)
        for half, (held, got) in enumerate(halves):

            @pl.when(block // 2 == half)
            def _(target=target, place=place, rows=rows, held=held, got=got):
                target[place] = held[rows, :] + got[rows, :]


def kernel_third_sum_a(held_one, got_one, held_two, got_two, send, keep):
    third_sum(place_x(), ((held_one, got_one), (held_two, got_two)), send, keep)


def kernel_third_sum_b(held_one, got_one, held_two, got_two, send, keep):
    third_sum(place_y(), ((held_one, got_one), (held_two, got_two)), send, keep)


def kernel_halve(keep, got, send, held):
    half = keep.shape[0] // 2
    held[...] = keep[:half] + got[:half]
    send[...] = keep[half:] + got[half:]


def kernel_columns(keep_a, got_a, keep_b, got_b, blocks):
    for rows, held, got in ((slice(0, 32), keep_a, got_a), (slice(32, 64), keep_b, got_b)):
        total = held[0].astype(F32) + got[0].astype(F32)
        for block in range(8):
            qkv = total[:, block * 96 : (block + 1) * 96]
            out = total[:, 768 + block * 32 : 768 + (block + 1) * 32]
            blocks[block, rows] = jnp.concatenate([qkv, out], axis=1).astype(BF16)


def kernel_total(parts, qkv_a, out_a, qkv_b, out_b):
    total = parts[0].astype(F32)
    for at in range(1, 8):
        total = total + parts[at].astype(F32)
    for rows, qkv, out in ((slice(0, 32), qkv_a, out_a), (slice(32, 64), qkv_b, out_b)):
        qkv[...] = total[rows, :96]
        out[...] = total[rows, 96:]


def call(kernel, outs, scratch, args, smem=(), hbm=(), copies=0, flops=0, final=()):
    def space(at):
        return pltpu.SMEM if at in smem else pltpu.HBM if at in hbm else pltpu.VMEM

    cost = pl.CostEstimate(flops=flops, bytes_accessed=1 << 20, transcendentals=0) if flops else None
    args = [
        pltpu.with_memory_space_constraint(arg, pltpu.HBM) if at in hbm or at in smem else arg
        for at, arg in enumerate(args)
    ]
    shapes = [pltpu.VMEM(*item) if isinstance(item, tuple) else item for item in scratch]
    if copies:
        shapes.append(pltpu.SemaphoreType.DMA((copies,)))
    return pl.pallas_call(
        kernel,
        out_shape=tuple(
            jax.ShapeDtypeStruct(shape, kind) if at in final else pltpu.VMEM(shape, kind)
            for at, (shape, kind) in enumerate(outs)
        ),
        in_specs=[pl.BlockSpec(memory_space=space(at)) for at in range(len(args))],
        out_specs=tuple(pl.BlockSpec(memory_space=pltpu.VMEM) for _ in outs),
        scratch_shapes=shapes,
        cost_estimate=cost,
        compiler_params=pltpu.CompilerParams(vmem_limit_bytes=VMEM_LIMIT),
    )(*args)


def permute(array, axis, target):
    length = lax.axis_size(axis)
    return lax.ppermute(array, axis, [(i, target(i) % length) for i in range(length)])


def permute_both(array, by):
    lons, lats = lax.axis_size("lon"), lax.axis_size("lat")
    pairs = [
        (lon * lats + lat, (lon + by) % lons * lats + (lat + by) % lats)
        for lon in range(lons)
        for lat in range(lats)
    ]
    return lax.ppermute(array, ("lon", "lat"), pairs)


def to_core(array):
    return permute(array, "lat", lambda i: i ^ 1)


def to_y(array, by):
    return permute(array, "lat", lambda i: i ^ (4 * by))


def to_x(array, by):
    if by == 1:
        return permute(array, "lat", lambda i: i ^ 2)
    lons, lats = lax.axis_size("lon"), lax.axis_size("lat")
    pairs = [
        (lon * lats + lat, (lon ^ 8) * lats + (lat ^ 2)) for lon in range(lons) for lat in range(lats)
    ]
    return lax.ppermute(array, ("lon", "lat"), pairs)


def quarters(kernel, keep, got):
    return call(kernel, [((2, 64, SIDE), BF16)] * 4, [], (keep, got))


def second_sum(parts):
    return call(kernel_second_sum, [((64, SIDE), BF16)] * 4, [], parts)


def halve(keep, got):
    shape = (keep.shape[0] // 2,) + keep.shape[1:]
    return call(kernel_halve, [(shape, BF16)] * 2, [], (keep, got))


def exchange_z(messages):
    groups = [[x_hi * 8 + z for z in range(8)] for x_hi in range(2)]
    return lax.all_to_all(messages, "lon", 0, 0, axis_index_groups=groups, tiled=True)


def body(
    fields, cotangent, land_ids, gain_a, table_a, qkv_weight_a, out_weight_a,
    gain_b, table_b, qkv_weight_b, out_weight_b,
):
    place = jnp.asarray(PLACE, BF16)
    place_t = jnp.asarray(PLACE.T, BF16)
    sort = jnp.asarray(SORT, BF16)
    sort_t = jnp.asarray(SORT.T, BF16)
    where = jnp.asarray(WHERE)
    fields = fields.transpose(1, 2, 0, 3)
    cotangent = cotangent.transpose(1, 2, 0, 3)
    table_a = table_a.transpose(1, 2, 0)
    table_b = table_b.transpose(1, 2, 0)
    grid = (fields.shape, BF16)
    piece = ((PIECE, WIDTH), BF16)
    token = ((TOKENS, WIDTH), BF16)
    token_wide = ((TOKENS, WIDTH), F32)
    packed = ((TOKENS, 3 * WIDTH), BF16)
    probs = ((WINDOWS * HEADS, LENGTH, LENGTH), BF16)
    scores = ((WINDOWS * HEADS, LENGTH, LENGTH), F32)
    mixed_t = ((WINDOWS, WIDTH, LENGTH), BF16)
    half_grads = ((WIDTH // 2, 4 * WIDTH), BF16)
    normed_t = ((WIDTH, TOKENS), BF16)
    square = ((TOKENS, TOKENS), BF16)
    spare = ((16, HEADS * GROUP), BF16)
    query = ((LENGTH, GROUP), BF16)
    keys = ((LENGTH, HEADS * GROUP), BF16)
    ids = (land_ids.shape, jnp.int32)
    place_of = (where.shape, jnp.int32)
    vector = ((WIDTH,), F32)
    qkv_shape = ((WIDTH, 3 * WIDTH), BF16)
    out_shape = ((WIDTH, WIDTH), BF16)

    p0, p1, p2, p3, inputs_a, middle_a, normed_a, packed_a, probs_a, mixed_a = call(
        kernel_forward_a,
        [piece] * 4 + [token] * 3 + [packed, probs, mixed_t],
        [
            grid, ids, vector, pltpu.SMEM(table_a.shape, F32), qkv_shape, out_shape, square, square,
            place_of, token_wide, spare, keys, scores,
        ],
        (fields, land_ids, gain_a, table_a, qkv_weight_a, out_weight_a, place, sort, where),
        hbm=(0, 1, 2, 3, 4, 5, 6, 7, 8), copies=9, flops=7 * 10**9,
    )
    diagonal = permute_both(p0, -1)
    eastern = permute(p2, "lon", lambda i: i - 1)
    below = permute(p1, "lat", lambda i: i - 1)
    c0, c1, c2, c3, upstream_a, normed_a_t, query_b, keys_b = call(
        kernel_cotangent,
        [piece] * 4 + [token, normed_t, query, keys],
        [grid, token_wide, spare],
        (cotangent, place, sort, normed_a, land_ids, table_b, where),
        smem=(5,), hbm=(0,), copies=1, flops=2 * 10**9,
    )
    c_diagonal = permute_both(c0, -1)
    c_eastern = permute(c2, "lon", lambda i: i - 1)
    c_below = permute(c1, "lat", lambda i: i - 1)
    b0, b1, b2, b3, inputs_b, normed_b, packed_b, probs_b, mixed_b = call(
        kernel_forward_b,
        [piece] * 4 + [token] * 2 + [packed, probs, mixed_t],
        [scores],
        (p3, eastern, diagonal, below, query_b, keys_b, gain_b, qkv_weight_b, out_weight_b, sort, sort_t),
        flops=5 * 10**9,
    )
    twin = ((2, PIECE, WIDTH), BF16)
    d0, d1, d2, d3, upstream_b, d_packed_b = call(
        kernel_backward_b,
        [twin] * 4 + [token, packed],
        [scores, probs],
        (
            c3, c_eastern, c_diagonal, c_below, b0, b1, b2, b3, inputs_b, gain_b, qkv_weight_b,
            out_weight_b, packed_b, probs_b, mixed_b, sort, sort_t,
        ),
        flops=5 * 10**9,
    )
    d3 = permute_both(d3, 1)
    d1 = permute(d1, "lon", lambda i: i + 1)
    d2 = permute(d2, "lat", lambda i: i + 1)
    send_b, keep_b = call(
        kernel_grads_b, [half_grads] * 2, [normed_t], (normed_b, mixed_b, upstream_b, d_packed_b),
        flops=2 * 10**9,
    )
    send_one_b, send_two_b, keep_one_b, keep_two_b = quarters(
        kernel_first_sum_b, keep_b, to_core(send_b)
    )
    parts_b = (keep_one_b, to_x(send_one_b, 1), keep_two_b, to_x(send_two_b, 3))
    send_one_b, send_two_b, held_one_b, held_two_b = second_sum(parts_b)
    parts_b = (held_one_b, to_x(send_one_b, 3), held_two_b, to_x(send_two_b, 1))
    grad_middle, d_packed_a, send_a = call(
        kernel_backward_a,
        [token, packed, half_grads],
        [scores, probs],
        (
            d3, d1, d2, d0, upstream_a, out_weight_a, packed_a, probs_a, mixed_a, normed_a_t,
            sort_t,
        ),
        flops=5 * 10**9,
    )
    got_a = to_core(send_a)
    keep_a = call(
        kernel_keep_a, [half_grads], [], (normed_a_t, mixed_a, grad_middle, d_packed_a),
        flops=10**9,
    )[0]
    send_one_a, send_two_a, keep_one_a, keep_two_a = quarters(kernel_first_sum_a, keep_a, got_a)
    send_one_a, send_two_a, d_packed_a = lax.optimization_barrier((send_one_a, send_two_a, d_packed_a))
    parts_a = (keep_one_a, to_y(send_one_a, 1), keep_two_a, to_y(send_two_a, 3))
    grad_fields = call(
        kernel_finish_a,
        [grid],
        [qkv_shape],
        (inputs_a, grad_middle, gain_a, qkv_weight_a, d_packed_a, place_t),
        hbm=(3,), copies=1, flops=4 * 10**9, final=(0,),
    )[0]
    pair = ((2, 32, SIDE), BF16)
    send_b, keep_b = call(kernel_third_sum_b, [pair] * 2, [], parts_b)
    got_b = to_y(send_b, 1)
    send_one_a, send_two_a, held_one_a, held_two_a = second_sum(parts_a)
    send_one_a, send_two_a, grad_fields = lax.optimization_barrier(
        (send_one_a, send_two_a, grad_fields)
    )
    parts_a = (held_one_a, to_y(send_one_a, 3), held_two_a, to_y(send_two_a, 1))
    send_a, keep_a = call(kernel_third_sum_a, [pair] * 2, [], parts_a)
    got_a = to_x(send_a, 1)
    send_b, keep_b = halve(keep_b, got_b)
    got_b = to_y(send_b, 3)
    send_a, keep_a = halve(keep_a, got_a)
    send_a, middle_a = lax.optimization_barrier((send_a, middle_a))
    got_a = to_x(send_a, 3)
    advanced = call(
        kernel_advanced, [grid], [], (d3, d1, d2, d0, middle_a, place_t, sort_t),
        flops=2 * 10**9, final=(0,),
    )[0]
    got_a, got_b, advanced = lax.optimization_barrier((got_a, got_b, advanced))
    blocks = call(
        kernel_columns, [((8, 64, GROUP), BF16)], [], (keep_a, got_a, keep_b, got_b)
    )[0]
    parts = exchange_z(blocks)
    grads = call(
        kernel_total,
        [((32, 96), F32), ((32, 32), F32)] * 2,
        [],
        (parts,),
        final=(0, 1, 2, 3),
    )
    return (advanced.transpose(2, 0, 1, 3), grad_fields.transpose(2, 0, 1, 3), *grads)


def solution(mesh):
    grid = P(None, "lat", "lon", None)
    return jax.shard_map(
        body,
        mesh=mesh,
        in_specs=(grid, grid) + (P(),) * 9,
        out_specs=(grid, grid) + (P("lat", "lon"),) * 4,
        check_vma=False,
    )
```
